32 devices in a mesh: dp: 8 (over z, y), seq: 4 (over x, core).
Axes of the slice: x: 2, y: 2, z: 4, core: 2. Of those that a mesh axis runs over, the one named last changes fastest.
Arguments:
- inputs: bfloat16 [16, 1024, 1536], P('dp', 'seq'), may hold values from -6 to 6
- doc_ids: int32 [16, 1024], P('dp', 'seq'), may hold values from 0 to 3, as said below
- gain_attn: float32 [1536], P('dp'), may hold values from 0.5 to 1.5
- w_proj: float32 [1536, 6144], P('dp'), may hold values from -0.15625 to 0.15625
- w_beta: float32 [1536, 12], P('dp'), may hold values from -0.15625 to 0.15625
- conv_taps: float32 [4, 1536], P(None, ('dp', 'seq')), may hold values from -3 to 3
- w_out: float32 [1536, 1536], P('dp'), may hold values from -0.625 to 0.625
- gain_mlp: float32 [1536], P('dp'), may hold values from 0.5 to 1.5
- w_gate: float32 [1536, 4096], P('dp'), may hold values from -0.15625 to 0.15625
- w_up: float32 [1536, 4096], P('dp'), may hold values from -0.15625 to 0.15625
- w_down: float32 [4096, 1536], P('dp'), may hold values from -0.09375 to 0.09375
- out_grad: bfloat16 [16, 1024, 1536], P('dp', 'seq'), may hold values from -6 to 6
Outputs:
- layer_out: bfloat16 [16, 1024, 1536], P('dp', 'seq')
- grad_inputs: float32 [16, 1024, 1536], P('dp', 'seq')
- grad_gain_attn: float32 [1536], P('dp')
- grad_w_proj: float32 [1536, 6144], P('dp')
- grad_w_beta: float32 [1536, 12], P('dp')
- grad_conv_taps: float32 [4, 1536], P(None, ('dp', 'seq'))
- grad_w_out: float32 [1536, 1536], P('dp')
- grad_gain_mlp: float32 [1536], P('dp')
- grad_w_gate: float32 [1536, 4096], P('dp')
- grad_w_up: float32 [1536, 4096], P('dp')
- grad_w_down: float32 [4096, 1536], P('dp')
The draws below stay inside these ranges and needn't reach their ends.
Inputs may be any that keep to these rules, and one draw needn't show every extreme that they name: `doc_ids`: each row is cut into four documents numbered 0 to 3 in order of position; one of them starts within the row's first eighth and ends within its last eighth.
All inputs are finite; a program needn't handle non-finite values.
Results may differ from the reference program's by a relative error of at most 0.019.
The reference program's roundings to bfloat16 on the way count: a program that leaves them out, or rounds other values in their place, can miss the bound.
Values may be sent and summed in bfloat16 or wider, within the bound.
No kernel may reach another device: no remote copies, remote signals or barrier semaphores. Data moves between devices by JAX's collectives and lax.ppermute only.
A program may use at most 384 MiB of HBM per device.

```python
from functools import partial
import jax
import jax.numpy as jnp
from jax import lax

D = 1536
HEADS = 12
FF = 4096
CONV_WIDTH = 4
SEQ_LEN = 1024
ROWS = 16


def draw_doc_ids(key, part):
    key = jax.random.fold_in(key, 17)
    keys_all = jax.random.split(key, 7)
    shape_col = (ROWS, 1)
    flipped = jax.random.randint(keys_all[0], shape_col, 0, 2)
    first_a = jax.random.randint(keys_all[1], shape_col, 1, SEQ_LEN // 8 + 1)
    second_a = jax.random.randint(keys_all[2], shape_col, 7 * SEQ_LEN // 8, SEQ_LEN - 1)
    third_a = second_a + 1 + jax.random.randint(keys_all[3], shape_col, 0, SEQ_LEN - 1 - second_a)
    first_b = jax.random.randint(keys_all[4], shape_col, 1, SEQ_LEN // 16 + 1)
    second_b = first_b + 1 + jax.random.randint(keys_all[5], shape_col, 0, SEQ_LEN // 8 - first_b)
    third_b = jax.random.randint(keys_all[6], shape_col, 7 * SEQ_LEN // 8, SEQ_LEN)
    bound_one = jnp.where(flipped == 1, first_b, first_a)
    bound_two = jnp.where(flipped == 1, second_b, second_a)
    bound_three = jnp.where(flipped == 1, third_b, third_a)
    positions = jnp.arange(SEQ_LEN, dtype=jnp.int32)[None, :]
    counted = (positions >= bound_one).astype(jnp.int32) + (positions >= bound_two).astype(jnp.int32) + (positions >= bound_three).astype(jnp.int32)
    return counted.astype(jnp.int32)


def steps_of(key, extent, shards, low, top_value):
    def one(dim, blocks):
        draws = jax.random.uniform(jax.random.fold_in(jax.random.fold_in(key, 6), dim), (blocks,), jnp.float32, low / len(shards), top_value / len(shards))
        return jnp.repeat(jnp.exp(draws), extent[dim] // blocks).reshape((-1,) + (1,) * (len(extent) - dim - 1))

    factor_of = one(*shards[0])
    for cut in shards[1:]:
        factor_of = factor_of * one(*cut)
    return factor_of


def bell_draw(rng, dims, width, bound, cuts=(), kind=jnp.bfloat16):
    gain = steps_of(rng, dims, cuts, -0.22, 0.18) if cuts else 1.0
    array = jax.random.normal(rng, dims, jnp.float32) * width * gain
    return jnp.minimum(jnp.maximum(array, -bound), bound).astype(kind)


def setup_inputs(seed: int = 0) -> dict:
    key_list = jax.random.split(jax.random.key(seed), 13)
    return {
        "inputs": bell_draw(key_list[0], (ROWS, SEQ_LEN, D), 1.0, 6.0, ((0, 8), (1, 4))),
        "doc_ids": draw_doc_ids(jax.random.fold_in(key_list[12], 71), 0),
        "gain_attn": jnp.clip(1.0 + 0.1 * jax.random.normal(key_list[2], (D,), jnp.float32), 0.5, 1.5),
        "w_proj": bell_draw(key_list[3], (D, 4 * D), D ** -0.5, 0.15625, ((0, 8),), jnp.float32),
        "w_beta": bell_draw(key_list[4], (D, HEADS), D ** -0.5, 0.15625, ((0, 8),), jnp.float32),
        "conv_taps": bell_draw(key_list[5], (CONV_WIDTH, D), 0.5, 3.0, ((1, 32),), jnp.float32),
        "w_out": bell_draw(key_list[6], (D, D), (D // 16) ** -0.5, 0.625, ((0, 8),), jnp.float32),
        "gain_mlp": jnp.clip(1.0 + 0.1 * jax.random.normal(key_list[7], (D,), jnp.float32), 0.5, 1.5),
        "w_gate": bell_draw(key_list[8], (D, FF), D ** -0.5, 0.15625, ((0, 8),), jnp.float32),
        "w_up": bell_draw(key_list[9], (D, FF), D ** -0.5, 0.15625, ((0, 8),), jnp.float32),
        "w_down": bell_draw(key_list[10], (FF, D), FF ** -0.5, 0.09375, ((0, 8),), jnp.float32),
        "out_grad": bell_draw(key_list[11], (ROWS, SEQ_LEN, D), 1.0, 6.0, ((0, 8), (1, 4))),
    }


NORM_EPS = 1e-06
PRECISE = lax.Precision.HIGHEST

@jax.custom_vjp
def low(v):
    return lax.optimization_barrier(v.astype(jnp.bfloat16)).astype(jnp.float32)

@jax.custom_vjp
def low_back(v):
    return v

def low_keep(v):
    return (low(v), None)

def low_pass(kept, grad):
    return (grad,)

def back_keep(v):
    return (v, None)

def back_low(kept, grad):
    return (low(grad),)
low.defvjp(low_keep, low_pass)
low_back.defvjp(back_keep, back_low)

def matmul_high(left, right):
    return jnp.matmul(left, right, precision=PRECISE)

def path_item(joined_in, beta_logit, taps_head, doc_row):
    head_width = taps_head.shape[1]
    length = joined_in.shape[0]
    query_rows = joined_in[:, :head_width]
    keys_in = joined_in[:, head_width:2 * head_width]
    values_in = joined_in[:, 2 * head_width:3 * head_width]
    w_raw = joined_in[:, 3 * head_width:]
    mixed_w = taps_head[0][None, :] * w_raw
    for shift_by in range(1, taps_head.shape[0]):
        earlier = jnp.concatenate([jnp.zeros((shift_by, head_width), jnp.float32), w_raw[:-shift_by]], 0)
        earlier_doc = jnp.concatenate([jnp.full((shift_by,), -1, jnp.int32), doc_row[:-shift_by]], 0)
        same_doc = (earlier_doc == doc_row)[:, None]
        mixed_w = mixed_w + jnp.where(same_doc, taps_head[shift_by][None, :] * earlier, 0.0)
    house_vec = mixed_w * lax.rsqrt(lax.optimization_barrier(jnp.sum(mixed_w * mixed_w, -1, keepdims=True)) + NORM_EPS)
    beta_vec = 2.0 * jax.nn.sigmoid(beta_logit)
    positions = jnp.arange(length)
    is_later = positions[:, None] > positions[None, :]
    not_before = positions[:, None] >= positions[None, :]
    system = beta_vec[:, None] * jnp.where(is_later, matmul_high(house_vec, house_vec.T), 0.0)
    right_side = beta_vec[:, None] * jnp.where(is_later, matmul_high(house_vec, keys_in.T), 0.0)
    solved = jax.scipy.linalg.solve_triangular(system, right_side, lower=True, unit_diagonal=True)
    query_house = jnp.where(not_before, matmul_high(query_rows, house_vec.T), 0.0)
    scores = (matmul_high(query_rows, keys_in.T) - matmul_high(query_house, solved)) * head_width ** (-0.5)
    allowed = not_before & (doc_row[:, None] == doc_row[None, :])
    scores = jnp.where(allowed, scores, -1e+30)
    row_peak = lax.optimization_barrier(jnp.max(scores, -1, keepdims=True))
    weights = jnp.exp(scores - row_peak)
    return matmul_high(weights, values_in) / lax.optimization_barrier(jnp.sum(weights, -1, keepdims=True))

def attend(joined_in, beta_logit, conv_taps, doc_ids):
    rows_n, length, heads_n, packed = joined_in.shape
    head_width = packed // 4
    taps_n = conv_taps.shape[0]
    head_items = joined_in.transpose(0, 2, 1, 3).reshape(rows_n * heads_n, length, packed)
    beta_items = beta_logit.transpose(0, 2, 1).reshape(rows_n * heads_n, length)
    taps_heads = conv_taps.reshape(taps_n, heads_n, head_width).transpose(1, 0, 2)
    taps_items = jnp.broadcast_to(taps_heads[None], (rows_n, heads_n, taps_n, head_width)).reshape(rows_n * heads_n, taps_n, head_width)
    doc_items = jnp.broadcast_to(doc_ids[:, None, :], (rows_n, heads_n, length)).reshape(rows_n * heads_n, length)
    outputs = lax.map(jax.checkpoint(lambda one_item: path_item(*one_item)), (head_items, beta_items, taps_items, doc_items))
    return outputs.reshape(rows_n, heads_n, length, head_width).transpose(0, 2, 1, 3)

def rms_norm(values_in, gain_vec):
    scale_inv = lax.rsqrt(lax.optimization_barrier(jnp.mean(values_in * values_in, -1, keepdims=True)) + NORM_EPS)
    return values_in * scale_inv * gain_vec

def forward(doc_ids, inputs, gain_attn, w_proj, w_beta, conv_taps, w_out, gain_mlp, w_gate, w_up, w_down):
    rows_n, length, model_dim = inputs.shape
    heads_n = w_beta.shape[1]
    normed = low(rms_norm(inputs, low(gain_attn)))
    joined_proj = low_back(low(matmul_high(normed, low(w_proj)))).reshape(rows_n, length, heads_n, -1)
    beta_logit = low_back(low(matmul_high(normed, low(w_beta))))
    attn_mixed = attend(joined_proj, beta_logit, low(conv_taps), doc_ids)
    attn_mixed = low_back(low(attn_mixed)).reshape(rows_n, length, model_dim)
    branch = low_back(matmul_high(attn_mixed, low(w_out)))
    middle = inputs + branch
    normed_two = low(rms_norm(middle, low(gain_mlp)))
    gate_act = low_back(matmul_high(normed_two, low(w_gate)))
    up_act = low_back(matmul_high(normed_two, low(w_up)))
    hidden = low(jax.nn.silu(gate_act) * up_act)
    return middle + low_back(matmul_high(hidden, low(w_down)))

def reference(inputs, doc_ids, gain_attn, w_proj, w_beta, conv_taps, w_out, gain_mlp, w_gate, w_up, w_down, out_grad):
    inputs_f = inputs.astype(jnp.float32)
    result, pullback = jax.vjp(partial(forward, doc_ids), inputs_f, gain_attn, w_proj, w_beta, conv_taps, w_out, gain_mlp, w_gate, w_up, w_down)
    all_grads = pullback(out_grad.astype(jnp.float32))
    return (result.astype(jnp.bfloat16), all_grads[0], all_grads[1], all_grads[2], all_grads[3], all_grads[4], all_grads[5], all_grads[6], all_grads[7], all_grads[8], all_grads[9])
```

```python
import functools
import jax
import jax.numpy as jnp
from jax import lax
from jax.experimental import pallas as pl
from jax.experimental.pallas import tpu as pltpu
from jax.sharding import PartitionSpec as P

F32 = jnp.float32
BF = jnp.bfloat16
NORM_EPS = 1e-06
BLOCK = 256
HALF = 128


def dot_nn(a, b):
    return lax.dot_general(a, b, (((1,), (0,)), ((), ())), preferred_element_type=F32)


def dot_nt(a, b):
    return lax.dot_general(a, b, (((1,), (1,)), ((), ())), preferred_element_type=F32)


def dot_tn(a, b):
    return lax.dot_general(a, b, (((0,), (0,)), ((), ())), preferred_element_type=F32)


def mul(a, b):
    return dot_nn(a.astype(BF), b.astype(BF))


def indices(rows, cols):
    return (
        lax.broadcasted_iota(jnp.int32, (rows, cols), 0),
        lax.broadcasted_iota(jnp.int32, (rows, cols), 1),
    )


def unit_inverse(systems):
    size = systems[0].shape[0]
    row, col = indices(size, size)
    eye = jnp.where(row == col, 1.0, 0.0).astype(F32)
    near = (row - col == 1) & (row % 2 == 1)
    solved = [eye - jnp.where(near, g, 0.0) for g in systems]
    span = 2
    while span < size:
        corner = (row // (2 * span) == col // (2 * span)) & (row % (2 * span) >= span) & (col % (2 * span) < span)
        below = [jnp.where(corner, g, 0.0) for g in systems]
        step = [mul(n, c) for n, c in zip(solved, below)]
        solved = [n - mul(s, n) for n, s in zip(solved, step)]
        span *= 2
    return solved


def block_inverse(g):
    h = HALF
    parts = unit_inverse([p for b in g for p in (b[:h, :h], b[h:, h:])])
    out = []
    for i, b in enumerate(g):
        top, bottom = parts[2 * i], parts[2 * i + 1]
        corner = -mul(mul(bottom, b[h:, :h]), top)
        upper = jnp.concatenate([top, jnp.zeros((h, h), F32)], 1)
        lower = jnp.concatenate([corner, bottom], 1)
        out.append(jnp.concatenate([upper, lower], 0))
    return out


def house(u, taps_ref, aux, taps_n):
    mixed = taps_ref[0:1, :] * u
    for s in range(1, taps_n):
        mixed = mixed + (taps_ref[s : s + 1, :] * aux[:, s : s + 1]) * pltpu.roll(u, s, 0)
    inv = lax.rsqrt(jnp.sum(mixed * mixed, -1, keepdims=True) + NORM_EPS)
    return mixed * inv, inv


def lane_pick(aux, lane):
    pos = lax.broadcasted_iota(jnp.int32, aux.shape, 1)
    return jnp.sum(jnp.where(pos == lane, aux, 0.0), 1, keepdims=True)


def fwd_kernel(taps_n, at_ref, join_ref, aux_ref, logit_ref, doc_ref, taps_ref, *rest):
    length = join_ref.shape[1]
    out_ref, rest = rest[0], rest[1:]
    part = out_ref.shape[1]
    (p_refs, x_ref, n_ref, m_ref, z_ref, qt_ref, w_ref, kt_ref, e_ref, run) = (rest[:-9],) + rest[-9:]
    d = taps_ref.shape[1]
    nb = length // BLOCK
    lane = at_ref[0] * pl.num_programs(1) + pl.program_id(1)
    aux = aux_ref[0]
    beta_all = 2.0 * jax.nn.sigmoid(lane_pick(logit_ref[0].astype(F32), lane))
    u = join_ref[0, :, 3 * d : 4 * d].astype(F32)
    w_all, _ = house(u, taps_ref, aux, taps_n)
    w_ref[0] = w_all.astype(BF)
    row, col = indices(BLOCK, BLOCK)
    later = row > col
    notbefore = row >= col
    scale = d ** -0.5
    sl = [slice(b * BLOCK, (b + 1) * BLOCK) for b in range(nb)]
    w = [w_ref[0, s, :] for s in sl]
    beta = [beta_all[s] for s in sl]
    k = [join_ref[0, s, d : 2 * d] for s in sl]
    q = [join_ref[0, s, 0:d] for s in sl]
    g = [jnp.where(later, beta[b] * dot_nt(w[b], w[b]), 0.0) for b in range(nb)]
    inv = block_inverse(g)
    for b in range(nb):
        nn = inv[b].astype(BF)
        n_ref[0, b] = nn
        r = jnp.where(later, beta[b] * dot_nt(w[b], k[b]), 0.0).astype(BF)
        z = dot_nn(nn, (beta[b] * w_all[sl[b]]).astype(BF)).astype(BF)
        z_ref[0, sl[b], :] = z
        x = dot_nn(nn, r).astype(BF)
        x_ref[0, b] = x
        m = jnp.where(notbefore, dot_nt(q[b], w[b]), 0.0).astype(BF)
        m_ref[0, b] = m
        diag = dot_nt(q[b], k[b]) - dot_nn(m, x)
        kb = k[b].astype(F32) - dot_tn(x, w[b])
        allowed = notbefore & (aux[sl[b], 0:1] == doc_ref[0, 0:1, sl[b]])
        diag = jnp.where(allowed, diag * scale, -1e30)
        if b > 0:
            start = b * BLOCK
            qt = (q[b].astype(F32) - dot_nn(m, z)).astype(BF)
            qt_ref[0, sl[b], :] = qt
            off = start * (b - 1) // 2
            kt = run[0:start, :].astype(BF)
            kt_ref[0, off : off + start, :] = kt
            side = dot_nt(qt, kt)
            ok = aux[sl[b], 0:1] == doc_ref[0, 0:1, 0:start]
            side = jnp.where(ok, side * scale, -1e30)
            peak = jnp.maximum(jnp.max(diag, 1, keepdims=True), jnp.max(side, 1, keepdims=True))
            ps = jnp.exp(side - peak)
            pd = jnp.exp(diag - peak)
            inv_total = 1.0 / (jnp.sum(ps, 1, keepdims=True) + jnp.sum(pd, 1, keepdims=True))
            ps = (ps * inv_total).astype(BF)
            pd = (pd * inv_total).astype(BF)
            p_refs[b][0, :, 0:start] = ps
            p_refs[b][0, :, start : start + BLOCK] = pd
            o = dot_nn(ps, join_ref[0, 0:start, 2 * d : 3 * d]) + dot_nn(pd, join_ref[0, sl[b], 2 * d : 3 * d])
        else:
            qt_ref[0, sl[b], :] = jnp.zeros((BLOCK, d), BF)
            peak = jnp.max(diag, 1, keepdims=True)
            pd = jnp.exp(diag - peak)
            pd = (pd / jnp.sum(pd, 1, keepdims=True)).astype(BF)
            p_refs[b][0] = pd
            o = dot_nn(pd, join_ref[0, sl[b], 2 * d : 3 * d])
        if part % BLOCK == 0:
            out_ref[(b * BLOCK // part) ^ at_ref[0], b * BLOCK % part : b * BLOCK % part + BLOCK, :] = o.astype(BF)
        else:
            for c in range(BLOCK // part):
                out_ref[(b * BLOCK // part + c) ^ at_ref[0]] = o[c * part : (c + 1) * part].astype(BF)
        if b < nb - 1:
            e = dot_tn(w[b], z).astype(BF)
            e_ref[0, b] = e
            if b > 0:
                run[0:start, :] = run[0:start, :] - dot_nt(kt, e)
            run[sl[b], :] = kb
        else:
            e_ref[0, b] = jnp.zeros((d, d), BF)


def bwd_kernel(taps_n, seq_n, has_prior, at_ref, join_ref, aux_ref, logit_ref, taps_ref, *rest):
    nb = join_ref.shape[1] // BLOCK
    go_parts, rest = rest[:seq_n], rest[seq_n:]
    if has_prior:
        rest = rest[: nb + 8] + rest[nb + 9 :]
    p_refs = rest[:nb]
    (x_ref, n_ref, m_ref, z_ref, qt_ref, w_ref, kt_ref, e_ref, gj_ref, gt_ref, gk, gv, gw, go_ref) = rest[nb:]
    part = go_parts[0].shape[0]
    for m in range(seq_n):
        go_ref[pl.ds(pl.multiple_of((at_ref[0] ^ m) * part, part), part), :] = go_parts[m][...]
    length = join_ref.shape[1]
    d = taps_ref.shape[1]
    head = pl.program_id(1)
    lane = at_ref[0] * pl.num_programs(1) + head
    aux = aux_ref[0]
    beta_all = 2.0 * jax.nn.sigmoid(lane_pick(logit_ref[0].astype(F32), lane))
    row, col = indices(BLOCK, BLOCK)
    later = row > col
    notbefore = row >= col
    scale = d ** -0.5
    gbeta = [None] * nb

    def span(i):
        return pl.ds(pl.multiple_of((4 * head + i) * d, d), d)

    for b in reversed(range(nb)):
        start, end = b * BLOCK, (b + 1) * BLOCK
        s = slice(start, end)
        last = b == nb - 1
        w, q, k = w_ref[0, s, :], join_ref[0, s, 0:d], join_ref[0, s, d : 2 * d]
        beta = beta_all[s]
        x, n, m, z = x_ref[0, b], n_ref[0, b], m_ref[0, b], z_ref[0, s, :]
        go = go_ref[s, :]
        p = p_refs[b][0]
        gp = dot_nt(go, join_ref[0, 0:end, 2 * d : 3 * d])
        pf = p.astype(F32)
        inner = jnp.sum(pf * gp, 1, keepdims=True)
        gs = (pf * (gp - inner) * scale).astype(BF)
        gv_new = dot_tn(p, go)
        gsd = gs[:, start:end]
        if last:
            gv[...] = gv_new
        else:
            gv[0:end, :] += gv_new
        stack_m = [gsd]
        if b > 0:
            off = start * (b - 1) // 2
            kt, qt = kt_ref[0, off : off + start, :], qt_ref[0, s, :]
            gside = gs[:, 0:start]
            gqt_f = dot_nn(gside, kt)
            gqt = gqt_f.astype(BF)
            fresh = dot_tn(gside, qt)
        if not last:
            gkt_f = gk[s, :]
            gkt = gkt_f.astype(BF)
        if b > 0 and not last:
            e = e_ref[0, b]
            old = gk[0:start, :]
            old_b = old.astype(BF)
            ge = (-dot_tn(old_b, kt)).astype(BF)
            gk[0:start, :] = old - dot_nn(old_b, e) + fresh
        elif b > 0:
            gk[0:start, :] = fresh
        gm = dot_nt(gsd, x)
        mt_s = dot_tn(m, gsd)
        gx = -mt_s
        if not last:
            gx = gx - dot_nt(w, gkt)
        gx = jnp.where(later, gx, 0.0).astype(BF)
        y_x = dot_tn(n, gx)
        has_z = b > 0
        if has_z:
            gm = gm + dot_nt(gqt, z)
            gz = -dot_tn(m, gqt)
            if not last:
                gz = gz + dot_nn(w, ge)
            y_z = dot_tn(n, gz.astype(BF))
        gm = jnp.where(notbefore, -gm, 0.0).astype(BF)
        gg = dot_nt(y_x.astype(BF), x)
        if has_z:
            gg = gg + dot_nt(y_z.astype(BF), z)
        gg = jnp.where(later, -gg, 0.0)
        y_x = jnp.where(later, y_x, 0.0)
        gbv = jnp.sum(y_x * dot_nt(w, k) + gg * dot_nt(w, w), 1, keepdims=True)
        by = (beta * y_x).astype(BF)
        bg = (beta * gg).astype(BF)
        gw_b = dot_tn(gm, q) + dot_tn(bg, w) + dot_nn(bg, w) + dot_nn(by, k)
        gq_b = dot_nn(gsd, k) + dot_nn(gm, w)
        gk_b = dot_tn(gsd, q) + dot_tn(by, w)
        if has_z:
            gq_b = gq_b + gqt_f
            gw_b = gw_b + beta * y_z
            gbv = gbv + jnp.sum(y_z * w.astype(F32), 1, keepdims=True)
        if not last:
            gk_b = gk_b + gkt_f
            gw_b = gw_b - dot_nn(x, gkt)
            if has_z:
                gw_b = gw_b + dot_nt(z, ge)
        gbeta[b] = gbv
        gw[s, :] = gw_b
        gj_ref[0, s, span(0)] = gq_b.astype(BF)
        gj_ref[0, s, span(1)] = gk_b.astype(BF)
    gj_ref[0, :, span(2)] = gv[...].astype(BF)
    u = join_ref[0, :, 3 * d : 4 * d].astype(F32)
    w_all, inv = house(u, taps_ref, aux, taps_n)
    gw_all = gw[...]
    gc = inv * (gw_all - w_all * jnp.sum(gw_all * w_all, 1, keepdims=True))
    gu = taps_ref[0:1, :] * gc
    gt = [jnp.sum(gc * u, 0, keepdims=True)]
    for s in range(1, taps_n):
        held = gc * aux[:, s : s + 1]
        gt.append(jnp.sum(held * pltpu.roll(u, s, 0), 0, keepdims=True))
        gu = gu + taps_ref[s : s + 1, :] * pltpu.roll(held, length - s, 0)
    gj_ref[0, :, span(3)] = gu.astype(BF)
    gt.append(jnp.zeros((8 - taps_n, d), F32))
    gt_ref[0, 0] = jnp.concatenate(gt, 0)
    gb_all = jnp.concatenate(gbeta, 0) * beta_all * (1.0 - 0.5 * beta_all)
    pos = lax.broadcasted_iota(jnp.int32, aux.shape, 1)
    mine = jnp.where(pos == lane, gb_all, 0.0).astype(BF)
    tail = slice(gj_ref.shape[2] - 128, gj_ref.shape[2])

    @pl.when(head == 0)
    def _():
        gj_ref[0, :, tail] = mine

    @pl.when(head != 0)
    def _():
        gj_ref[0, :, tail] += mine


def res_specs(length, d, heads):
    nb = length // BLOCK
    shapes = [(BLOCK, (b + 1) * BLOCK) for b in range(nb)]
    shapes += [(nb, BLOCK, BLOCK)] * 3 + [(length, d)] * 3
    shapes += [(max(1, nb * (nb - 1) // 2) * BLOCK, d), (nb, d, d)]
    specs = [
        pl.BlockSpec((1,) + s, functools.partial(lambda n, r, h: (r * heads + h,) + (0,) * n, len(s))) for s in shapes
    ]
    return shapes, specs


def attend_fwd(joined, aux, logit, doc_rows, taps, at, heads, taps_n, seq_n):
    rows, length, packed = joined.shape
    d = taps.shape[1] // heads
    shapes, specs = res_specs(length, d, heads)
    return pl.pallas_call(
        functools.partial(fwd_kernel, taps_n),
        grid=(rows, heads),
        in_specs=[
            pl.BlockSpec(memory_space=pltpu.SMEM),
            pl.BlockSpec((1, length, 4 * d), lambda r, h: (r, 0, h)),
            pl.BlockSpec((1, length, 128), lambda r, h: (r, 0, 0)),
            pl.BlockSpec((1, length, 128), lambda r, h: (r, 0, 0)),
            pl.BlockSpec((1, 8, length), lambda r, h: (r, 0, 0)),
            pl.BlockSpec((8, d), lambda r, h: (0, h)),
        ],
        out_specs=[pl.BlockSpec((seq_n, length // seq_n, d), lambda r, h: (0, 0, h))] + specs,
        out_shape=[jax.ShapeDtypeStruct((seq_n, length // seq_n, heads * d), BF)]
        + [jax.ShapeDtypeStruct((rows * heads,) + s, BF) for s in shapes],
        scratch_shapes=[pltpu.VMEM((length, d), F32)],
        compiler_params=pltpu.CompilerParams(vmem_limit_bytes=56 * 2**20),
        cost_estimate=pl.CostEstimate(
            flops=rows * heads * 8 * 10**9, bytes_accessed=rows * heads * 5 * 10**6, transcendentals=0
        ),
    )(at[None], joined, aux, logit, doc_rows, taps)


def attend_bwd(joined, aux, logit, taps, grad_parts, res, at, heads, taps_n, row, rows_n, prior):
    rows, length, packed = joined.shape
    d = taps.shape[1] // heads
    shapes, specs = res_specs(length, d, heads)
    wide = heads * 4 * d + 128
    seq_n = len(grad_parts)
    args = [at[None], joined, aux, logit, taps, *grad_parts, *res]
    aliases = {}
    if prior is not None:
        aliases = {len(args): 0}
        args.append(prior)
    return pl.pallas_call(
        functools.partial(bwd_kernel, taps_n, seq_n, prior is not None),
        grid=(rows, heads),
        in_specs=[
            pl.BlockSpec(memory_space=pltpu.SMEM),
            pl.BlockSpec((1, length, 4 * d), lambda r, h: (r, 0, h)),
            pl.BlockSpec((1, length, 128), lambda r, h: (r, 0, 0)),
            pl.BlockSpec((1, length, 128), lambda r, h: (r, 0, 0)),
            pl.BlockSpec((8, d), lambda r, h: (0, h)),
        ]
        + [pl.BlockSpec((length // seq_n, d), lambda r, h: (0, h))] * seq_n
        + specs
        + [pl.BlockSpec(memory_space=pl.ANY)] * (0 if prior is None else 1),
        out_specs=[
            pl.BlockSpec((1, length, wide), lambda r, h: (row, 0, 0)),
            pl.BlockSpec((1, 1, 8, d), lambda r, h: (r, h, 0, 0)),
        ],
        out_shape=[
            jax.ShapeDtypeStruct((rows_n, length, wide), BF),
            jax.ShapeDtypeStruct((rows, heads, 8, d), F32),
        ],
        scratch_shapes=[pltpu.VMEM((length, d), F32)] * 3 + [pltpu.VMEM((length, d), BF)],
        input_output_aliases=aliases,
        compiler_params=pltpu.CompilerParams(vmem_limit_bytes=56 * 2**20),
        cost_estimate=pl.CostEstimate(
            flops=rows * heads * 16 * 10**9, bytes_accessed=rows * heads * 6 * 10**6, transcendentals=0
        ),
    )(*args)


def rects_of(sizes, rows):
    rects, at = [], 0
    for i, (r, c) in enumerate(sizes):
        if r == rows:
            rects.append((i, 0, r, 0, c, 0, at))
            at += c
        else:
            wide, rest = r * c // rows, rows - r
            rects.append((i, 0, r, 0, wide, 0, at))
            rects.append((i, 0, rest, wide, wide // 2, r, at))
            rects.append((i, rest, rest, wide, wide // 2, r, at + wide // 2))
            at += wide
    return rects, at


def clip(rects, low, high):
    out = []
    for i, r0, rows, c0, cols, p0, pc in rects:
        a, b = max(p0, low), min(p0 + rows, high)
        if a < b:
            out.append((i, r0 + a - p0, b - a, c0, cols, a - low, pc))
    return out


def ring_order(n):
    return list(range(0, n, 2)) + list(range(n - 1, 0, -2))


def ring_index(steps):
    n = lax.axis_size("dp")
    me = lax.axis_index("dp")
    place = jnp.where(me % 2 == 0, me // 2, n - 1 - me // 2)
    there = (place + jnp.array([(k + n) % n for k in steps], jnp.int32)) % n
    return jnp.where(there < n // 2, 2 * there, 2 * (n - 1 - there) + 1)


def to_right(value):
    order = ring_order(lax.axis_size("dp"))
    return lax.ppermute(value, "dp", [(a, b) for a, b in zip(order, order[1:] + order[:1])])


def to_left(value):
    order = ring_order(lax.axis_size("dp"))
    return lax.ppermute(value, "dp", [(b, a) for a, b in zip(order, order[1:] + order[:1])])


def middle_row(rows):
    return (rows // 2 + 15) // 16 * 16


def ring_gather(own, sent=None):
    n = lax.axis_size("dp")
    cut = middle_row(own.shape[0])
    pieces, steps = [own], [0]
    pair = (own, own)
    for k in range(1, n // 2 + 1):
        if k == n // 2:
            pair = (pair[0][:cut], pair[1][cut:])
        if sent is not None:
            sent[:] = pair
        pair = yield (to_right(pair[0]), to_left(pair[1]))
        pieces += list(pair)
        steps += [-k, k] if k < n // 2 else [k]
    return pieces, ring_index(steps)


def drain(gen, value=None):
    try:
        value = next(gen) if value is None else gen.send(value)
        while True:
            value = gen.send(value)
    except StopIteration as stop:
        return stop.value


def place_kernel(rects, count, cut, index_ref, *refs):
    pieces, outs = refs[:count], refs[count:]
    for w in range(count - 1):
        @pl.when(pl.program_id(0) == w)
        def _():
            for i, r0, rows, c0, cols, p0, pc in rects:
                if w < count - 2:
                    outs[i][r0 : r0 + rows, c0 : c0 + cols] = pieces[w][p0 : p0 + rows, pc : pc + cols]
                    continue
                for piece, low, high in ((pieces[w], 0, cut), (pieces[w + 1], cut, 1 << 20)):
                    for i2, q0, r, d0, c, s0, sc in clip([(i, r0, rows, c0, cols, p0, pc)], low, high):
                        outs[i][q0 : q0 + r, d0 : d0 + c] = piece[s0 : s0 + r, sc : sc + c]


def place(gathered, sizes):
    pieces, index = gathered
    n = lax.axis_size("dp")
    rows = pieces[0].shape[0]
    rects, width = rects_of(sizes, rows)
    return pl.pallas_call(
        functools.partial(place_kernel, rects, len(pieces), middle_row(rows)),
        grid_spec=pltpu.PrefetchScalarGridSpec(
            num_scalar_prefetch=1,
            grid=(n,),
            in_specs=[pl.BlockSpec(p.shape, lambda i, ref: (0, 0)) for p in pieces],
            out_specs=[pl.BlockSpec(size, lambda i, ref: (ref[i], 0)) for size in sizes],
        ),
        out_shape=[jax.ShapeDtypeStruct((n * r, c), BF) for r, c in sizes],
        compiler_params=pltpu.CompilerParams(vmem_limit_bytes=48 * 2**20),
        cost_estimate=pl.CostEstimate(flops=0, bytes_accessed=4 * n * rows * width, transcendentals=0),
    )(index, *pieces)


def join_kernel(rects, lanes, count, has_extra, index_ref, *refs):
    outs, refs = refs[-len(lanes) :], refs[: -len(lanes)]
    srcs, got = refs[: count * len(lanes)], refs[count * len(lanes) :]
    if has_extra:
        extra, got = got[: len(lanes)], got[len(lanes) :]
    for j, (low, high, adds) in enumerate(lanes):
        for i, r0, rows, c0, cols, p0, pc in clip(rects, low, high):
            value = srcs[j * count + i][r0 : r0 + rows, c0 : c0 + cols]
            if not adds:
                outs[j][p0 : p0 + rows, pc : pc + cols] = value
                continue
            total = value.astype(F32)
            spans = []
            for g, first in adds:
                top, end = first, first + got[g].shape[0]
                spans.append((g, top, end))
            if all(top <= p0 and p0 + rows <= end for _, top, end in spans):
                for g, top, _ in spans:
                    total = total + got[g][p0 - top : p0 - top + rows, pc : pc + cols].astype(F32)
                outs[j][p0 : p0 + rows, pc : pc + cols] = total.astype(BF)
            else:
                outs[j][p0 : p0 + rows, pc : pc + cols] = value
                for g, top, end in spans:
                    a, b = max(top, p0), min(end, p0 + rows)
                    if a < b:
                        sub = total[a - p0 : b - p0] + got[g][a - top : b - top, pc : pc + cols].astype(F32)
                        outs[j][a:b, pc : pc + cols] = sub.astype(BF)
        if has_extra:
            tail = slice(outs[j].shape[1] - extra[j].shape[1], outs[j].shape[1])
            outs[j][:, tail] = (outs[j][:, tail].astype(F32) + extra[j][low:high].astype(F32)).astype(BF)


def join(sources, index, received, lanes, extra=None):
    n = lax.axis_size("dp")
    sizes = [(s.shape[0] // n, s.shape[1]) for s in sources]
    rows = max(r for r, _ in sizes)
    rects, width = rects_of(sizes, rows)
    specs, args = [], []
    for j in range(len(lanes)):
        for s, size in zip(sources, sizes):
            specs.append(pl.BlockSpec(size, functools.partial(lambda j, i, ref: (ref[j], 0), j)))
            args.append(s)
    if extra is not None:
        for j in range(len(lanes)):
            specs.append(pl.BlockSpec((rows, extra.shape[1]), functools.partial(lambda j, i, ref: (ref[j], 0), j)))
            args.append(extra)
    for v in received:
        specs.append(pl.BlockSpec(v.shape, lambda i, ref: (0, 0)))
    heights = [high - low for low, high, _ in lanes]
    return pl.pallas_call(
        functools.partial(join_kernel, rects, lanes, len(sources), extra is not None),
        grid_spec=pltpu.PrefetchScalarGridSpec(
            num_scalar_prefetch=1,
            grid=(1,),
            in_specs=specs,
            out_specs=[pl.BlockSpec((h, width), lambda i, ref: (0, 0)) for h in heights],
        ),
        out_shape=[jax.ShapeDtypeStruct((h, width), BF) for h in heights],
        compiler_params=pltpu.CompilerParams(vmem_limit_bytes=48 * 2**20),
        cost_estimate=pl.CostEstimate(
            flops=0, bytes_accessed=6 * sum(heights) * width, transcendentals=0
        ),
    )(index, *args, *received)


def ring_scatter(sources, extra=None, sent=None):
    n = lax.axis_size("dp")
    half = n // 2
    rows = max(s.shape[0] // n for s in sources)
    cut = middle_row(rows)
    out = join(sources, ring_index([half, half]), [], [(0, cut, []), (cut, rows, [])], extra)
    for k in range(half - 1, -1, -1):
        if sent is not None:
            sent[:] = out
        got = yield (to_right(out[0]), to_left(out[1]))
        first = cut if k == half - 1 else 0
        if k > 0:
            out = join(sources, ring_index([k, -k]), got, [(0, rows, [(0, 0)]), (0, rows, [(1, first)])], extra)
    return join(sources, ring_index([0]), got, [(0, rows, [(0, 0), (1, first)])], extra)[0]


def pack_units_kernel(seq_n, at_ref, gate_ref, up_ref, down_ref, out_ref):
    i = pl.program_id(0)
    n = pl.num_programs(0)
    unit = gate_ref.shape[1]
    rows, wide = out_ref.shape
    mine = wide // 3
    out_ref[:, pl.ds(pl.multiple_of(i * unit, unit), unit)] = gate_ref[...].astype(BF)
    out_ref[:, pl.ds(pl.multiple_of(mine + i * unit, unit), unit)] = up_ref[...].astype(BF)

    @pl.when(i == 0)
    def _():
        rects, _ = rects_of([(rows, mine), (rows, mine), down_ref.shape], rows)
        for _, r0, r, c0, c, p0, pc in rects[2:]:
            out_ref[p0 : p0 + r, pc : pc + c] = down_ref[r0 : r0 + r, c0 : c0 + c].astype(BF)


def pack_units(w_gate, w_up, w_down, at):
    dp_n, seq_n = lax.axis_size("dp"), lax.axis_size("seq")
    shard, ff = w_gate.shape
    unit = ff // (dp_n * seq_n)
    mine = dp_n * unit
    if unit % 128:
        def units(w):
            w = w.reshape(shard, dp_n, seq_n, unit)
            return lax.dynamic_index_in_dim(w, at, 2, keepdims=False).astype(BF).reshape(shard, mine)

        down = lax.dynamic_slice_in_dim(w_down, at * unit, unit, 0).astype(BF)
        rects, _ = rects_of([(shard, mine), (shard, mine), down.shape], shard)
        tops = [down[r0 : r0 + r, c0 : c0 + c] for _, r0, r, c0, c, _, _ in rects[2:]]
        folded = jnp.concatenate([tops[0], jnp.concatenate(tops[1:], 1)], 0)
        return jnp.concatenate([units(w_gate), units(w_up), folded], 1)
    return pl.pallas_call(
        functools.partial(pack_units_kernel, seq_n),
        grid_spec=pltpu.PrefetchScalarGridSpec(
            num_scalar_prefetch=1,
            grid=(dp_n,),
            in_specs=[
                pl.BlockSpec((shard, unit), lambda i, ref: (0, i * seq_n + ref[0])),
                pl.BlockSpec((shard, unit), lambda i, ref: (0, i * seq_n + ref[0])),
                pl.BlockSpec((unit, w_down.shape[1]), lambda i, ref: (ref[0], 0)),
            ],
            out_specs=pl.BlockSpec((shard, 3 * mine), lambda i, ref: (0, 0)),
        ),
        out_shape=jax.ShapeDtypeStruct((shard, 3 * mine), BF),
        compiler_params=pltpu.CompilerParams(vmem_limit_bytes=48 * 2**20),
        cost_estimate=pl.CostEstimate(flops=0, bytes_accessed=6 * 3 * shard * mine, transcendentals=0),
    )(at[None], w_gate, w_up, w_down)


def spread_kernel(seq_n, at_ref, *refs):
    gates, ups = refs[:seq_n], refs[seq_n : 2 * seq_n]
    wg_ref, wu_ref, og_ref, ou_ref, gain_ref = refs[2 * seq_n :]
    unit = gates[0].shape[1]
    total = jnp.zeros((wg_ref.shape[0], unit), F32)
    for m in range(seq_n):
        span = pl.ds(pl.multiple_of((at_ref[0] ^ m) * unit, unit), unit)
        for piece, w, out in ((gates[m], wg_ref, og_ref), (ups[m], wu_ref, ou_ref)):
            value = piece[...].astype(F32)
            out[:, span] = value
            total = total + value * w[:, span].astype(BF).astype(F32)

    @pl.when(pl.program_id(0) == 0)
    def _():
        gain_ref[...] = total

    @pl.when(pl.program_id(0) != 0)
    def _():
        gain_ref[...] += total


def unfold_kernel(seq_n, at_ref, *refs):
    pieces, out = refs[:seq_n], refs[seq_n]
    rows, wide = pieces[0].shape
    rects, _ = rects_of([out.shape], rows)
    for m in range(seq_n):
        @pl.when(pl.program_id(0) == m)
        def _():
            for _, r0, r, c0, c, p0, pc in rects:
                out[r0 : r0 + r, c0 : c0 + c] = pieces[m][p0 : p0 + r, pc : pc + c].astype(F32)


def spread_units(rel, w_gate, w_up, w_down, at):
    dp_n, seq_n = lax.axis_size("dp"), lax.axis_size("seq")
    shard, ff = w_gate.shape
    unit = ff // (dp_n * seq_n)
    mine = dp_n * unit
    if unit % 128:
        pieces = in_order(rel, at)

        def spread(start):
            blocks = [g[:, start : start + mine].reshape(shard, dp_n, 1, unit) for g in pieces]
            return jnp.concatenate(blocks, 2).reshape(shard, ff).astype(F32)

        gate, up = spread(0), spread(mine)
        sums = jnp.sum(gate * w_gate.astype(BF).astype(F32) + up * w_up.astype(BF).astype(F32), 1)
        rects, _ = rects_of([(unit, w_down.shape[1])], shard)
        downs = []
        for p in pieces:
            a, b, c = [p[p0 : p0 + r, 2 * mine + pc : 2 * mine + pc + w] for _, _, r, _, w, p0, pc in rects]
            downs.append(jnp.concatenate([a, jnp.concatenate([b, c], 0)], 1))
        return gate, up, jnp.concatenate(downs, 0).astype(F32), sums
    gate, up, sums = pl.pallas_call(
        functools.partial(spread_kernel, seq_n),
        grid_spec=pltpu.PrefetchScalarGridSpec(
            num_scalar_prefetch=1,
            grid=(dp_n,),
            in_specs=[pl.BlockSpec((shard, unit), lambda i, ref: (0, i))] * seq_n
            + [pl.BlockSpec((shard, unit), lambda i, ref: (0, dp_n + i))] * seq_n
            + [pl.BlockSpec((shard, seq_n * unit), lambda i, ref: (0, i))] * 2,
            out_specs=[pl.BlockSpec((shard, seq_n * unit), lambda i, ref: (0, i))] * 2
            + [pl.BlockSpec((shard, unit), lambda i, ref: (0, 0))],
        ),
        out_shape=[jax.ShapeDtypeStruct((shard, ff), F32)] * 2 + [jax.ShapeDtypeStruct((shard, unit), F32)],
        compiler_params=pltpu.CompilerParams(vmem_limit_bytes=48 * 2**20),
        cost_estimate=pl.CostEstimate(flops=0, bytes_accessed=20 * shard * ff, transcendentals=0),
    )(at[None], *rel, *rel, w_gate, w_up)
    down = pl.pallas_call(
        functools.partial(unfold_kernel, seq_n),
        grid_spec=pltpu.PrefetchScalarGridSpec(
            num_scalar_prefetch=1,
            grid=(seq_n,),
            in_specs=[pl.BlockSpec((shard, mine), lambda i, ref: (0, 2))] * seq_n,
            out_specs=pl.BlockSpec((unit, w_down.shape[1]), lambda i, ref: (i ^ ref[0], 0)),
        ),
        out_shape=jax.ShapeDtypeStruct(w_down.shape, F32),
        compiler_params=pltpu.CompilerParams(vmem_limit_bytes=48 * 2**20),
        cost_estimate=pl.CostEstimate(flops=0, bytes_accessed=6 * w_down.size, transcendentals=0),
    )(at[None], *rel)
    return gate, up, down, jnp.sum(sums, 1)


def columns_kernel(seq_n, wide, at_ref, *refs):
    pieces, (w_ref, out_ref, sum_ref) = refs[:seq_n], refs[seq_n:]
    for m in range(seq_n):
        @pl.when(pl.program_id(0) == m)
        def _():
            value = pieces[m][:, :wide].astype(F32)
            out_ref[...] = value
            prod = value * w_ref[...].astype(BF).astype(F32)
            total = prod[:, 0:128]
            for c in range(128, wide, 128):
                total = total + prod[:, c : c + 128]
            if m == 0:
                sum_ref[...] = total
            else:
                sum_ref[...] += total


def spread_columns(rel, w_proj, at):
    seq_n = lax.axis_size("seq")
    rows, wide = w_proj.shape[0], w_proj.shape[1] // seq_n
    grad, sums = pl.pallas_call(
        functools.partial(columns_kernel, seq_n, wide),
        grid_spec=pltpu.PrefetchScalarGridSpec(
            num_scalar_prefetch=1,
            grid=(seq_n,),
            in_specs=[pl.BlockSpec(rel[0].shape, lambda i, ref: (0, 0))] * seq_n
            + [pl.BlockSpec((rows, wide), lambda i, ref: (0, i ^ ref[0]))],
            out_specs=[
                pl.BlockSpec((rows, wide), lambda i, ref: (0, i ^ ref[0])),
                pl.BlockSpec((rows, 128), lambda i, ref: (0, 0)),
            ],
        ),
        out_shape=[jax.ShapeDtypeStruct(w_proj.shape, F32), jax.ShapeDtypeStruct((rows, 128), F32)],
        compiler_params=pltpu.CompilerParams(vmem_limit_bytes=48 * 2**20),
        cost_estimate=pl.CostEstimate(flops=0, bytes_accessed=10 * w_proj.size, transcendentals=0),
    )(at[None], *rel, w_proj)
    return grad, jnp.sum(sums, 1)


def matmul_low(left, right):
    return jnp.dot(left, right, preferred_element_type=F32)


def matmul_tn(left, right):
    return dot_tn(left, right)


def matmul_nt(left, right):
    return dot_nt(left, right)


def inv_rms(values):
    return lax.rsqrt(jnp.mean(values * values, -1, keepdims=True) + NORM_EPS)


def norm_backward(values, scale_inv, gain, grad_norm):
    scaled = grad_norm * gain
    return scale_inv * scaled - values * scale_inv**3 * jnp.mean(scaled * values, -1, keepdims=True)


def after(value, earlier):
    return lax.optimization_barrier((value, earlier))[0]


def swap(value, m):
    n = lax.axis_size("seq")
    return lax.ppermute(value, "seq", [(i, i ^ m) for i in range(n)])


def gather_rel(own):
    far = swap(own, 2)
    return [own, swap(own, 1), far, swap(far, 1)]


def in_order(rel, seq_at):
    odd = seq_at % 2 == 1
    high = seq_at // 2 == 1
    pairs = []
    for a, b in (rel[0:2], rel[2:4]):
        pairs.append((jnp.where(odd, b, a), jnp.where(odd, a, b)))
    (a0, a1), (b0, b1) = pairs
    return [jnp.where(high, b0, a0), jnp.where(high, b1, a1), jnp.where(high, a0, b0), jnp.where(high, a1, b1)]


def project_kernel(count, lane, has_prior, at_ref, *refs):
    pieces = refs[:count]
    w_ref, b_ref = refs[count : count + 2]
    norm_ref, join_ref, logit_ref, gains_ref = refs[count + (3 if has_prior else 2) :]
    part = pieces[0].shape[0]

    @pl.when(pl.program_id(0) == 0)
    def _():
        i, j = indices(8, 128)
        gains_ref[...] = dot_nt(jnp.where(j == lane + i, 1.0, 0.0).astype(BF), b_ref[...])
        for m in range(count):
            x = pieces[m][...].astype(F32)
            here = pl.ds(pl.multiple_of((at_ref[0] ^ m) * part, part), part)
            norm_ref[0, here, :] = (x * inv_rms(x) * gains_ref[0:1, :]).astype(BF)
        logit_ref[0] = dot_nn(norm_ref[0], b_ref[...]).astype(BF)

    join_ref[0] = dot_nn(norm_ref[0], w_ref[...]).astype(BF)


def project(pieces, lane, w_side, wide, at, r, rows_n, prior):
    count = len(pieces)
    part, model = pieces[0].shape
    length = part * count
    tile = 256
    hold = pl.Buffered(1)

    def whole(shape, **more):
        return pl.BlockSpec(shape, lambda j, ref: (0,) * len(shape), **more)

    args = [at[None], *pieces, w_side, w_side]
    aliases = {}
    if prior is not None:
        aliases = {len(args): 0}
        args.append(prior)
    return pl.pallas_call(
        functools.partial(project_kernel, count, lane, prior is not None),
        grid_spec=pltpu.PrefetchScalarGridSpec(
            num_scalar_prefetch=1,
            grid=(wide // tile,),
            in_specs=[whole((part, model), pipeline_mode=hold)] * count
            + [
                pl.BlockSpec((model, tile), lambda j, ref: (0, j)),
                pl.BlockSpec((model, 128), lambda j, ref: (0, wide // 128)),
            ]
            + [pl.BlockSpec(memory_space=pl.ANY)] * (0 if prior is None else 1),
            out_specs=[
                pl.BlockSpec((1, length, model), lambda j, ref: (r, 0, 0)),
                pl.BlockSpec((1, length, tile), lambda j, ref: (0, 0, j)),
                whole((1, length, 128)),
                whole((8, model)),
            ],
        ),
        out_shape=[
            jax.ShapeDtypeStruct((rows_n, length, model), BF),
            jax.ShapeDtypeStruct((1, length, wide), BF),
            jax.ShapeDtypeStruct((1, length, 128), BF),
            jax.ShapeDtypeStruct((8, model), F32),
        ],
        input_output_aliases=aliases,
        compiler_params=pltpu.CompilerParams(vmem_limit_bytes=56 * 2**20),
        cost_estimate=pl.CostEstimate(
            flops=2 * length * model * wide, bytes_accessed=6 * length * model, transcendentals=0
        ),
    )(*args)


def hidden_kernel(seq_n, has_prior, *refs):
    two, top = refs[:seq_n], refs[seq_n : 2 * seq_n]
    wg_ref, wu_ref, wd_ref = refs[2 * seq_n : 2 * seq_n + 3]
    hid_ref, gg_ref, gu_ref, two_ref, top_ref = refs[2 * seq_n + (6 if has_prior else 3) :]
    part = two[0].shape[0]

    @pl.when(pl.program_id(0) == 0)
    def _():
        for m in range(seq_n):
            s = slice(m * part, (m + 1) * part)
            two_ref[s, :] = two[m][...]
            top_ref[s, :] = top[m][...]

    gate = dot_nn(two_ref[...], wg_ref[...])
    up = dot_nn(two_ref[...], wu_ref[...])
    gh = dot_nt(top_ref[...], wd_ref[...])
    sig = jax.nn.sigmoid(gate)
    act = gate * sig
    hid_ref[0] = (act * up).astype(BF)
    gg_ref[0] = (gh * up * sig * (1.0 + gate * (1.0 - sig))).astype(BF)
    gu_ref[0] = (gh * act).astype(BF)


def hidden_units(two, top, gate_full, up_full, down_full, r, rows_n, prior):
    seq_n = len(two)
    part, model = two[0].shape
    mine = gate_full.shape[1]
    tile = 256
    length = part * seq_n
    piece = pl.BlockSpec((part, model), lambda j: (0, 0), pipeline_mode=pl.Buffered(1))
    columns = pl.BlockSpec((model, tile), lambda j: (0, j))
    hidden = pl.BlockSpec((1, length, tile), lambda j: (r, 0, j))
    args = [*two, *top, gate_full, up_full, down_full]
    aliases = {}
    if prior is not None:
        aliases = {len(args) + i: i for i in range(3)}
        args += prior
    return pl.pallas_call(
        functools.partial(hidden_kernel, seq_n, prior is not None),
        grid=(mine // tile,),
        in_specs=[piece] * (2 * seq_n)
        + [columns, columns, pl.BlockSpec((tile, model), lambda j: (j, 0))]
        + [pl.BlockSpec(memory_space=pl.ANY)] * (3 if prior is not None else 0),
        out_specs=[hidden] * 3,
        out_shape=[jax.ShapeDtypeStruct((rows_n, length, mine), BF)] * 3,
        scratch_shapes=[pltpu.VMEM((length, model), BF)] * 2,
        input_output_aliases=aliases,
        compiler_params=pltpu.CompilerParams(vmem_limit_bytes=56 * 2**20),
        cost_estimate=pl.CostEstimate(
            flops=6 * length * model * mine, bytes_accessed=8 * length * model + 6 * model * mine, transcendentals=0
        ),
    )(*args)


def model_kernel(seq_n, hid_ref, gg_ref, gu_ref, wg_ref, wu_ref, wd_ref, *outs):
    part = outs[0].shape[0]
    back = dot_nt(gg_ref[0], wg_ref[...]) + dot_nt(gu_ref[0], wu_ref[...])
    for m in range(seq_n):
        outs[m][...] = back[m * part : (m + 1) * part].astype(BF)
    fore = dot_nn(hid_ref[0], wd_ref[...])
    for m in range(seq_n):
        outs[seq_n + m][...] = fore[m * part : (m + 1) * part].astype(BF)


def model_units(units, gate_full, up_full, down_full, r, seq_n):
    hid, gg, gu = units[:3]
    rows_n, length, mine = hid.shape
    model = gate_full.shape[0]
    part = length // seq_n
    tile = 256
    hold = pl.BlockSpec((1, length, mine), lambda j: (r, 0, 0), pipeline_mode=pl.Buffered(1))
    rows = pl.BlockSpec((tile, mine), lambda j: (j, 0))
    outs = pl.pallas_call(
        functools.partial(model_kernel, seq_n),
        grid=(model // tile,),
        in_specs=[hold] * 3 + [rows, rows, pl.BlockSpec((mine, tile), lambda j: (0, j))],
        out_specs=[pl.BlockSpec((part, tile), lambda j: (0, j))] * (2 * seq_n),
        out_shape=[jax.ShapeDtypeStruct((part, model), BF)] * (2 * seq_n),
        compiler_params=pltpu.CompilerParams(vmem_limit_bytes=56 * 2**20),
        cost_estimate=pl.CostEstimate(
            flops=6 * length * model * mine, bytes_accessed=8 * length * model + 6 * model * mine, transcendentals=0
        ),
    )(hid, gg, gu, gate_full, up_full, down_full)
    return outs[:seq_n], outs[seq_n:]


def outer_kernel(lefts, counts, *refs):
    left, refs = refs[:lefts], refs[lefts:]
    groups = []
    for n in counts:
        groups.append(refs[:n])
        refs = refs[n:]
    outs, scratch = refs[: len(counts)], list(refs[len(counts) :])

    def gather(pieces, into):
        row = 0
        for p in pieces:
            into[row : row + p.shape[0], :] = p[...]
            row += p.shape[0]

    if lefts > 1:
        tall = scratch.pop(0)
        gather(left, tall)
    else:
        tall = left[0]
    for n, group, out in zip(counts, groups, outs):
        if n > 1:
            whole = scratch.pop(0)

            @pl.when(pl.program_id(0) == 0)
            def _():
                gather(group, whole)
        else:
            whole = group[0]
        out[...] = dot_tn(tall[...], whole[...]).astype(BF)


def outer(left, rights):
    total = sum(p.shape[0] for p in left)
    model = left[0].shape[1]
    tile = 256
    hold = pl.Buffered(1)
    scratch = [pltpu.VMEM((total, tile), BF)] if len(left) > 1 else []
    scratch += [pltpu.VMEM((total, g[0].shape[1]), BF) for g in rights if len(g) > 1]
    return pl.pallas_call(
        functools.partial(outer_kernel, len(left), [len(g) for g in rights]),
        grid=(model // tile,),
        in_specs=[pl.BlockSpec((p.shape[0], tile), lambda j: (0, j)) for p in left]
        + [pl.BlockSpec(p.shape, lambda j: (0, 0), pipeline_mode=hold) for g in rights for p in g],
        out_specs=[pl.BlockSpec((tile, g[0].shape[1]), lambda j: (j, 0)) for g in rights],
        out_shape=[jax.ShapeDtypeStruct((model, g[0].shape[1]), BF) for g in rights],
        scratch_shapes=scratch,
        compiler_params=pltpu.CompilerParams(vmem_limit_bytes=56 * 2**20),
        cost_estimate=pl.CostEstimate(
            flops=2 * total * model * sum(g[0].shape[1] for g in rights),
            bytes_accessed=2 * total * (model + sum(g[0].shape[1] for g in rights)),
            transcendentals=0,
        ),
    )(*left, *[p for g in rights for p in g])


def middle_kernel(count, at_ref, *refs):
    parts, outs_w = refs[:count], refs[count : 2 * count]
    x_ref, gain_ref, mixed_ref, mid_ref, two_ref = refs[2 * count :]
    cols = parts[0].shape[1]
    spans = [pl.ds(pl.multiple_of((at_ref[0] ^ m) * cols, cols), cols) for m in range(count)]
    for m in range(count):
        mixed_ref[:, spans[m]] = parts[m][...]
    mixed = mixed_ref[...]
    for m in range(count):
        mid_ref[:, spans[m]] = x_ref[:, spans[m]].astype(F32) + dot_nn(mixed, outs_w[m][...])
    mid = mid_ref[...]
    two_ref[...] = (mid * inv_rms(mid) * gain_ref[...]).astype(BF)


def to_middle(parts, out_rel, x, gain, at):
    part, model = x.shape
    count = len(parts)
    return pl.pallas_call(
        functools.partial(middle_kernel, count),
        in_specs=[pl.BlockSpec(memory_space=pltpu.SMEM)] + [pl.BlockSpec(memory_space=pltpu.VMEM)] * (2 * count + 2),
        out_specs=[pl.BlockSpec(memory_space=pltpu.VMEM)] * 3,
        out_shape=[
            jax.ShapeDtypeStruct((part, model), BF),
            jax.ShapeDtypeStruct((part, model), F32),
            jax.ShapeDtypeStruct((part, model), BF),
        ],
        compiler_params=pltpu.CompilerParams(vmem_limit_bytes=48 * 2**20),
        cost_estimate=pl.CostEstimate(flops=2 * part * model * model, bytes_accessed=3 * model * model, transcendentals=0),
    )(at[None], *parts, *out_rel, x, gain)


def second_kernel(count, at_ref, *refs):
    outs_w = refs[:count]
    own_ref, near_ref, far_ref, mid_ref, g_ref, gain_ref, grad_ref, low_ref = refs[count : count + 8]
    parts, mixed = refs[count + 8 : 2 * count + 8], refs[2 * count + 8]
    cols = parts[0].shape[1]
    spans = [pl.ds(pl.multiple_of((at_ref[0] ^ m) * cols, cols), cols) for m in range(count)]
    got = own_ref[...].astype(F32) + near_ref[...].astype(F32) + far_ref[...].astype(F32)
    mid = mid_ref[...]
    grad_ref[...] = g_ref[...].astype(F32) + norm_backward(mid, inv_rms(mid), gain_ref[...], got)
    low_ref[...] = grad_ref[...].astype(BF)
    total = dot_nt(low_ref[:, spans[0]], outs_w[0][...])
    for m in range(1, count):
        total = total + dot_nt(low_ref[:, spans[m]], outs_w[m][...])
    mixed[...] = total
    for m in range(count):
        parts[m][...] = mixed[:, spans[m]].astype(BF)


def second_back(own, near, far, mid, grad_top, gain, out_rel, at):
    part, model = mid.shape
    count = len(out_rel)
    cols = out_rel[0].shape[1]
    outs = pl.pallas_call(
        functools.partial(second_kernel, count),
        in_specs=[pl.BlockSpec(memory_space=pltpu.SMEM)] + [pl.BlockSpec(memory_space=pltpu.VMEM)] * (count + 6),
        out_specs=[pl.BlockSpec(memory_space=pltpu.VMEM)] * (count + 2),
        out_shape=[jax.ShapeDtypeStruct((part, model), F32), jax.ShapeDtypeStruct((part, model), BF)]
        + [jax.ShapeDtypeStruct((part, cols), BF)] * count,
        scratch_shapes=[pltpu.VMEM((part, model), F32)],
        compiler_params=pltpu.CompilerParams(vmem_limit_bytes=48 * 2**20),
        cost_estimate=pl.CostEstimate(flops=2 * part * model * model, bytes_accessed=3 * model * model, transcendentals=0),
    )(at[None], *out_rel, own, near, far, mid, grad_top, gain)
    return outs[0], outs[1], outs[2:]


def out_kernel(count, rows_n, at_ref, *refs):
    mixed, low, outs = refs[:rows_n], refs[rows_n : 2 * rows_n], refs[2 * rows_n :]
    cols = outs[0].shape[1]
    for m in range(count):
        span = pl.ds(pl.multiple_of((at_ref[0] ^ m) * cols, cols), cols)
        total = dot_tn(mixed[0][...], low[0][:, span])
        for r in range(1, rows_n):
            total = total + dot_tn(mixed[r][...], low[r][:, span])
        outs[m][...] = total.astype(BF)


def grad_out_parts(mixed, low, count, at):
    part, model = mixed[0].shape
    rows_n = len(mixed)
    cols = model // count
    tile = 256
    return pl.pallas_call(
        functools.partial(out_kernel, count, rows_n),
        grid_spec=pltpu.PrefetchScalarGridSpec(
            num_scalar_prefetch=1,
            grid=(model // tile,),
            in_specs=[pl.BlockSpec((part, tile), lambda j, ref: (0, j))] * rows_n
            + [pl.BlockSpec((part, model), lambda j, ref: (0, 0))] * rows_n,
            out_specs=[pl.BlockSpec((tile, cols), lambda j, ref: (j, 0))] * count,
        ),
        out_shape=[jax.ShapeDtypeStruct((model, cols), BF)] * count,
        compiler_params=pltpu.CompilerParams(vmem_limit_bytes=48 * 2**20),
        cost_estimate=pl.CostEstimate(flops=4 * part * model * model, bytes_accessed=3 * model * model, transcendentals=0),
    )(at[None], *mixed, *low)


def first_kernel(count, at_ref, grad_ref, w_ref, *refs):
    outs, total = refs[:count], refs[count]
    part = outs[0].shape[0]
    total[...] = dot_nt(grad_ref[0], w_ref[...])
    for m in range(count):
        here = pl.ds(pl.multiple_of((at_ref[0] ^ m) * part, part), part)
        outs[m][...] = total[here, :].astype(BF)


def first_parts(grad_joined, w_side, r, count, at):
    _, length, wide = grad_joined.shape
    model = w_side.shape[0]
    part = length // count
    tile = 256
    return pl.pallas_call(
        functools.partial(first_kernel, count),
        grid_spec=pltpu.PrefetchScalarGridSpec(
            num_scalar_prefetch=1,
            grid=(model // tile,),
            in_specs=[
                pl.BlockSpec((1, length, wide), lambda j, ref: (r, 0, 0), pipeline_mode=pl.Buffered(1)),
                pl.BlockSpec((tile, wide), lambda j, ref: (j, 0)),
            ],
            out_specs=[pl.BlockSpec((part, tile), lambda j, ref: (0, j))] * count,
            scratch_shapes=[pltpu.VMEM((length, tile), F32)],
        ),
        out_shape=[jax.ShapeDtypeStruct((part, model), BF)] * count,
        compiler_params=pltpu.CompilerParams(vmem_limit_bytes=48 * 2**20),
        cost_estimate=pl.CostEstimate(
            flops=2 * length * wide * model, bytes_accessed=4 * length * wide, transcendentals=0
        ),
    )(at[None], grad_joined, w_side)


def last_kernel(rows_n, *refs):
    owns, nears, fars, mids = [refs[i * rows_n : (i + 1) * rows_n] for i in range(4)]
    x_ref, gain_ref, out_ref = refs[4 * rows_n :]
    for r in range(rows_n):
        got = owns[r][...].astype(F32) + nears[r][...].astype(F32) + fars[r][...].astype(F32)
        x = x_ref[r].astype(F32)
        out_ref[r] = mids[r][...] + norm_backward(x, inv_rms(x), gain_ref[...], got)


def grad_input(own, near, far, mids, x, gain):
    return pl.pallas_call(
        functools.partial(last_kernel, len(mids)),
        out_shape=jax.ShapeDtypeStruct(x.shape, F32),
        compiler_params=pltpu.CompilerParams(vmem_limit_bytes=48 * 2**20),
        cost_estimate=pl.CostEstimate(flops=0, bytes_accessed=16 * x.size, transcendentals=0),
    )(*own, *near, *far, *mids, x, gain)


def layer_kernel(rows_n, *refs):
    owns, nears, fars, mids = [refs[i * rows_n : (i + 1) * rows_n] for i in range(4)]
    for r in range(rows_n):
        got = owns[r][...].astype(F32) + nears[r][...].astype(F32) + fars[r][...].astype(F32)
        refs[-1][r] = (mids[r][...] + got).astype(BF)


def layer_sum(own, near, far, mids):
    rows_n = len(mids)
    return pl.pallas_call(
        functools.partial(layer_kernel, rows_n),
        out_shape=jax.ShapeDtypeStruct((rows_n,) + mids[0].shape, BF),
        compiler_params=pltpu.CompilerParams(vmem_limit_bytes=48 * 2**20),
        cost_estimate=pl.CostEstimate(flops=0, bytes_accessed=12 * rows_n * mids[0].size, transcendentals=0),
    )(*own, *near, *far, *mids)


def fold(part, passed):
    return (part.astype(F32) + passed.astype(F32)).astype(BF)


def tie(*groups):
    return lax.optimization_barrier(groups)


def per_device(
    inputs,
    doc_ids,
    gain_attn,
    w_proj,
    w_beta,
    conv_taps,
    w_out,
    gain_mlp,
    w_gate,
    w_up,
    w_down,
    out_grad,
):
    rows_n, part, model = inputs.shape
    heads_n = w_beta.shape[1]
    taps_n, width_out = conv_taps.shape
    dp_n, seq_n = lax.axis_size("dp"), lax.axis_size("seq")
    at = lax.axis_index("seq")
    length = part * seq_n
    heads = heads_n // seq_n
    width = model // heads_n
    cols = heads * width
    wide = 4 * cols
    shard = w_proj.shape[0]
    ff = w_gate.shape[1]
    unit = ff // (dp_n * seq_n)
    mine_n = dp_n * unit
    quarter = model // seq_n
    rows = range(rows_n)
    last = rows_n - 1

    proj_mine = lax.dynamic_slice_in_dim(w_proj, at * wide, wide, 1)
    side = jnp.concatenate([w_beta, gain_attn[:, None], gain_mlp[:, None]], 1)
    side = jnp.pad(side.astype(BF), ((0, 0), (0, 126 - heads_n)))
    packed = jnp.concatenate([proj_mine.astype(BF), side], 1)
    sent = []
    ring = ring_gather(packed, sent)
    hop = next(ring)

    flat = jnp.concatenate([doc_ids.astype(BF).reshape(-1), conv_taps.astype(BF).reshape(-1)])
    flat = after(flat, packed)
    flat = [flat, swap(flat, 1), swap(flat, 2), swap(flat, 3)]
    own_x = after(inputs, flat)
    own_x = [own_x[r] for r in rows]
    far_x = [swap(x, 2) for x in own_x]
    near_x = [swap(x, 1) for x in own_x]
    hop, flat = tie(hop, flat)
    hop = ring.send(hop)
    flat, _ = tie(flat, sent)
    flat = in_order(flat, at)
    cut = rows_n * part
    doc = jnp.concatenate([t[:cut].reshape(rows_n, part) for t in flat], 1).astype(F32)
    taps_shard = jnp.concatenate([t[cut:].reshape(taps_n, width_out) for t in flat], 1)
    taps_shard = jnp.pad(taps_shard, ((0, 16 - taps_n), (0, quarter - taps_shard.shape[1])))
    out_mine = lax.dynamic_slice_in_dim(w_out, at * quarter, quarter, 1).astype(BF)
    out_mine = lax.all_gather(jnp.concatenate([out_mine, taps_shard], 0), "dp", axis=0)
    units = pack_units(w_gate, w_up, w_down, at)
    hop, units, near_x, doc = tie(hop, units, near_x, doc)
    hop = ring.send(hop)
    doc, _ = tie(doc, sent)
    lanes = lax.broadcasted_iota(jnp.int32, (1, 1, 128), 2)
    info = jnp.where(lanes == 0, doc[:, :, None], 0.0)
    for shift_by in range(1, taps_n):
        same = (doc[:, shift_by:] == doc[:, :-shift_by]).astype(F32)
        info = jnp.where(lanes == shift_by, jnp.pad(same, ((0, 0), (shift_by, 0)))[:, :, None], info)
    aux = [info[r : r + 1] for r in rows]
    doc_rows = [jnp.broadcast_to(doc[r : r + 1, None, :], (1, 8, length)) for r in rows]
    hop, far_x, aux, doc_rows = tie(hop, far_x, aux, doc_rows)
    hop = ring.send(hop)
    far_x, _ = tie(far_x, sent)
    skew_x = [swap(x, 1) for x in far_x]
    hop, skew_x = tie(hop, skew_x)
    gathered = drain(ring, hop)
    x_rel = [list(v) for v in zip(own_x, near_x, far_x, skew_x)]

    ring = ring_gather(after(units, gathered[0]), sent)
    hop = next(ring)
    gathered = (gathered[0], after(gathered[1], sent))
    (proj_full,) = place(gathered, [(shard, packed.shape[1])])
    own_g = after([out_grad[r] for r in rows], skew_x)
    far_g = [swap(g, 2) for g in own_g]
    normed, joined, logit = None, [], []
    for r in rows:
        normed, j, l, gains = project(x_rel[r], heads_n, proj_full, wide, at, r, rows_n, normed)
        joined.append(j)
        logit.append(l)
    gain_one, gain_two = gains[0:1], gains[1:2]
    hop, joined, logit, out_mine = tie(hop, joined, logit, out_mine)
    hop = ring.send(hop)
    joined, out_mine, own_g, _ = tie(joined, out_mine, own_g, sent)
    taps_full = out_mine[:, shard : shard + taps_n, :shard].transpose(1, 0, 2).reshape(taps_n, model)
    taps_mine = lax.dynamic_slice_in_dim(taps_full.astype(F32), at * cols, cols, 1)
    taps_mine = jnp.pad(taps_mine, ((0, 8 - taps_n), (0, 0)))
    out_mine = out_mine[:, :shard].reshape(model, quarter)
    out_far, out_near = swap(out_mine, 2), swap(out_mine, 1)
    near_g = [swap(g, 1) for g in own_g]

    def exchange(parts):
        return [parts[0]] + [swap(parts[m], m) for m in range(1, seq_n)]

    kept, mixed_rel = [], []
    for r in rows:
        outs = attend_fwd(joined[r], aux[r], logit[r], doc_rows[r], taps_mine, at, heads, taps_n, seq_n)
        if r == 0:
            outs, hop, joined, out_far, out_near, near_g, far_g = tie(
                outs, hop, joined, out_far, out_near, near_g, far_g
            )
            out_skew = swap(out_far, 1)
            skew_g = [swap(g, 1) for g in far_g]
        elif r == last:
            outs, hop, mixed_rel, out_skew, skew_g = tie(outs, hop, mixed_rel, out_skew, skew_g)
        hop = ring.send(hop)
        mine = [outs[0][m] for m in range(seq_n)]
        if r == 0:
            mine, joined, _ = tie(mine, joined, sent)
        else:
            mine, mixed_rel, _ = tie(mine, mixed_rel, sent)
        mixed_rel.append(exchange(mine))
        kept.append(outs[1:])
    out_rel = [out_mine, out_near, out_far, out_skew]
    g_rel = [list(v) for v in zip(own_g, near_g, far_g, skew_g)]
    mixed, middle, two_rel = [], [], []
    for r in rows:
        mix, mid, two = to_middle(mixed_rel[r], out_rel, inputs[r], gain_two, at)
        if r < last:
            mix, mid, two, mixed_rel[r + 1] = tie(mix, mid, two, mixed_rel[r + 1])
        else:
            mix, mid, two, hop = tie(mix, mid, two, hop)
        mixed.append(mix)
        middle.append(mid)
        two_rel.append([two, swap(two, 1), swap(two, 2)])
    gathered = drain(ring, hop)
    full = place(gathered, [(shard, mine_n), (shard, mine_n), (unit, model)])
    full, two_rel[0] = tie(full, two_rel[0])

    prior, layer_parts, norm_parts, near_n, pass_n, near_l, pass_l = None, [], [], [], [], [], []
    for r in rows:
        two_rel[r].append(swap(two_rel[r][2], 1))
        prior = hidden_units(two_rel[r], g_rel[r], *full, r, rows_n, prior)
        if r == 0:
            prior, two_rel[1] = tie(prior, two_rel[1])
        if r == last:
            prior, near_n, pass_n = tie(prior, near_n, pass_n)
            far_n = [fold(norm_parts[0][2], pass_n[0])]
            prior, far_n = tie(prior, far_n)
            far_n = [swap(far_n[0], 2)]
        back, fore = model_units(prior, *full, r, seq_n)
        norm_parts.append(back)
        layer_parts.append(fore)
        if r < last:
            near_n.append(swap(back[1], 1))
            pass_n.append(swap(back[3], 1))
    hid, g_gate, g_up = [v.reshape(rows_n * length, -1) for v in prior]

    norm_parts[last], layer_parts[last], hid, far_n = tie(norm_parts[last], layer_parts[last], hid, far_n)
    near_n.append(swap(norm_parts[last][1], 1))
    pass_n.append(swap(norm_parts[last][3], 1))

    def second(r):
        return second_back(
            norm_parts[r][0], near_n[r], far_n[r], middle[r], out_grad[r], gain_two, out_rel, at
        )

    done = [second(0)]
    done[0], hid, near_n, pass_n = tie(done[0], hid, near_n, pass_n)
    heads_rel = [exchange(done[0][2])]
    far_n.append(fold(norm_parts[last][2], pass_n[last]))
    hid, far_n[last] = tie(hid, far_n[last])
    far_n[last] = swap(far_n[last], 2)
    (grad_down,) = outer([hid], [[p for rel in g_rel for p in rel]])
    grad_down, g_gate, heads_rel, layer_parts = tie(grad_down, g_gate, heads_rel, layer_parts)
    near_l = [swap(layer_parts[r][1], 1) for r in rows]
    pass_l = [swap(layer_parts[r][3], 1) for r in rows]
    grad_gate, grad_up = outer([p for rel in two_rel for p in rel], [[g_gate], [g_up]])
    grad_gate, grad_up, far_n, near_l, pass_l = tie(grad_gate, grad_up, far_n, near_l, pass_l)
    ring = ring_scatter([grad_gate, grad_up, grad_down], None, sent)
    hop = next(ring)
    far_n, _ = tie(far_n, sent)
    done.append(second(last))
    grad_mid, low = [d[0] for d in done], [d[1] for d in done]
    out_parts = grad_out_parts(mixed, low, seq_n, at)
    hop, out_parts, done[last], grad_mid = tie(hop, out_parts, done[last], grad_mid)
    hop = ring.send(hop)
    far_l = [fold(layer_parts[0][2], pass_l[0])]
    out_parts, parts, heads_rel, far_l, _ = tie(out_parts, done[last][2], heads_rel, far_l, sent)
    heads_rel.append(exchange(parts))
    near_out, pass_out = swap(out_parts[1], 1), swap(out_parts[3], 1)
    far_l = [swap(far_l[0], 2)]

    grad_joined, grad_taps = None, []
    for r in rows:
        outs = attend_bwd(
            joined[r], aux[r], logit[r], taps_mine, heads_rel[r], kept[r], at, heads, taps_n, r, rows_n, grad_joined
        )
        if r == 0:
            outs, hop, heads_rel, near_out, pass_out, far_l = tie(outs, hop, heads_rel, near_out, pass_out, far_l)
            hop = ring.send(hop)
            far_out = fold(out_parts[2], pass_out)
            far_l.append(fold(layer_parts[last][2], pass_l[last]))
            heads_rel, far_out, far_l, _ = tie(heads_rel, far_out, far_l, sent)
            far_out = swap(far_out, 2)
            far_l[last] = swap(far_l[last], 2)
        if r == last:
            outs, hop, far_out = tie(outs, hop, far_out)
            hop = ring.send(hop)
            outs, far_out, _ = tie(outs, far_out, sent)
        grad_joined = outs[0]
        grad_taps.append(outs[1][0])
    grad_out = out_parts[0].astype(F32) + near_out.astype(F32) + far_out.astype(F32)
    grad_out = lax.psum_scatter(grad_out.astype(BF), "dp", scatter_dimension=0, tiled=True)

    taps_grad = sum(grad_taps)[:, :taps_n].transpose(1, 0, 2).reshape(taps_n, cols)
    taps_grad = lax.dynamic_update_slice_in_dim(jnp.zeros((taps_n, model), F32), taps_grad, at * cols, 1)
    taps_grad = jnp.pad(taps_grad.T.astype(BF), ((0, 0), (heads_n, 128 - heads_n - taps_n)))
    (grad_proj,) = outer([normed.reshape(rows_n * length, model)], [[grad_joined.reshape(rows_n * length, -1)]])
    late = ring_scatter([grad_proj], taps_grad, sent)
    late_hop = next(late)

    grad_joined, _ = tie(grad_joined, sent)
    parts = [first_parts(grad_joined, proj_full, 0, seq_n, at)]
    late_hop, hop, parts = tie(late_hop, hop, parts)
    late_hop = late.send(late_hop)
    hop, grad_joined, parts, _ = tie(hop, grad_joined, parts, sent)
    grad_units = drain(ring, hop)
    grad_units, grad_joined = tie(grad_units, grad_joined)
    units_far, units_near = swap(grad_units, 2), swap(grad_units, 1)
    near_in, pass_in = [swap(parts[0][1], 1)], [swap(parts[0][3], 1)]
    for r in rows[1:]:
        parts.append(first_parts(grad_joined, proj_full, r, seq_n, at))
    late_hop, parts, units_near, near_in, pass_in = tie(late_hop, parts, units_near, near_in, pass_in)
    late_hop = late.send(late_hop)
    far_in = [fold(parts[0][2], pass_in[0])]
    layer_parts, far_in, parts, _ = tie(layer_parts, far_in, parts, sent)
    far_in = [swap(far_in[0], 2)]
    for r in rows[1:]:
        near_in.append(swap(parts[r][1], 1))
        pass_in.append(swap(parts[r][3], 1))
    layer_out = layer_sum([p[0] for p in layer_parts], near_l, far_l, middle)
    layer_out, near_in, pass_in, units_far = tie(layer_out, near_in, pass_in, units_far)
    for r in rows[1:]:
        far_in.append(swap(fold(parts[r][2], pass_in[r]), 2))
    units_rel = [grad_units, units_near, units_far, swap(units_far, 1)]
    gate_out, up_out, down_out, sums = spread_units(units_rel, w_gate, w_up, w_down, at)
    gain_two_out = sums / gain_mlp.astype(BF).astype(F32)
    late_hop, gate_out, up_out, down_out, gain_two_out = tie(late_hop, gate_out, up_out, down_out, gain_two_out)
    late_hop = late.send(late_hop)
    far_in, grad_out, _ = tie(far_in, grad_out, sent)
    grad_in = grad_input([p[0] for p in parts], near_in, far_in, grad_mid, inputs, gain_one)
    out_far, out_near = swap(grad_out, 2), swap(grad_out, 1)
    late_hop, grad_in, out_far, out_near = tie(late_hop, grad_in, out_far, out_near)
    grad_proj = drain(late, late_hop)
    proj_far, proj_near, out_skew = swap(grad_proj, 2), swap(grad_proj, 1), swap(out_far, 1)
    out_out = jnp.concatenate(in_order([grad_out, out_near, out_far, out_skew], at), 1).astype(F32)
    proj_far, out_out = tie(proj_far, out_out)
    rel = [grad_proj, proj_near, proj_far, swap(proj_far, 1)]
    proj_out, sums = spread_columns(rel, w_proj, at)
    tail = [t[:, wide:].astype(F32) for t in rel]
    tail = (tail[0] + tail[1]) + (tail[2] + tail[3])
    beta_out = tail[:, :heads_n]
    sums = sums + jnp.sum(beta_out * w_beta.astype(BF).astype(F32), 1)
    gain_one_out = sums / gain_attn.astype(BF).astype(F32)
    taps_out = lax.dynamic_slice_in_dim(tail[:, heads_n : heads_n + taps_n], at * width_out, width_out, 0).T
    return (
        layer_out,
        grad_in,
        gain_one_out,
        proj_out,
        beta_out,
        taps_out,
        out_out,
        gain_two_out,
        gate_out,
        up_out,
        down_out,
    )


def solution(mesh):
    in_specs = (
        P("dp", "seq", None),
        P("dp", "seq"),
        P("dp"),
        P("dp", None),
        P("dp", None),
        P(None, ("dp", "seq")),
        P("dp", None),
        P("dp"),
        P("dp", None),
        P("dp", None),
        P("dp", None),
        P("dp", "seq", None),
    )
    out_specs = (
        P("dp", "seq", None),
        P("dp", "seq", None),
        P("dp"),
        P("dp", None),
        P("dp", None),
        P(None, ("dp", "seq")),
        P("dp", None),
        P("dp"),
        P("dp", None),
        P("dp", None),
        P("dp", None),
    )
    return jax.shard_map(per_device, mesh=mesh, in_specs=in_specs, out_specs=out_specs, check_vma=False)
```

```python
import functools
import jax
import jax.numpy as jnp
from jax import lax
from jax.experimental import pallas as pl
from jax.experimental.pallas import tpu as pltpu
from jax.sharding import PartitionSpec as P

F32 = jnp.float32
BF = jnp.bfloat16
NORM_EPS = 1e-06
BLOCK = 256
HALF = 128


def dot_nn(a, b):
    return lax.dot_general(a, b, (((1,), (0,)), ((), ())), preferred_element_type=F32)


def dot_nt(a, b):
    return lax.dot_general(a, b, (((1,), (1,)), ((), ())), preferred_element_type=F32)


def dot_tn(a, b):
    return lax.dot_general(a, b, (((0,), (0,)), ((), ())), preferred_element_type=F32)


def mul(a, b):
    return dot_nn(a.astype(BF), b.astype(BF))


def indices(rows, cols):
    return (
        lax.broadcasted_iota(jnp.int32, (rows, cols), 0),
        lax.broadcasted_iota(jnp.int32, (rows, cols), 1),
    )


def unit_inverse(systems, fill=()):
    size = systems[0].shape[0]
    row, col = indices(size, size)
    eye = jnp.where(row == col, 1.0, 0.0).astype(F32)
    near = (row - col == 1) & (row % 2 == 1)
    solved = [eye - jnp.where(near, g, 0.0) for g in systems]
    span = 2
    fill = list(fill)
    share = -(-len(fill) // 6)
    while span < size:
        for _ in range(share):
            if fill:
                fill.pop(0)()
        corner = (row // (2 * span) == col // (2 * span)) & (row % (2 * span) >= span) & (col % (2 * span) < span)
        below = [jnp.where(corner, g, 0.0) for g in systems]
        step = [mul(n, c) for n, c in zip(solved, below)]
        solved = [n - mul(s, n) for n, s in zip(solved, step)]
        span *= 2
    for more in fill:
        more()
    return solved


def block_inverse(g, fill=()):
    h = HALF
    parts = unit_inverse([p for b in g for p in (b[:h, :h], b[h:, h:])], fill)
    out = []
    for i, b in enumerate(g):
        top, bottom = parts[2 * i], parts[2 * i + 1]
        corner = -mul(mul(bottom, b[h:, :h]), top)
        upper = jnp.concatenate([top, jnp.zeros((h, h), F32)], 1)
        lower = jnp.concatenate([corner, bottom], 1)
        out.append(jnp.concatenate([upper, lower], 0))
    return out


def house(u, taps_ref, aux, taps_n):
    mixed = taps_ref[0:1, :] * u
    for s in range(1, taps_n):
        mixed = mixed + (taps_ref[s : s + 1, :] * aux[:, s : s + 1]) * pltpu.roll(u, s, 0)
    inv = lax.rsqrt(jnp.sum(mixed * mixed, -1, keepdims=True) + NORM_EPS)
    return mixed * inv, inv


def lane_pick(aux, lane):
    pos = lax.broadcasted_iota(jnp.int32, aux.shape, 1)
    return jnp.sum(jnp.where(pos == lane, aux, 0.0), 1, keepdims=True)


def fwd_kernel(taps_n, at_ref, join_ref, aux_ref, logit_ref, doc_ref, taps_ref, *rest):
    length = join_ref.shape[1]
    out_ref, rest = rest[0], rest[1:]
    part = out_ref.shape[1]
    (p_refs, x_ref, n_ref, m_ref, z_ref, qt_ref, w_ref, kt_ref, e_ref, run) = (rest[:-9],) + rest[-9:]
    d = taps_ref.shape[1]
    nb = length // BLOCK
    lane = at_ref[0] * pl.num_programs(1) + pl.program_id(1)
    aux = aux_ref[0]
    beta_all = 2.0 * jax.nn.sigmoid(lane_pick(logit_ref[0].astype(F32), lane))
    u = join_ref[0, :, 3 * d : 4 * d].astype(F32)
    w_all, _ = house(u, taps_ref, aux, taps_n)
    w_ref[0] = w_all.astype(BF)
    row, col = indices(BLOCK, BLOCK)
    later = row > col
    notbefore = row >= col
    scale = d ** -0.5
    sl = [slice(b * BLOCK, (b + 1) * BLOCK) for b in range(nb)]
    w = [w_ref[0, s, :] for s in sl]
    beta = [beta_all[s] for s in sl]
    k = [join_ref[0, s, d : 2 * d] for s in sl]
    q = [join_ref[0, s, 0:d] for s in sl]
    g = [jnp.where(later, beta[b] * dot_nt(w[b], w[b]), 0.0) for b in range(nb)]
    side_products = [[None] * nb for _ in range(3)]

    def make(i, b):
        def run_one():
            if i == 0:
                side_products[0][b] = jnp.where(later, beta[b] * dot_nt(w[b], k[b]), 0.0).astype(BF)
            elif i == 1:
                m_ref[0, b] = jnp.where(notbefore, dot_nt(q[b], w[b]), 0.0).astype(BF)
            else:
                side_products[2][b] = dot_nt(q[b], k[b])

        return run_one

    inv = block_inverse(g, [make(i, b) for i in range(3) for b in range(nb)])
    for b in range(nb):
        nn = inv[b].astype(BF)
        n_ref[0, b] = nn
        r = side_products[0][b]
        z = dot_nn(nn, (beta[b] * w_all[sl[b]]).astype(BF)).astype(BF)
        z_ref[0, sl[b], :] = z
        x = dot_nn(nn, r).astype(BF)
        x_ref[0, b] = x
        m = m_ref[0, b]
        diag = side_products[2][b] - dot_nn(m, x)
        kb = k[b].astype(F32) - dot_tn(x, w[b])
        allowed = notbefore & (aux[sl[b], 0:1] == doc_ref[0, 0:1, sl[b]])
        diag = jnp.where(allowed, diag * scale, -1e30)
        if b > 0:
            start = b * BLOCK
            qt = (q[b].astype(F32) - dot_nn(m, z)).astype(BF)
            qt_ref[0, sl[b], :] = qt
            off = start * (b - 1) // 2
            kt = run[0:start, :].astype(BF)
            kt_ref[0, off : off + start, :] = kt
            side = dot_nt(qt, kt)
            ok = aux[sl[b], 0:1] == doc_ref[0, 0:1, 0:start]
            side = jnp.where(ok, side * scale, -1e30)
            peak = jnp.maximum(jnp.max(diag, 1, keepdims=True), jnp.max(side, 1, keepdims=True))
            ps = jnp.exp(side - peak)
            pd = jnp.exp(diag - peak)
            inv_total = 1.0 / (jnp.sum(ps, 1, keepdims=True) + jnp.sum(pd, 1, keepdims=True))
            ps = (ps * inv_total).astype(BF)
            pd = (pd * inv_total).astype(BF)
            p_refs[b][0, :, 0:start] = ps
            p_refs[b][0, :, start : start + BLOCK] = pd
            o = dot_nn(ps, join_ref[0, 0:start, 2 * d : 3 * d]) + dot_nn(pd, join_ref[0, sl[b], 2 * d : 3 * d])
        else:
            qt_ref[0, sl[b], :] = jnp.zeros((BLOCK, d), BF)
            peak = jnp.max(diag, 1, keepdims=True)
            pd = jnp.exp(diag - peak)
            pd = (pd / jnp.sum(pd, 1, keepdims=True)).astype(BF)
            p_refs[b][0] = pd
            o = dot_nn(pd, join_ref[0, sl[b], 2 * d : 3 * d])
        if part % BLOCK == 0:
            out_ref[(b * BLOCK // part) ^ at_ref[0], b * BLOCK % part : b * BLOCK % part + BLOCK, :] = o.astype(BF)
        else:
            for c in range(BLOCK // part):
                out_ref[(b * BLOCK // part + c) ^ at_ref[0]] = o[c * part : (c + 1) * part].astype(BF)
        if b < nb - 1:
            e = dot_tn(w[b], z).astype(BF)
            e_ref[0, b] = e
            if b > 0:
                run[0:start, :] = run[0:start, :] - dot_nt(kt, e)
            run[sl[b], :] = kb
        else:
            e_ref[0, b] = jnp.zeros((d, d), BF)


def bwd_kernel(taps_n, seq_n, has_prior, at_ref, join_ref, aux_ref, logit_ref, taps_ref, *rest):
    nb = join_ref.shape[1] // BLOCK
    go_parts, rest = rest[:seq_n], rest[seq_n:]
    if has_prior:
        rest = rest[: nb + 8] + rest[nb + 9 :]
    p_refs = rest[:nb]
    (x_ref, n_ref, m_ref, z_ref, qt_ref, w_ref, kt_ref, e_ref, gj_ref, gt_ref, gk, gv, gw, go_ref) = rest[nb:]
    part = go_parts[0].shape[1]
    for m in range(seq_n):
        go_ref[pl.ds(pl.multiple_of((at_ref[0] ^ m) * part, part), part), :] = go_parts[m][0]
    length = join_ref.shape[1]
    d = taps_ref.shape[1]
    head = pl.program_id(1)
    lane = at_ref[0] * pl.num_programs(1) + head
    aux = aux_ref[0]
    beta_all = 2.0 * jax.nn.sigmoid(lane_pick(logit_ref[0].astype(F32), lane))
    row, col = indices(BLOCK, BLOCK)
    later = row > col
    notbefore = row >= col
    scale = d ** -0.5
    gbeta = [None] * nb

    def span(i):
        return pl.ds(pl.multiple_of((4 * head + i) * d, d), d)

    for b in reversed(range(nb)):
        start, end = b * BLOCK, (b + 1) * BLOCK
        s = slice(start, end)
        last = b == nb - 1
        w, q, k = w_ref[0, s, :], join_ref[0, s, 0:d], join_ref[0, s, d : 2 * d]
        beta = beta_all[s]
        x, n, m, z = x_ref[0, b], n_ref[0, b], m_ref[0, b], z_ref[0, s, :]
        go = go_ref[s, :]
        p = p_refs[b][0]
        gp = dot_nt(go, join_ref[0, 0:end, 2 * d : 3 * d])
        pf = p.astype(F32)
        inner = jnp.sum(pf * gp, 1, keepdims=True)
        gs = (pf * (gp - inner) * scale).astype(BF)
        gv_new = dot_tn(p, go)
        gsd = gs[:, start:end]
        if last:
            gv[...] = gv_new
        else:
            gv[0:end, :] += gv_new
        stack_m = [gsd]
        if b > 0:
            off = start * (b - 1) // 2
            kt, qt = kt_ref[0, off : off + start, :], qt_ref[0, s, :]
            gside = gs[:, 0:start]
            gqt_f = dot_nn(gside, kt)
            gqt = gqt_f.astype(BF)
            fresh = dot_tn(gside, qt)
        if not last:
            gkt_f = gk[s, :]
            gkt = gkt_f.astype(BF)
        if b > 0 and not last:
            e = e_ref[0, b]
            old = gk[0:start, :]
            old_b = old.astype(BF)
            ge = (-dot_tn(old_b, kt)).astype(BF)
            gk[0:start, :] = old - dot_nn(old_b, e) + fresh
        elif b > 0:
            gk[0:start, :] = fresh
        gm = dot_nt(gsd, x)
        mt_s = dot_tn(m, gsd)
        gx = -mt_s
        if not last:
            gx = gx - dot_nt(w, gkt)
        gx = jnp.where(later, gx, 0.0).astype(BF)
        y_x = dot_tn(n, gx)
        has_z = b > 0
        if has_z:
            gm = gm + dot_nt(gqt, z)
            gz = -dot_tn(m, gqt)
            if not last:
                gz = gz + dot_nn(w, ge)
            y_z = dot_tn(n, gz.astype(BF))
        gm = jnp.where(notbefore, -gm, 0.0).astype(BF)
        gg = dot_nt(y_x.astype(BF), x)
        if has_z:
            gg = gg + dot_nt(y_z.astype(BF), z)
        gg = jnp.where(later, -gg, 0.0)
        y_x = jnp.where(later, y_x, 0.0)
        gbv = jnp.sum(y_x * dot_nt(w, k) + gg * dot_nt(w, w), 1, keepdims=True)
        by = (beta * y_x).astype(BF)
        bg = (beta * gg).astype(BF)
        gw_b = dot_tn(gm, q) + dot_tn(bg, w) + dot_nn(bg, w) + dot_nn(by, k)
        gq_b = dot_nn(gsd, k) + dot_nn(gm, w)
        gk_b = dot_tn(gsd, q) + dot_tn(by, w)
        if has_z:
            gq_b = gq_b + gqt_f
            gw_b = gw_b + beta * y_z
            gbv = gbv + jnp.sum(y_z * w.astype(F32), 1, keepdims=True)
        if not last:
            gk_b = gk_b + gkt_f
            gw_b = gw_b - dot_nn(x, gkt)
            if has_z:
                gw_b = gw_b + dot_nt(z, ge)
        gbeta[b] = gbv
        gw[s, :] = gw_b
        gj_ref[0, s, span(0)] = gq_b.astype(BF)
        gj_ref[0, s, span(1)] = gk_b.astype(BF)
    gj_ref[0, :, span(2)] = gv[...].astype(BF)
    u = join_ref[0, :, 3 * d : 4 * d].astype(F32)
    w_all, inv = house(u, taps_ref, aux, taps_n)
    gw_all = gw[...]
    gc = inv * (gw_all - w_all * jnp.sum(gw_all * w_all, 1, keepdims=True))
    gu = taps_ref[0:1, :] * gc
    gt = [jnp.sum(gc * u, 0, keepdims=True)]
    for s in range(1, taps_n):
        held = gc * aux[:, s : s + 1]
        gt.append(jnp.sum(held * pltpu.roll(u, s, 0), 0, keepdims=True))
        gu = gu + taps_ref[s : s + 1, :] * pltpu.roll(held, length - s, 0)
    gj_ref[0, :, span(3)] = gu.astype(BF)
    gt.append(jnp.zeros((8 - taps_n, d), F32))
    gt_ref[0, 0] = jnp.concatenate(gt, 0)
    gb_all = jnp.concatenate(gbeta, 0) * beta_all * (1.0 - 0.5 * beta_all)
    pos = lax.broadcasted_iota(jnp.int32, aux.shape, 1)
    mine = jnp.where(pos == lane, gb_all, 0.0).astype(BF)
    tail = slice(gj_ref.shape[2] - 128, gj_ref.shape[2])

    @pl.when(head == 0)
    def _():
        gj_ref[0, :, tail] = mine

    @pl.when(head != 0)
    def _():
        gj_ref[0, :, tail] += mine


def res_specs(length, d, heads):
    nb = length // BLOCK
    shapes = [(BLOCK, (b + 1) * BLOCK) for b in range(nb)]
    shapes += [(nb, BLOCK, BLOCK)] * 3 + [(length, d)] * 3
    shapes += [(max(1, nb * (nb - 1) // 2) * BLOCK, d), (nb, d, d)]
    specs = [
        pl.BlockSpec((1,) + s, functools.partial(lambda n, r, h: (r * heads + h,) + (0,) * n, len(s))) for s in shapes
    ]
    return shapes, specs


def attend_fwd(joined, aux, logit, doc_rows, taps, at, heads, taps_n, seq_n):
    rows, length, packed = joined.shape
    d = taps.shape[1] // heads
    shapes, specs = res_specs(length, d, heads)
    return pl.pallas_call(
        functools.partial(fwd_kernel, taps_n),
        grid=(rows, heads),
        in_specs=[
            pl.BlockSpec(memory_space=pltpu.SMEM),
            pl.BlockSpec((1, length, 4 * d), lambda r, h: (r, 0, h)),
            pl.BlockSpec((1, length, 128), lambda r, h: (r, 0, 0)),
            pl.BlockSpec((1, length, 128), lambda r, h: (r, 0, 0)),
            pl.BlockSpec((1, 8, length), lambda r, h: (r, 0, 0)),
            pl.BlockSpec((8, d), lambda r, h: (0, h)),
        ],
        out_specs=[pl.BlockSpec((seq_n, length // seq_n, d), lambda r, h: (0, 0, h))] + specs,
        out_shape=[jax.ShapeDtypeStruct((seq_n, length // seq_n, heads * d), BF)]
        + [jax.ShapeDtypeStruct((rows * heads,) + s, BF) for s in shapes],
        scratch_shapes=[pltpu.VMEM((length, d), F32)],
        compiler_params=pltpu.CompilerParams(vmem_limit_bytes=56 * 2**20),
        cost_estimate=pl.CostEstimate(
            flops=rows * heads * 8 * 10**9, bytes_accessed=rows * heads * 5 * 10**6, transcendentals=0
        ),
    )(at[None], joined, aux, logit, doc_rows, taps)


def attend_bwd(joined, aux, logit, taps, grad_parts, res, at, heads, taps_n, row, rows_n, prior):
    rows, length, packed = joined.shape
    d = taps.shape[1] // heads
    shapes, specs = res_specs(length, d, heads)
    wide = heads * 4 * d + 128
    seq_n = len(grad_parts)
    args = [at[None], joined, aux, logit, taps, *[p for p, _ in grad_parts], *res]
    aliases = {}
    if prior is not None:
        aliases = {len(args): 0}
        args.append(prior)
    return pl.pallas_call(
        functools.partial(bwd_kernel, taps_n, seq_n, prior is not None),
        grid=(rows, heads),
        in_specs=[
            pl.BlockSpec(memory_space=pltpu.SMEM),
            pl.BlockSpec((1, length, 4 * d), lambda r, h: (r, 0, h)),
            pl.BlockSpec((1, length, 128), lambda r, h: (r, 0, 0)),
            pl.BlockSpec((1, length, 128), lambda r, h: (r, 0, 0)),
            pl.BlockSpec((8, d), lambda r, h: (0, h)),
        ]
        + [
            pl.BlockSpec((1, length // seq_n, d), functools.partial(lambda i, r, h: (i, 0, h), i)) for _, i in grad_parts
        ]
        + specs
        + [pl.BlockSpec(memory_space=pl.ANY)] * (0 if prior is None else 1),
        out_specs=[
            pl.BlockSpec((1, length, wide), lambda r, h: (row, 0, 0)),
            pl.BlockSpec((1, 1, 8, d), lambda r, h: (r, h, 0, 0)),
        ],
        out_shape=[
            jax.ShapeDtypeStruct((rows_n, length, wide), BF),
            jax.ShapeDtypeStruct((rows, heads, 8, d), F32),
        ],
        scratch_shapes=[pltpu.VMEM((length, d), F32)] * 3 + [pltpu.VMEM((length, d), BF)],
        input_output_aliases=aliases,
        compiler_params=pltpu.CompilerParams(vmem_limit_bytes=56 * 2**20),
        cost_estimate=pl.CostEstimate(
            flops=rows * heads * 16 * 10**9, bytes_accessed=rows * heads * 6 * 10**6, transcendentals=0
        ),
    )(*args)


def rects_of(sizes, rows):
    rects, at = [], 0
    for i, (r, c) in enumerate(sizes):
        if r == rows:
            rects.append((i, 0, r, 0, c, 0, at))
            at += c
        else:
            wide, rest = r * c // rows, rows - r
            rects.append((i, 0, r, 0, wide, 0, at))
            rects.append((i, 0, rest, wide, wide // 2, r, at))
            rects.append((i, rest, rest, wide, wide // 2, r, at + wide // 2))
            at += wide
    return rects, at


def clip(rects, low, high):
    out = []
    for i, r0, rows, c0, cols, p0, pc in rects:
        a, b = max(p0, low), min(p0 + rows, high)
        if a < b:
            out.append((i, r0 + a - p0, b - a, c0, cols, a - low, pc))
    return out


def ring_order(n):
    return list(range(0, n, 2)) + list(range(n - 1, 0, -2))


def ring_index(steps):
    n = lax.axis_size("dp")
    me = lax.axis_index("dp")
    place = jnp.where(me % 2 == 0, me // 2, n - 1 - me // 2)
    there = (place + jnp.array([(k + n) % n for k in steps], jnp.int32)) % n
    return jnp.where(there < n // 2, 2 * there, 2 * (n - 1 - there) + 1)


def to_right(value):
    order = ring_order(lax.axis_size("dp"))
    return lax.ppermute(value, "dp", [(a, b) for a, b in zip(order, order[1:] + order[:1])])


def to_left(value):
    order = ring_order(lax.axis_size("dp"))
    return lax.ppermute(value, "dp", [(b, a) for a, b in zip(order, order[1:] + order[:1])])


def middle_row(rows):
    return (rows // 2 + 15) // 16 * 16


def ring_gather(own, sent=None):
    n = lax.axis_size("dp")
    cut = middle_row(own.shape[0])
    pieces, steps = [own], [0]
    pair = (own, own)
    for k in range(1, n // 2 + 1):
        if k == n // 2:
            pair = (pair[0][:cut], pair[1][cut:])
        if sent is not None:
            sent[:] = pair
        pair = yield (to_right(pair[0]), to_left(pair[1]))
        pieces += list(pair)
        steps += [-k, k] if k < n // 2 else [k]
    return pieces, ring_index(steps)


def drain(gen, value=None):
    try:
        value = next(gen) if value is None else gen.send(value)
        while True:
            value = gen.send(value)
    except StopIteration as stop:
        return stop.value


def place_kernel(rects, count, cut, index_ref, *refs):
    pieces, outs = refs[:count], refs[count:]
    for w in range(count - 1):
        @pl.when(pl.program_id(0) == w)
        def _():
            for i, r0, rows, c0, cols, p0, pc in rects:
                if w < count - 2:
                    outs[i][r0 : r0 + rows, c0 : c0 + cols] = pieces[w][p0 : p0 + rows, pc : pc + cols]
                    continue
                for piece, low, high in ((pieces[w], 0, cut), (pieces[w + 1], cut, 1 << 20)):
                    for i2, q0, r, d0, c, s0, sc in clip([(i, r0, rows, c0, cols, p0, pc)], low, high):
                        outs[i][q0 : q0 + r, d0 : d0 + c] = piece[s0 : s0 + r, sc : sc + c]


def place(gathered, sizes):
    pieces, index = gathered
    n = lax.axis_size("dp")
    rows = pieces[0].shape[0]
    rects, width = rects_of(sizes, rows)
    return pl.pallas_call(
        functools.partial(place_kernel, rects, len(pieces), middle_row(rows)),
        grid_spec=pltpu.PrefetchScalarGridSpec(
            num_scalar_prefetch=1,
            grid=(n,),
            in_specs=[pl.BlockSpec(p.shape, lambda i, ref: (0, 0)) for p in pieces],
            out_specs=[pl.BlockSpec(size, lambda i, ref: (ref[i], 0)) for size in sizes],
        ),
        out_shape=[jax.ShapeDtypeStruct((n * r, c), BF) for r, c in sizes],
        compiler_params=pltpu.CompilerParams(vmem_limit_bytes=48 * 2**20),
        cost_estimate=pl.CostEstimate(flops=0, bytes_accessed=4 * n * rows * width, transcendentals=0),
    )(index, *pieces)


def join_kernel(rects, lanes, count, has_extra, index_ref, *refs):
    outs, refs = refs[-len(lanes) :], refs[: -len(lanes)]
    srcs, got = refs[: count * len(lanes)], refs[count * len(lanes) :]
    if has_extra:
        extra, got = got[: len(lanes)], got[len(lanes) :]
    for j, (low, high, adds) in enumerate(lanes):
        for i, r0, rows, c0, cols, p0, pc in clip(rects, low, high):
            value = srcs[j * count + i][r0 : r0 + rows, c0 : c0 + cols]
            if not adds:
                outs[j][p0 : p0 + rows, pc : pc + cols] = value
                continue
            total = value.astype(F32)
            spans = []
            for g, first in adds:
                top, end = first, first + got[g].shape[0]
                spans.append((g, top, end))
            if all(top <= p0 and p0 + rows <= end for _, top, end in spans):
                for g, top, _ in spans:
                    total = total + got[g][p0 - top : p0 - top + rows, pc : pc + cols].astype(F32)
                outs[j][p0 : p0 + rows, pc : pc + cols] = total.astype(BF)
            else:
                outs[j][p0 : p0 + rows, pc : pc + cols] = value
                for g, top, end in spans:
                    a, b = max(top, p0), min(end, p0 + rows)
                    if a < b:
                        sub = total[a - p0 : b - p0] + got[g][a - top : b - top, pc : pc + cols].astype(F32)
                        outs[j][a:b, pc : pc + cols] = sub.astype(BF)
        if has_extra:
            tail = slice(outs[j].shape[1] - extra[j].shape[1], outs[j].shape[1])
            outs[j][:, tail] = (outs[j][:, tail].astype(F32) + extra[j][low:high].astype(F32)).astype(BF)


def join(sources, index, received, lanes, extra=None):
    n = lax.axis_size("dp")
    sizes = [(s.shape[0] // n, s.shape[1]) for s in sources]
    rows = max(r for r, _ in sizes)
    rects, width = rects_of(sizes, rows)
    specs, args = [], []
    for j in range(len(lanes)):
        for s, size in zip(sources, sizes):
            specs.append(pl.BlockSpec(size, functools.partial(lambda j, i, ref: (ref[j], 0), j)))
            args.append(s)
    if extra is not None:
        for j in range(len(lanes)):
            specs.append(pl.BlockSpec((rows, extra.shape[1]), functools.partial(lambda j, i, ref: (ref[j], 0), j)))
            args.append(extra)
    for v in received:
        specs.append(pl.BlockSpec(v.shape, lambda i, ref: (0, 0)))
    heights = [high - low for low, high, _ in lanes]
    return pl.pallas_call(
        functools.partial(join_kernel, rects, lanes, len(sources), extra is not None),
        grid_spec=pltpu.PrefetchScalarGridSpec(
            num_scalar_prefetch=1,
            grid=(1,),
            in_specs=specs,
            out_specs=[pl.BlockSpec((h, width), lambda i, ref: (0, 0)) for h in heights],
        ),
        out_shape=[jax.ShapeDtypeStruct((h, width), BF) for h in heights],
        compiler_params=pltpu.CompilerParams(vmem_limit_bytes=48 * 2**20),
        cost_estimate=pl.CostEstimate(
            flops=0, bytes_accessed=6 * sum(heights) * width, transcendentals=0
        ),
    )(index, *args, *received)


def ring_scatter(sources, extra=None, sent=None):
    n = lax.axis_size("dp")
    half = n // 2
    rows = max(s.shape[0] // n for s in sources)
    cut = middle_row(rows)
    out = join(sources, ring_index([half, half]), [], [(0, cut, []), (cut, rows, [])], extra)
    for k in range(half - 1, -1, -1):
        if sent is not None:
            sent[:] = out
        got = yield (to_right(out[0]), to_left(out[1]))
        first = cut if k == half - 1 else 0
        if k > 0:
            out = join(sources, ring_index([k, -k]), got, [(0, rows, [(0, 0)]), (0, rows, [(1, first)])], extra)
    return join(sources, ring_index([0]), got, [(0, rows, [(0, 0), (1, first)])], extra)[0]


def pack_units_kernel(seq_n, at_ref, gate_ref, up_ref, down_ref, out_ref):
    i = pl.program_id(0)
    n = pl.num_programs(0)
    unit = gate_ref.shape[1]
    rows, wide = out_ref.shape
    mine = wide // 3
    out_ref[:, pl.ds(pl.multiple_of(i * unit, unit), unit)] = gate_ref[...].astype(BF)
    out_ref[:, pl.ds(pl.multiple_of(mine + i * unit, unit), unit)] = up_ref[...].astype(BF)

    @pl.when(i == 0)
    def _():
        rects, _ = rects_of([(rows, mine), (rows, mine), down_ref.shape], rows)
        for _, r0, r, c0, c, p0, pc in rects[2:]:
            out_ref[p0 : p0 + r, pc : pc + c] = down_ref[r0 : r0 + r, c0 : c0 + c].astype(BF)


def pack_units(w_gate, w_up, w_down, at):
    dp_n, seq_n = lax.axis_size("dp"), lax.axis_size("seq")
    shard, ff = w_gate.shape
    unit = ff // (dp_n * seq_n)
    mine = dp_n * unit
    if unit % 128:
        def units(w):
            w = w.reshape(shard, dp_n, seq_n, unit)
            return lax.dynamic_index_in_dim(w, at, 2, keepdims=False).astype(BF).reshape(shard, mine)

        down = lax.dynamic_slice_in_dim(w_down, at * unit, unit, 0).astype(BF)
        rects, _ = rects_of([(shard, mine), (shard, mine), down.shape], shard)
        tops = [down[r0 : r0 + r, c0 : c0 + c] for _, r0, r, c0, c, _, _ in rects[2:]]
        folded = jnp.concatenate([tops[0], jnp.concatenate(tops[1:], 1)], 0)
        return jnp.concatenate([units(w_gate), units(w_up), folded], 1)
    return pl.pallas_call(
        functools.partial(pack_units_kernel, seq_n),
        grid_spec=pltpu.PrefetchScalarGridSpec(
            num_scalar_prefetch=1,
            grid=(dp_n,),
            in_specs=[
                pl.BlockSpec((shard, unit), lambda i, ref: (0, i * seq_n + ref[0])),
                pl.BlockSpec((shard, unit), lambda i, ref: (0, i * seq_n + ref[0])),
                pl.BlockSpec((unit, w_down.shape[1]), lambda i, ref: (ref[0], 0)),
            ],
            out_specs=pl.BlockSpec((shard, 3 * mine), lambda i, ref: (0, 0)),
        ),
        out_shape=jax.ShapeDtypeStruct((shard, 3 * mine), BF),
        compiler_params=pltpu.CompilerParams(vmem_limit_bytes=48 * 2**20),
        cost_estimate=pl.CostEstimate(flops=0, bytes_accessed=6 * 3 * shard * mine, transcendentals=0),
    )(at[None], w_gate, w_up, w_down)


def spread_kernel(seq_n, at_ref, *refs):
    gates, ups = refs[:seq_n], refs[seq_n : 2 * seq_n]
    wg_ref, wu_ref, og_ref, ou_ref, gain_ref = refs[2 * seq_n :]
    unit = gates[0].shape[1]
    total = jnp.zeros((wg_ref.shape[0], unit), F32)
    for m in range(seq_n):
        span = pl.ds(pl.multiple_of((at_ref[0] ^ m) * unit, unit), unit)
        for piece, w, out in ((gates[m], wg_ref, og_ref), (ups[m], wu_ref, ou_ref)):
            value = piece[...].astype(F32)
            out[:, span] = value
            total = total + value * w[:, span].astype(BF).astype(F32)

    @pl.when(pl.program_id(0) == 0)
    def _():
        gain_ref[...] = total

    @pl.when(pl.program_id(0) != 0)
    def _():
        gain_ref[...] += total


def unfold_kernel(seq_n, at_ref, *refs):
    pieces, out = refs[:seq_n], refs[seq_n]
    rows, wide = pieces[0].shape
    rects, _ = rects_of([out.shape], rows)
    for m in range(seq_n):
        @pl.when(pl.program_id(0) == m)
        def _():
            for _, r0, r, c0, c, p0, pc in rects:
                out[r0 : r0 + r, c0 : c0 + c] = pieces[m][p0 : p0 + r, pc : pc + c].astype(F32)


def spread_units(rel, w_gate, w_up, at):
    dp_n, seq_n = lax.axis_size("dp"), lax.axis_size("seq")
    shard, ff = w_gate.shape
    unit = ff // (dp_n * seq_n)
    mine = dp_n * unit
    if unit % 128:
        pieces = in_order(rel, at)

        def spread(start):
            blocks = [g[:, start : start + mine].reshape(shard, dp_n, 1, unit) for g in pieces]
            return jnp.concatenate(blocks, 2).reshape(shard, ff).astype(F32)

        gate, up = spread(0), spread(mine)
        return gate, up, jnp.sum(gate * w_gate.astype(BF).astype(F32) + up * w_up.astype(BF).astype(F32), 1)
    gate, up, sums = pl.pallas_call(
        functools.partial(spread_kernel, seq_n),
        grid_spec=pltpu.PrefetchScalarGridSpec(
            num_scalar_prefetch=1,
            grid=(dp_n,),
            in_specs=[pl.BlockSpec((shard, unit), lambda i, ref: (0, i))] * seq_n
            + [pl.BlockSpec((shard, unit), lambda i, ref: (0, dp_n + i))] * seq_n
            + [pl.BlockSpec((shard, seq_n * unit), lambda i, ref: (0, i))] * 2,
            out_specs=[pl.BlockSpec((shard, seq_n * unit), lambda i, ref: (0, i))] * 2
            + [pl.BlockSpec((shard, unit), lambda i, ref: (0, 0))],
        ),
        out_shape=[jax.ShapeDtypeStruct((shard, ff), F32)] * 2 + [jax.ShapeDtypeStruct((shard, unit), F32)],
        compiler_params=pltpu.CompilerParams(vmem_limit_bytes=60 * 2**20),
        cost_estimate=pl.CostEstimate(flops=0, bytes_accessed=20 * shard * ff, transcendentals=0),
    )(at[None], *rel, *rel, w_gate, w_up)
    return gate, up, jnp.sum(sums, 1)


def unfold_units(rel, w_down, at):
    seq_n = len(rel)
    unit, model = w_down.shape[0] // seq_n, w_down.shape[1]
    shard, mine = rel[0].shape[0], rel[0].shape[1] // 3
    if unit % 128:
        rects, _ = rects_of([(unit, model)], shard)
        downs = []
        for p in in_order(rel, at):
            a, b, c = [p[p0 : p0 + r, 2 * mine + pc : 2 * mine + pc + w] for _, _, r, _, w, p0, pc in rects]
            downs.append(jnp.concatenate([a, jnp.concatenate([b, c], 0)], 1))
        return jnp.concatenate(downs, 0).astype(F32)
    return pl.pallas_call(
        functools.partial(unfold_kernel, seq_n),
        grid_spec=pltpu.PrefetchScalarGridSpec(
            num_scalar_prefetch=1,
            grid=(seq_n,),
            in_specs=[pl.BlockSpec((shard, mine), lambda i, ref: (0, 2))] * seq_n,
            out_specs=pl.BlockSpec((unit, model), lambda i, ref: (i ^ ref[0], 0)),
        ),
        out_shape=jax.ShapeDtypeStruct(w_down.shape, F32),
        compiler_params=pltpu.CompilerParams(vmem_limit_bytes=60 * 2**20),
        cost_estimate=pl.CostEstimate(flops=0, bytes_accessed=6 * w_down.size, transcendentals=0),
    )(at[None], *rel)


def lane_sums(value):
    total = value[:, 0:128]
    for c in range(128, value.shape[1], 128):
        total = total + value[:, c : c + 128]
    return total


def first_columns_kernel(seq_n, at_ref, *refs):
    pieces, (w_ref, out_ref, sum_ref) = refs[:seq_n], refs[seq_n:]
    cols = w_ref.shape[1]
    for m in range(seq_n):
        for h in range(2):
            @pl.when((pl.program_id(0) == m) & (pl.program_id(1) == h))
            def _():
                value = pieces[m][:, h * cols : (h + 1) * cols].astype(F32)
                out_ref[...] = value
                total = lane_sums(value * w_ref[...].astype(BF).astype(F32))
                if m + h == 0:
                    sum_ref[...] = total
                else:
                    sum_ref[...] += total


def spread_first(rel, w_proj, at):
    seq_n = lax.axis_size("seq")
    rows, cols = w_proj.shape[0], w_proj.shape[1] // seq_n // 3

    def block(i, h, ref):
        return (0, (i ^ ref[0]) * 3 + h)

    grad, sums = pl.pallas_call(
        functools.partial(first_columns_kernel, seq_n),
        grid_spec=pltpu.PrefetchScalarGridSpec(
            num_scalar_prefetch=1,
            grid=(seq_n, 2),
            in_specs=[pl.BlockSpec(rel[0].shape, lambda i, h, ref: (0, 0))] * seq_n + [pl.BlockSpec((rows, cols), block)],
            out_specs=[pl.BlockSpec((rows, cols), block), pl.BlockSpec((rows, 128), lambda i, h, ref: (0, 0))],
        ),
        out_shape=[jax.ShapeDtypeStruct(w_proj.shape, F32), jax.ShapeDtypeStruct((rows, 128), F32)],
        compiler_params=pltpu.CompilerParams(vmem_limit_bytes=60 * 2**20),
        cost_estimate=pl.CostEstimate(flops=0, bytes_accessed=7 * w_proj.size, transcendentals=0),
    )(at[None], *rel, w_proj)
    return grad, jnp.sum(sums, 1)


def last_columns_kernel(seq_n, first, at_ref, *refs):
    pieces, (w_ref, _, out_ref, first_ref, sum_ref) = refs[:seq_n], refs[seq_n:]
    cols = w_ref.shape[1]
    for m in range(seq_n):
        @pl.when(pl.program_id(0) == m)
        def _():
            first_ref[...] = pieces[m][:, :first].astype(F32)
            value = pieces[m][:, first : first + cols].astype(F32)
            out_ref[...] = value
            total = lane_sums(value * w_ref[...].astype(BF).astype(F32))
            if m == 0:
                sum_ref[...] = total
            else:
                sum_ref[...] += total


def spread_last(rel, w_proj, first, prior, at):
    seq_n = lax.axis_size("seq")
    rows, cols = w_proj.shape[0], w_proj.shape[1] // seq_n // 3

    def block(i, ref):
        return (0, (i ^ ref[0]) * 3 + 2)

    grad, grad_first, sums = pl.pallas_call(
        functools.partial(last_columns_kernel, seq_n, first),
        grid_spec=pltpu.PrefetchScalarGridSpec(
            num_scalar_prefetch=1,
            grid=(seq_n,),
            in_specs=[pl.BlockSpec(rel[0].shape, lambda i, ref: (0, 0))] * seq_n
            + [pl.BlockSpec((rows, cols), block), pl.BlockSpec(memory_space=pl.ANY)],
            out_specs=[
                pl.BlockSpec((rows, cols), block),
                pl.BlockSpec((rows, first), lambda i, ref: (0, i ^ ref[0])),
                pl.BlockSpec((rows, 128), lambda i, ref: (0, 0)),
            ],
        ),
        out_shape=[
            jax.ShapeDtypeStruct(w_proj.shape, F32),
            jax.ShapeDtypeStruct((rows, seq_n * first), F32),
            jax.ShapeDtypeStruct((rows, 128), F32),
        ],
        input_output_aliases={seq_n + 2: 0},
        compiler_params=pltpu.CompilerParams(vmem_limit_bytes=60 * 2**20),
        cost_estimate=pl.CostEstimate(flops=0, bytes_accessed=5 * w_proj.size, transcendentals=0),
    )(at[None], *rel, w_proj, prior)
    return grad, grad_first, jnp.sum(sums, 1)


def matmul_low(left, right):
    return jnp.dot(left, right, preferred_element_type=F32)


def matmul_tn(left, right):
    return dot_tn(left, right)


def matmul_nt(left, right):
    return dot_nt(left, right)


def inv_rms(values):
    return lax.rsqrt(jnp.mean(values * values, -1, keepdims=True) + NORM_EPS)


def norm_backward(values, scale_inv, gain, grad_norm):
    scaled = grad_norm * gain
    return scale_inv * scaled - values * scale_inv**3 * jnp.mean(scaled * values, -1, keepdims=True)


def after(value, earlier):
    return lax.optimization_barrier((value, earlier))[0]


def swap(value, m):
    n = lax.axis_size("seq")
    return lax.ppermute(value, "seq", [(i, i ^ m) for i in range(n)])


def gather_rel(own):
    far = swap(own, 2)
    return [own, swap(own, 1), far, swap(far, 1)]


def in_order(rel, seq_at):
    odd = seq_at % 2 == 1
    high = seq_at // 2 == 1
    pairs = []
    for a, b in (rel[0:2], rel[2:4]):
        pairs.append((jnp.where(odd, b, a), jnp.where(odd, a, b)))
    (a0, a1), (b0, b1) = pairs
    return [jnp.where(high, b0, a0), jnp.where(high, b1, a1), jnp.where(high, a0, b0), jnp.where(high, a1, b1)]


def piece_spec(shape, i, hold=False):
    more = {"pipeline_mode": pl.Buffered(1)} if hold else {}
    return pl.BlockSpec((1,) + shape[1:], lambda *_: (i,) + (0,) * (len(shape) - 1), **more)


def project_kernel(count, shards, cut, lane, has_prior, at_ref, index_ref, *refs):
    pieces, refs = refs[:count], refs[count:]
    tiles, sides = refs[:shards], refs[shards : 2 * shards]
    norm_ref, join_ref, logit_ref, gains_ref, w_ref, b_ref = refs[2 * shards + (1 if has_prior else 0) :]
    part = pieces[0].shape[1]
    rows = tiles[0].shape[0]
    starts = []
    for k in range(shards):
        which = min(k, shards - 2)
        first = index_ref[which] * rows + (cut if k == shards - 1 else 0)
        starts.append(pl.ds(pl.multiple_of(first, 16), tiles[k].shape[0]))
        w_ref[starts[k], :] = tiles[k][...]

    @pl.when(pl.program_id(0) == 0)
    def _():
        for k in range(shards):
            b_ref[starts[k], :] = sides[k][...]
        i, j = indices(8, 128)
        gains_ref[...] = dot_nt(jnp.where(j == lane + i, 1.0, 0.0).astype(BF), b_ref[...])
        for m in range(count):
            x = pieces[m][0].astype(F32)
            here = pl.ds(pl.multiple_of((at_ref[0] ^ m) * part, part), part)
            norm_ref[0, here, :] = (x * inv_rms(x) * gains_ref[0:1, :]).astype(BF)
        logit_ref[0] = dot_nn(norm_ref[0], b_ref[...]).astype(BF)

    join_ref[0] = dot_nn(norm_ref[0], w_ref[...]).astype(BF)


def project(x_rel, lane, gathered, wide, at, r, prior):
    shards, index = gathered
    count = len(x_rel)
    rows_n, part, model = x_rel[0][0].shape
    length = part * count
    tile = 256

    def whole(shape):
        return pl.BlockSpec(shape, lambda j, *_: (0,) * len(shape))

    args = [at[None], index, *[x for x, _ in x_rel], *shards, *shards]
    aliases = {}
    if prior is not None:
        aliases = {len(args): 0}
        args.append(prior)
    return pl.pallas_call(
        functools.partial(project_kernel, count, len(shards), middle_row(shards[0].shape[0]), lane, prior is not None),
        grid_spec=pltpu.PrefetchScalarGridSpec(
            num_scalar_prefetch=2,
            grid=(wide // tile,),
            in_specs=[piece_spec(x.shape, i, True) for x, i in x_rel]
            + [pl.BlockSpec((s.shape[0], tile), lambda j, *_: (0, j)) for s in shards]
            + [pl.BlockSpec((s.shape[0], 128), lambda j, *_: (0, wide // 128)) for s in shards]
            + [pl.BlockSpec(memory_space=pl.ANY)] * (0 if prior is None else 1),
            out_specs=[
                pl.BlockSpec((1, length, model), lambda j, *_: (r, 0, 0)),
                pl.BlockSpec((1, length, tile), lambda j, *_: (0, 0, j)),
                whole((1, length, 128)),
                whole((8, model)),
            ],
            scratch_shapes=[pltpu.VMEM((model, tile), BF), pltpu.VMEM((model, 128), BF)],
        ),
        out_shape=[
            jax.ShapeDtypeStruct((rows_n, length, model), BF),
            jax.ShapeDtypeStruct((1, length, wide), BF),
            jax.ShapeDtypeStruct((1, length, 128), BF),
            jax.ShapeDtypeStruct((8, model), F32),
        ],
        input_output_aliases=aliases,
        compiler_params=pltpu.CompilerParams(vmem_limit_bytes=56 * 2**20),
        cost_estimate=pl.CostEstimate(
            flops=2 * length * model * wide, bytes_accessed=6 * length * model, transcendentals=0
        ),
    )(*args)


def hidden_kernel(seq_n, has_prior, *refs):
    two, top = refs[:seq_n], refs[seq_n : 2 * seq_n]
    wg_ref, wu_ref, wd_ref = refs[2 * seq_n : 2 * seq_n + 3]
    hid_ref, gg_ref, gu_ref, two_ref, top_ref = refs[2 * seq_n + (6 if has_prior else 3) :]
    part = two[0].shape[0]

    @pl.when(pl.program_id(0) == 0)
    def _():
        for m in range(seq_n):
            s = slice(m * part, (m + 1) * part)
            two_ref[s, :] = two[m][...]
            top_ref[s, :] = top[m][0]

    gate = dot_nn(two_ref[...], wg_ref[...])
    up = dot_nn(two_ref[...], wu_ref[...])
    gh = dot_nt(top_ref[...], wd_ref[...])
    sig = jax.nn.sigmoid(gate)
    act = gate * sig
    hid_ref[0] = (act * up).astype(BF)
    gg_ref[0] = (gh * up * sig * (1.0 + gate * (1.0 - sig))).astype(BF)
    gu_ref[0] = (gh * act).astype(BF)


def hidden_units(two, top, gate_full, up_full, down_full, r, prior):
    seq_n = len(two)
    part, model = two[0].shape
    rows_n = top[0][0].shape[0]
    mine = gate_full.shape[1]
    tile = 256
    length = part * seq_n
    piece = pl.BlockSpec((part, model), lambda j: (0, 0), pipeline_mode=pl.Buffered(1))
    columns = pl.BlockSpec((model, tile), lambda j: (0, j))
    hidden = pl.BlockSpec((1, length, tile), lambda j: (r, 0, j))
    args = [*two, *[g for g, _ in top], gate_full, up_full, down_full]
    aliases = {}
    if prior is not None:
        aliases = {len(args) + i: i for i in range(3)}
        args += prior
    return pl.pallas_call(
        functools.partial(hidden_kernel, seq_n, prior is not None),
        grid=(mine // tile,),
        in_specs=[piece] * seq_n
        + [piece_spec(g.shape, i, True) for g, i in top]
        + [columns, columns, pl.BlockSpec((tile, model), lambda j: (j, 0))]
        + [pl.BlockSpec(memory_space=pl.ANY)] * (3 if prior is not None else 0),
        out_specs=[hidden] * 3,
        out_shape=[jax.ShapeDtypeStruct((rows_n, length, mine), BF)] * 3,
        scratch_shapes=[pltpu.VMEM((length, model), BF)] * 2,
        input_output_aliases=aliases,
        compiler_params=pltpu.CompilerParams(vmem_limit_bytes=56 * 2**20),
        cost_estimate=pl.CostEstimate(
            flops=6 * length * model * mine, bytes_accessed=8 * length * model + 6 * model * mine, transcendentals=0
        ),
    )(*args)


def by_device(total, keep, send, part):
    for m in range(total.shape[0] // part):
        (keep, send)[m % 2][m // 2] = total[m * part : (m + 1) * part].astype(BF)


def model_kernel(seq_n, hid_ref, gg_ref, gu_ref, wg_ref, wu_ref, wd_ref, keep_b, send_b, keep_f, send_f):
    part = keep_b.shape[1]
    by_device(dot_nt(gg_ref[0], wg_ref[...]) + dot_nt(gu_ref[0], wu_ref[...]), keep_b, send_b, part)
    by_device(dot_nn(hid_ref[0], wd_ref[...]), keep_f, send_f, part)


def model_units(units, gate_full, up_full, down_full, r, seq_n):
    hid, gg, gu = units
    rows_n, length, mine = hid.shape
    model = gate_full.shape[0]
    part = length // seq_n
    tile = 256
    hold = pl.BlockSpec((1, length, mine), lambda j: (r, 0, 0), pipeline_mode=pl.Buffered(1))
    rows = pl.BlockSpec((tile, mine), lambda j: (j, 0))
    return pl.pallas_call(
        functools.partial(model_kernel, seq_n),
        grid=(model // tile,),
        in_specs=[hold] * 3 + [rows, rows, pl.BlockSpec((mine, tile), lambda j: (0, j))],
        out_specs=[pl.BlockSpec((seq_n // 2, part, tile), lambda j: (0, 0, j))] * 4,
        out_shape=[jax.ShapeDtypeStruct((seq_n // 2, part, model), BF)] * 4,
        compiler_params=pltpu.CompilerParams(vmem_limit_bytes=56 * 2**20),
        cost_estimate=pl.CostEstimate(
            flops=6 * length * model * mine, bytes_accessed=8 * length * model + 6 * model * mine, transcendentals=0
        ),
    )(hid, gg, gu, gate_full, up_full, down_full)


def outer_kernel(lefts, counts, lanes, *refs):
    left, refs = refs[:lefts], refs[lefts:]
    groups = []
    for n in counts:
        groups.append(refs[:n])
        refs = refs[n:]
    outs, scratch = refs[: len(counts)], list(refs[len(counts) :])

    def gather(pieces, into):
        row = 0
        for p in pieces:
            value = p[...] if len(p.shape) == 2 else p[0]
            into[row : row + value.shape[0], :] = value
            row += value.shape[0]

    if lefts > 1:
        tall = scratch.pop(0)
        gather(left, tall)
    else:
        tall = left[0]
    for n, group, out in zip(counts, groups, outs):
        if n > 1:
            whole = scratch.pop(0)

            @pl.when(pl.program_id(0) == 0)
            def _():
                gather(group, whole)
        else:
            whole = group[0]
        out[...] = dot_tn(tall[...], whole[:, slice(*lanes)]).astype(BF)


def outer(left, rights, lanes=(None, None)):
    total = sum(p.shape[0] for p in left)
    model = left[0].shape[1]
    tile = 256
    widths = [(g[0][0] if isinstance(g[0], tuple) else g[0]).shape[-1] for g in rights]
    spans = [len(range(w)[slice(*lanes)]) for w in widths]
    scratch = [pltpu.VMEM((total, tile), BF)] if len(left) > 1 else []
    scratch += [pltpu.VMEM((total, w), BF) for g, w in zip(rights, widths) if len(g) > 1]
    specs = [pl.BlockSpec((p.shape[0], tile), lambda j: (0, j)) for p in left]
    args = list(left)
    for g in rights:
        for p in g:
            if isinstance(p, tuple):
                specs.append(piece_spec(p[0].shape, p[1], True))
                args.append(p[0])
            else:
                specs.append(pl.BlockSpec(p.shape, lambda j: (0, 0), pipeline_mode=pl.Buffered(1)))
                args.append(p)
    return pl.pallas_call(
        functools.partial(outer_kernel, len(left), [len(g) for g in rights], lanes),
        grid=(model // tile,),
        in_specs=specs,
        out_specs=[pl.BlockSpec((tile, w), lambda j: (j, 0)) for w in spans],
        out_shape=[jax.ShapeDtypeStruct((model, w), BF) for w in spans],
        scratch_shapes=scratch,
        compiler_params=pltpu.CompilerParams(vmem_limit_bytes=56 * 2**20),
        cost_estimate=pl.CostEstimate(
            flops=2 * total * model * sum(widths), bytes_accessed=2 * total * (model + sum(widths)), transcendentals=0
        ),
    )(*args)


def middle_kernel(count, at_ref, *refs):
    parts, weights, (x_ref, gain_ref, mixed, mid, two) = refs[:count], refs[count : 2 * count], refs[2 * count :]
    cols = weights[0].shape[1]
    spans = [pl.ds(pl.multiple_of((at_ref[0] ^ m) * cols, cols), cols) for m in range(count)]
    for m in range(count):
        mixed[:, spans[m]] = parts[m][0]
    for m in range(count):
        mid[:, spans[m]] = x_ref[0, :, spans[m]].astype(F32) + dot_nn(mixed[...], weights[m][...])
    value = mid[...]
    two[...] = (value * inv_rms(value) * gain_ref[...]).astype(BF)


def to_middle(parts, out_rel, x, r, gain, at):
    _, part, model = x.shape
    count = len(out_rel)
    return pl.pallas_call(
        functools.partial(middle_kernel, count),
        grid=(1,),
        in_specs=[pl.BlockSpec(memory_space=pltpu.SMEM)]
        + [piece_spec(p.shape, i) for p, i in parts]
        + [pl.BlockSpec(w.shape, lambda j: (0, 0)) for w in out_rel]
        + [piece_spec(x.shape, r), pl.BlockSpec(gain.shape, lambda j: (0, 0))],
        out_specs=[pl.BlockSpec((part, model), lambda j: (0, 0))] * 3,
        out_shape=[
            jax.ShapeDtypeStruct((part, model), BF),
            jax.ShapeDtypeStruct((part, model), F32),
            jax.ShapeDtypeStruct((part, model), BF),
        ],
        compiler_params=pltpu.CompilerParams(vmem_limit_bytes=48 * 2**20),
        cost_estimate=pl.CostEstimate(flops=2 * part * model * model, bytes_accessed=3 * model * model, transcendentals=0),
    )(at[None], *[p for p, _ in parts], *out_rel, x, gain)


def stacked(refs):
    values = [v[...].astype(F32) for v in refs]
    return values[0] if len(values) == 1 else jnp.concatenate(values, 0)


def second_kernel(count, fars, at_ref, *refs):
    weights, far, refs = refs[:count], refs[count : count + fars], refs[count + fars :]
    own_ref, near_ref, mid_ref, g_ref, gain_ref, grad_ref, low_ref, parts, mixed = refs
    cols = parts.shape[2]
    spans = [pl.ds(pl.multiple_of((at_ref[0] ^ m) * cols, cols), cols) for m in range(count)]
    got = own_ref[0].astype(F32) + near_ref[0].astype(F32) + stacked(far)
    mid = mid_ref[...]
    grad_ref[...] = g_ref[0].astype(F32) + norm_backward(mid, inv_rms(mid), gain_ref[...], got)
    low_ref[...] = grad_ref[...].astype(BF)
    total = dot_nt(low_ref[:, spans[0]], weights[0][...])
    for m in range(1, count):
        total = total + dot_nt(low_ref[:, spans[m]], weights[m][...])
    mixed[...] = total
    for m in range(count):
        parts[m] = mixed[:, spans[m]].astype(BF)


def second_back(keep, near, far, mid, out_grad, r, gain, out_rel, at):
    part, model = mid.shape
    count = len(out_rel)
    cols = out_rel[0].shape[1]

    def whole(v):
        return pl.BlockSpec(v.shape, lambda j: (0, 0))

    return pl.pallas_call(
        functools.partial(second_kernel, count, len(far)),
        grid=(1,),
        in_specs=[pl.BlockSpec(memory_space=pltpu.SMEM)]
        + [whole(w) for w in [*out_rel, *far]]
        + [piece_spec(keep.shape, 0), piece_spec(near.shape, 0), whole(mid)]
        + [piece_spec(out_grad.shape, r), whole(gain)],
        out_specs=[whole(mid), whole(mid), pl.BlockSpec((count, part, cols), lambda j: (0, 0, 0))],
        out_shape=[
            jax.ShapeDtypeStruct((part, model), F32),
            jax.ShapeDtypeStruct((part, model), BF),
            jax.ShapeDtypeStruct((count, part, cols), BF),
        ],
        scratch_shapes=[pltpu.VMEM((part, model), F32)],
        compiler_params=pltpu.CompilerParams(vmem_limit_bytes=48 * 2**20),
        cost_estimate=pl.CostEstimate(flops=2 * part * model * model, bytes_accessed=3 * model * model, transcendentals=0),
    )(at[None], *out_rel, *far, keep, near, mid, out_grad, gain)


def out_kernel(count, rows_n, at_ref, *refs):
    mixed, low, outs = refs[:rows_n], refs[rows_n : 2 * rows_n], refs[2 * rows_n :]
    cols = outs[0].shape[2]
    for m in range(count):
        span = pl.ds(pl.multiple_of((at_ref[0] ^ m) * cols, cols), cols)
        total = dot_tn(mixed[0][...], low[0][:, span])
        for r in range(1, rows_n):
            total = total + dot_tn(mixed[r][...], low[r][:, span])
        outs[m % 2][m // 2] = total.astype(BF)


def grad_out_parts(mixed, low, count, at):
    part, model = mixed[0].shape
    rows_n = len(mixed)
    cols = model // count
    tile = 256
    return pl.pallas_call(
        functools.partial(out_kernel, count, rows_n),
        grid_spec=pltpu.PrefetchScalarGridSpec(
            num_scalar_prefetch=1,
            grid=(model // tile,),
            in_specs=[pl.BlockSpec((part, tile), lambda j, ref: (0, j))] * rows_n
            + [pl.BlockSpec((part, model), lambda j, ref: (0, 0))] * rows_n,
            out_specs=[pl.BlockSpec((count // 2, tile, cols), lambda j, ref: (0, j, 0))] * 2,
        ),
        out_shape=[jax.ShapeDtypeStruct((count // 2, model, cols), BF)] * 2,
        compiler_params=pltpu.CompilerParams(vmem_limit_bytes=48 * 2**20),
        cost_estimate=pl.CostEstimate(flops=4 * part * model * model, bytes_accessed=3 * model * model, transcendentals=0),
    )(at[None], *mixed, *low)


def first_kernel(count, at_ref, grad_ref, w_ref, keep, send, total):
    part = keep.shape[1]
    total[...] = dot_nt(grad_ref[0], w_ref[...])
    for m in range(count):
        here = pl.ds(pl.multiple_of((at_ref[0] ^ m) * part, part), part)
        (keep, send)[m % 2][m // 2] = total[here, :].astype(BF)


def first_parts(grad_joined, w_side, r, count, at):
    _, length, wide = grad_joined.shape
    model = w_side.shape[0]
    part = length // count
    tile = 256
    return pl.pallas_call(
        functools.partial(first_kernel, count),
        grid_spec=pltpu.PrefetchScalarGridSpec(
            num_scalar_prefetch=1,
            grid=(model // tile,),
            in_specs=[
                pl.BlockSpec((1, length, wide), lambda j, ref: (r, 0, 0), pipeline_mode=pl.Buffered(1)),
                pl.BlockSpec((tile, wide), lambda j, ref: (j, 0)),
            ],
            out_specs=[pl.BlockSpec((count // 2, part, tile), lambda j, ref: (0, 0, j))] * 2,
            scratch_shapes=[pltpu.VMEM((length, tile), F32)],
        ),
        out_shape=[jax.ShapeDtypeStruct((count // 2, part, model), BF)] * 2,
        compiler_params=pltpu.CompilerParams(vmem_limit_bytes=48 * 2**20),
        cost_estimate=pl.CostEstimate(
            flops=2 * length * wide * model, bytes_accessed=4 * length * wide, transcendentals=0
        ),
    )(at[None], grad_joined, w_side)


def last_kernel(rows_n, spans, *refs):
    keeps, nears, mids, refs = refs[:rows_n], refs[rows_n : 2 * rows_n], refs[2 * rows_n : 3 * rows_n], refs[3 * rows_n :]
    fars, (x_ref, gain_ref, out_ref) = refs[:-3], refs[-3:]
    for r, (low, high) in enumerate(spans):
        got = keeps[r][0].astype(F32) + nears[r][0].astype(F32) + stacked(fars[low:high])
        x = x_ref[r].astype(F32)
        out_ref[r] = mids[r][...] + norm_backward(x, inv_rms(x), gain_ref[...], got)


def layer_kernel(rows_n, spans, *refs):
    keeps, nears, mids, refs = refs[:rows_n], refs[rows_n : 2 * rows_n], refs[2 * rows_n : 3 * rows_n], refs[3 * rows_n :]
    fars, out_ref = refs[:-1], refs[-1]
    for r, (low, high) in enumerate(spans):
        got = keeps[r][0].astype(F32) + nears[r][0].astype(F32) + stacked(fars[low:high])
        out_ref[r] = (mids[r][...] + got).astype(BF)


def sum_rows(kernel, dtype, keep, near, far, mids, *more):
    rows_n = len(mids)
    shape = (rows_n,) + mids[0].shape
    spans, flat = [], []
    for row in far:
        spans.append((len(flat), len(flat) + len(row)))
        flat += row
    return pl.pallas_call(
        functools.partial(kernel, rows_n, spans),
        grid=(1,),
        in_specs=[piece_spec(v.shape, 0) for v in [*keep, *near]]
        + [pl.BlockSpec(v.shape, lambda j: (0, 0)) for v in mids]
        + [pl.BlockSpec((n, v.shape[1]), functools.partial(lambda i, j: (i, 0), i)) for v, i, n in flat]
        + [pl.BlockSpec(v.shape, functools.partial(lambda n, j: (0,) * n, v.ndim)) for v in more],
        out_specs=pl.BlockSpec(shape, lambda j: (0, 0, 0)),
        out_shape=jax.ShapeDtypeStruct(shape, dtype),
        compiler_params=pltpu.CompilerParams(vmem_limit_bytes=48 * 2**20),
        cost_estimate=pl.CostEstimate(flops=0, bytes_accessed=16 * rows_n * mids[0].size, transcendentals=0),
    )(*keep, *near, *mids, *[v for v, _, _ in flat], *more)


def fold(keep, got, low=0, high=None):
    return (keep[1, low:high].astype(F32) + got[1, low:high].astype(F32)).astype(BF)


def tie(*groups):
    return lax.optimization_barrier(groups)


def per_device(
    inputs,
    doc_ids,
    gain_attn,
    w_proj,
    w_beta,
    conv_taps,
    w_out,
    gain_mlp,
    w_gate,
    w_up,
    w_down,
    out_grad,
):
    rows_n, part, model = inputs.shape
    heads_n = w_beta.shape[1]
    taps_n, width_out = conv_taps.shape
    dp_n, seq_n = lax.axis_size("dp"), lax.axis_size("seq")
    at = lax.axis_index("seq")
    length = part * seq_n
    heads = heads_n // seq_n
    width = model // heads_n
    cols = heads * width
    wide = 4 * cols
    shard = w_proj.shape[0]
    ff = w_gate.shape[1]
    unit = ff // (dp_n * seq_n)
    mine_n = dp_n * unit
    quarter = model // seq_n
    rows = range(rows_n)
    last = rows_n - 1

    proj_mine = lax.dynamic_slice_in_dim(w_proj, at * wide, wide, 1)
    side = jnp.concatenate([w_beta, gain_attn[:, None], gain_mlp[:, None]], 1)
    side = jnp.pad(side.astype(BF), ((0, 0), (0, 126 - heads_n)))
    packed = jnp.concatenate([proj_mine.astype(BF), side], 1)
    sent = []
    ring = ring_gather(packed, sent)
    hop = next(ring)

    flat = jnp.concatenate([doc_ids.astype(BF).reshape(-1), conv_taps.astype(BF).reshape(-1)])
    flat = after(flat, packed)
    flat = [flat, swap(flat, 1), swap(flat, 2), swap(flat, 3)]
    own_x, units = inputs, pack_units(w_gate, w_up, w_down, at)
    hop, flat, own_x, units = tie(hop, flat, own_x, units)
    hop = ring.send(hop)
    flat, own_x, _ = tie(flat, own_x, sent)
    far_x = [swap(own_x[0:1], 2)]
    flat = in_order(flat, at)
    cut = rows_n * part
    doc = jnp.concatenate([t[:cut].reshape(rows_n, part) for t in flat], 1).astype(F32)
    taps_shard = jnp.concatenate([t[cut:].reshape(taps_n, width_out) for t in flat], 1)
    taps_shard = jnp.pad(taps_shard, ((0, 16 - taps_n), (0, quarter - taps_shard.shape[1])))
    out_mine = lax.dynamic_slice_in_dim(w_out, at * quarter, quarter, 1).astype(BF)
    out_mine = lax.all_gather(jnp.concatenate([out_mine, taps_shard], 0), "dp", axis=0)
    hop, far_x, doc = tie(hop, far_x, doc)
    hop = ring.send(hop)
    doc, own_x, far_x, _ = tie(doc, own_x, far_x, sent)
    far_x += [swap(own_x[r : r + 1], 2) for r in rows[1:]]
    skew_x = [swap(far_x[0], 1)]
    near_x = swap(own_x, 1)
    lanes = lax.broadcasted_iota(jnp.int32, (1, 1, 128), 2)
    info = jnp.where(lanes == 0, doc[:, :, None], 0.0)
    for shift_by in range(1, taps_n):
        same = (doc[:, shift_by:] == doc[:, :-shift_by]).astype(F32)
        info = jnp.where(lanes == shift_by, jnp.pad(same, ((0, 0), (shift_by, 0)))[:, :, None], info)
    aux = [info[r : r + 1] for r in rows]
    doc_rows = [jnp.broadcast_to(doc[r : r + 1, None, :], (1, 8, length)) for r in rows]
    hop, far_x, near_x, skew_x, aux, doc_rows = tie(hop, far_x, near_x, skew_x, aux, doc_rows)
    hop = ring.send(hop)
    far_x, _ = tie(far_x, sent)
    skew_x += [swap(far_x[r], 1) for r in rows[1:]]
    hop, skew_x = tie(hop, skew_x)
    proj_shards = drain(ring, hop)
    x_rel = [[(own_x, r), (near_x, r), (far_x[r], 0), (skew_x[r], 0)] for r in rows]

    ring = ring_gather(after(units, proj_shards[0]), sent)
    hop = next(ring)
    own_g, _ = tie(out_grad, sent)
    far_g, near_g = swap(own_g, 2), swap(own_g, 1)
    normed, joined, logit = None, [], []
    for r in rows:
        normed, j, l, gains = project(x_rel[r], heads_n, proj_shards, wide, at, r, normed)
        joined.append(j)
        logit.append(l)
    gain_one, gain_two = gains[0:1], gains[1:2]
    hop, joined, logit, out_mine = tie(hop, joined, logit, out_mine)
    hop = ring.send(hop)
    joined, out_mine, _ = tie(joined, out_mine, sent)
    taps_full = out_mine[:, shard : shard + taps_n, :shard].transpose(1, 0, 2).reshape(taps_n, model)
    taps_mine = lax.dynamic_slice_in_dim(taps_full.astype(F32), at * cols, cols, 1)
    taps_mine = jnp.pad(taps_mine, ((0, 8 - taps_n), (0, 0)))
    out_mine = out_mine[:, :shard].reshape(model, quarter)
    out_far, out_near = swap(out_mine, 2), swap(out_mine, 1)

    def exchange(parts):
        return [(parts, 0)] + [(swap(parts[m : m + 1], m), 0) for m in range(1, seq_n)]

    kept, attn, pair = [], [], []
    for r in rows:
        outs = attend_fwd(joined[r], aux[r], logit[r], doc_rows[r], taps_mine, at, heads, taps_n, seq_n)
        if r == 0:
            outs, hop, joined, out_far, out_near, near_g, far_g = tie(
                outs, hop, joined, out_far, out_near, near_g, far_g
            )
        elif r == last:
            outs, hop, pair, out_skew, skew_g = tie(outs, hop, pair, out_skew, skew_g)
        hop = ring.send(hop)
        mine, joined, pair, _ = tie(outs[0], joined, pair, sent)
        attn.append(mine)
        pair.append(swap(mine[2:], 2))
        if r == 0:
            out_skew, skew_g = swap(out_far, 1), swap(far_g, 1)
        kept.append(outs[1:])
    pair_near = [swap(jnp.stack([attn[0][1], pair[0][1]]), 1)]
    out_rel = [out_mine, out_near, out_far, out_skew]

    def middle_of(r):
        parts = [(attn[r], 0), (pair_near[r], 0), (pair[r], 0), (pair_near[r], 1)]
        return to_middle(parts, out_rel, inputs, r, gain_two, at)

    done = [middle_of(0)]
    done[0], pair[1] = tie(done[0], pair[1])
    pair_near.append(swap(jnp.stack([attn[1][1], pair[1][1]]), 1))
    two = done[0][2]
    two_rel = [[two, swap(two, 1), swap(two, 2)]]
    done.append(middle_of(1))
    done[1], hop = tie(done[1], hop)
    mixed, middle = [v[0] for v in done], [v[1] for v in done]
    two = done[1][2]
    two_rel.append([two, swap(two, 1), swap(two, 2)])
    full = place(drain(ring, hop), [(shard, mine_n), (shard, mine_n), (unit, model)])
    full, two_rel[0] = tie(full, two_rel[0])
    g_rel = [[(own_g, r), (near_g, r), (far_g, r), (skew_g, r)] for r in rows]

    prior, norm, layer = None, [], []
    for r in rows:
        two_rel[r].append(swap(two_rel[r][2], 1))
        prior = hidden_units(two_rel[r], g_rel[r], *full, r, prior)
        if r == 0:
            prior, two_rel[1] = tie(prior, two_rel[1])
        else:
            prior, near_n = tie(prior, near_n)
            far_n = fold(norm[0][0], near_n[0])
            prior, far_n = tie(prior, far_n)
            far_n = [[swap(far_n, 2)]]
        outs = model_units(prior, *full, r, seq_n)
        norm.append(outs[:2])
        layer.append(outs[2:])
        if r == 0:
            near_n = [swap(norm[0][1], 1)]
    hid, g_gate, g_up = [v.reshape(rows_n * length, -1) for v in prior]
    upper, lower = (0, part // 2), (part // 2, part)

    def second(r):
        return second_back(norm[r][0], near_n[r], far_n[r], middle[r], out_grad, r, gain_two, out_rel, at)

    norm[last], layer, hid, far_n = tie(norm[last], layer, hid, far_n)
    near_n.append(swap(norm[last][1], 1))
    done = [second(0)]
    done[0], hid, near_n, layer = tie(done[0], hid, near_n, layer)
    heads_rel = [exchange(done[0][2])]
    far_n.append([fold(norm[last][0], near_n[last], *upper)])
    hid, far_n[last] = tie(hid, far_n[last])
    far_n[last] = [swap(far_n[last][0], 2)]
    near_l = [swap(layer[r][1], 1) for r in rows]
    (grad_down,) = outer([hid], [[g for rel in g_rel for g in rel]])
    grad_down, g_gate, near_l, far_n, heads_got = tie(grad_down, g_gate, near_l, far_n, [p for p, _ in heads_rel[0]])
    heads_rel = [[(p, 0) for p in heads_got]]
    far_n[last].append(fold(norm[last][0], near_n[last], *lower))
    far_l = [fold(layer[0][0], near_l[0], *upper)]
    g_gate, far_n[last][1], far_l = tie(g_gate, far_n[last][1], far_l)
    far_n[last][1] = swap(far_n[last][1], 2)
    far_l = [swap(far_l[0], 2)]
    grad_gate, grad_up = outer([p for rel in two_rel for p in rel], [[g_gate], [g_up]])
    grad_gate, grad_up, far_n, far_l = tie(grad_gate, grad_up, far_n, far_l)
    ring = ring_scatter([grad_gate, grad_up, grad_down], None, sent)
    hop = next(ring)
    far_n, _ = tie(far_n, sent)
    done.append(second(last))
    grad_mid, low = [d[0] for d in done], [d[1] for d in done]
    keep_out, send_out = grad_out_parts(mixed, low, seq_n, at)
    hop, keep_out, send_out, heads_1, grad_mid = tie(hop, keep_out, send_out, done[last][2], grad_mid)
    hop = ring.send(hop)
    far_l.append(jnp.concatenate([fold(layer[0][0], near_l[0], *lower), fold(layer[last][0], near_l[last], *upper)], 0))
    send_out, heads_1, far_l, _ = tie(send_out, heads_1, far_l, sent)
    pair = swap(heads_1[2:], 2)
    near_out = swap(send_out, 1)
    far_l[1] = swap(far_l[1], 2)

    def backward(r, prior):
        return attend_bwd(
            joined[r], aux[r], logit[r], taps_mine, heads_rel[r], kept[r], at, heads, taps_n, r, rows_n, prior
        )

    outs = backward(0, None)
    outs, hop, pair, near_out, far_l = tie(outs, hop, pair, near_out, far_l)
    (proj_full,) = place(proj_shards, [(shard, packed.shape[1])])
    hop = ring.send(hop)
    far_out = fold(keep_out, near_out)
    outs, far_out, pair, _ = tie(outs, far_out, pair, sent)
    pair_near = swap(jnp.stack([heads_1[1], pair[1]]), 1)
    far_out = swap(far_out, 2)
    parts = [first_parts(outs[0], proj_full, 0, seq_n, at)]
    outs, parts, pair_near = tie(outs, parts, pair_near)
    heads_rel.append([(heads_1, 0), (pair_near, 0), (pair, 0), (pair_near, 1)])
    near_in = [swap(parts[0][1], 1)]
    far_l.append(swap(fold(layer[last][0], near_l[last], *lower), 2))
    grad_taps = [outs[1][0]]
    outs = backward(last, outs[0])
    outs, hop, far_out, far_l, near_in = tie(outs, hop, far_out, far_l, near_in)
    hop = ring.send(hop)
    grad_joined = outs[0]
    grad_taps.append(outs[1][0])
    far_in = [fold(parts[0][0], near_in[0])]
    grad_joined, far_in, far_out, _ = tie(grad_joined, far_in, far_out, sent)
    far_in = [swap(far_in[0], 2)]
    parts.append(first_parts(grad_joined, proj_full, last, seq_n, at))
    parts, grad_joined = tie(parts, grad_joined)
    near_in.append(swap(parts[last][1], 1))

    grad_out = (keep_out[0].astype(F32) + near_out[0].astype(F32) + far_out.astype(F32)).astype(BF)
    taps_grad = sum(grad_taps)[:, :taps_n].transpose(1, 0, 2).reshape(taps_n, cols)
    taps_grad = lax.dynamic_update_slice_in_dim(jnp.zeros((taps_n, model), F32), taps_grad, at * cols, 1)
    taps_grad = jnp.pad(taps_grad.T.astype(BF), ((0, 0), (heads_n, 128 - heads_n - taps_n)))
    tall, joined_all = normed.reshape(rows_n * length, model), grad_joined.reshape(rows_n * length, -1)
    split = wide // 3 * 2
    (grad_one,) = outer([tall], [[joined_all]], (0, split))
    grad_one, joined_all, taps_grad, grad_out, near_in = tie(grad_one, joined_all, taps_grad, grad_out, near_in)
    more = []
    ring_one = ring_scatter([grad_one], None, sent)
    hop_one = next(ring_one)
    next_in = fold(parts[last][0], near_in[last])
    joined_all, next_in, _ = tie(joined_all, next_in, sent)
    (grad_two,) = outer([tall], [[joined_all]], (split, joined_all.shape[1]))
    grad_two, hop_one, hop, far_in = tie(grad_two, hop_one, hop, far_in)
    hop_one = ring_one.send(hop_one)
    ring_two = ring_scatter([grad_out, grad_two], taps_grad, more)
    hop_two = next(ring_two)
    grad_units = drain(ring, hop)
    middle, grad_units, next_in, _, _ = tie(middle, grad_units, next_in, sent, more)
    far_in.append(swap(next_in, 2))
    thirds = [i * (shard // 48) * 16 for i in range(3)] + [shard]
    units_cut = [grad_units[lo:hi] for lo, hi in zip(thirds, thirds[1:])]
    half = part // 2
    layer_out = sum_rows(
        layer_kernel, BF, [v[0] for v in layer], near_l, [[(far_l[0], 0, half), (far_l[1], 0, half)], [(far_l[1], 1, half), (far_l[2], 0, half)]], middle
    )
    layer_out, hop_one, units_cut = tie(layer_out, hop_one, units_cut)
    hop_one = ring_one.send(hop_one)
    hop_two, far_in, units_cut, _ = tie(hop_two, far_in, units_cut, sent)
    hop_two = ring_two.send(hop_two)
    far_in, units_cut, _ = tie(far_in, units_cut, more)
    units_far = [swap(units_cut[0], 2)]
    grad_in = sum_rows(
        last_kernel, F32, [v[0] for v in parts], near_in, [[(v, 0, part)] for v in far_in], grad_mid, inputs, gain_one
    )
    grad_in, hop_one, units_far = tie(grad_in, hop_one, units_far)
    hop_one = ring_one.send(hop_one)
    units_cut, _ = tie(units_cut, sent)
    units_far.append(swap(units_cut[1], 2))
    hop_two, units_far = tie(hop_two, units_far)
    hop_two = ring_two.send(hop_two)
    units_cut, _ = tie(units_cut, more)
    units_far.append(swap(units_cut[2], 2))
    hop_one, units_far = tie(hop_one, units_far)
    grad_one = drain(ring_one, hop_one)
    far_all = jnp.concatenate(units_far, 0)
    hop_two, grad_one, far_all = tie(hop_two, grad_one, far_all)
    hop_two = ring_two.send(hop_two)
    far_all, grad_one, _ = tie(far_all, grad_one, more)
    units_near, units_skew = swap(grad_units, 1), swap(far_all, 1)
    one_far, one_near = swap(grad_one, 2), swap(grad_one, 1)
    units_rel = [grad_units, units_near, far_all, units_skew]
    gate_out, up_out, sums = spread_units(units_rel, w_gate, w_up, at)
    gain_two_out = sums / gain_mlp.astype(BF).astype(F32)
    hop_two, gate_out, up_out, gain_two_out, one_far, one_near = tie(
        hop_two, gate_out, up_out, gain_two_out, one_far, one_near
    )
    grad_two = drain(ring_two, hop_two)
    two_far, two_near = swap(grad_two, 2), swap(grad_two, 1)
    units_rel, one_far, _ = tie(units_rel, one_far, grad_two)
    down_out = unfold_units(units_rel, w_down, at)
    proj_out, sums = spread_first([grad_one, one_near, one_far, swap(one_far, 1)], w_proj, at)
    two_far, two_near, proj_out, down_out = tie(two_far, two_near, proj_out, down_out)
    rel = [grad_two, two_near, two_far, swap(two_far, 1)]
    proj_out, out_out, more_sums = spread_last(rel, w_proj, quarter, proj_out, at)
    sums = sums + more_sums
    tail = [t[:, -128:].astype(F32) for t in rel]
    tail = (tail[0] + tail[1]) + (tail[2] + tail[3])
    beta_out = tail[:, :heads_n]
    sums = sums + jnp.sum(beta_out * w_beta.astype(BF).astype(F32), 1)
    gain_one_out = sums / gain_attn.astype(BF).astype(F32)
    taps_out = lax.dynamic_slice_in_dim(tail[:, heads_n : heads_n + taps_n], at * width_out, width_out, 0).T
    return (
        layer_out,
        grad_in,
        gain_one_out,
        proj_out,
        beta_out,
        taps_out,
        out_out,
        gain_two_out,
        gate_out,
        up_out,
        down_out,
    )


def solution(mesh):
    in_specs = (
        P("dp", "seq", None),
        P("dp", "seq"),
        P("dp"),
        P("dp", None),
        P("dp", None),
        P(None, ("dp", "seq")),
        P("dp", None),
        P("dp"),
        P("dp", None),
        P("dp", None),
        P("dp", None),
        P("dp", "seq", None),
    )
    out_specs = (
        P("dp", "seq", None),
        P("dp", "seq", None),
        P("dp"),
        P("dp", None),
        P("dp", None),
        P(None, ("dp", "seq")),
        P("dp", None),
        P("dp"),
        P("dp", None),
        P("dp", None),
        P("dp", None),
    )
    return jax.shard_map(per_device, mesh=mesh, in_specs=in_specs, out_specs=out_specs, check_vma=False)
```

```python
import functools
import jax
import jax.numpy as jnp
from jax import lax
from jax.experimental import pallas as pl
from jax.experimental.pallas import tpu as pltpu
from jax.sharding import PartitionSpec as P

F32 = jnp.float32
BF = jnp.bfloat16
NORM_EPS = 1e-06
BLOCK = 256
HALF = 128


def dot_nn(a, b):
    return lax.dot_general(a, b, (((1,), (0,)), ((), ())), preferred_element_type=F32)


def dot_nt(a, b):
    return lax.dot_general(a, b, (((1,), (1,)), ((), ())), preferred_element_type=F32)


def dot_tn(a, b):
    return lax.dot_general(a, b, (((0,), (0,)), ((), ())), preferred_element_type=F32)


def mul(a, b):
    return dot_nn(a.astype(BF), b.astype(BF))


def indices(rows, cols):
    return (
        lax.broadcasted_iota(jnp.int32, (rows, cols), 0),
        lax.broadcasted_iota(jnp.int32, (rows, cols), 1),
    )


def unit_inverse(systems, fill=()):
    size = systems[0].shape[0]
    row, col = indices(size, size)
    eye = jnp.where(row == col, 1.0, 0.0).astype(F32)
    near = (row - col == 1) & (row % 2 == 1)
    solved = [eye - jnp.where(near, g, 0.0) for g in systems]
    span = 2
    fill = list(fill)
    share = -(-len(fill) // 6)
    while span < size:
        for _ in range(share):
            if fill:
                fill.pop(0)()
        corner = (row // (2 * span) == col // (2 * span)) & (row % (2 * span) >= span) & (col % (2 * span) < span)
        below = [jnp.where(corner, g, 0.0) for g in systems]
        step = [mul(n, c) for n, c in zip(solved, below)]
        solved = [n - mul(s, n) for n, s in zip(solved, step)]
        span *= 2
    for more in fill:
        more()
    return solved


def block_inverse(g, fill=()):
    h = HALF
    parts = unit_inverse([p for b in g for p in (b[:h, :h], b[h:, h:])], fill)
    out = []
    for i, b in enumerate(g):
        top, bottom = parts[2 * i], parts[2 * i + 1]
        corner = -mul(mul(bottom, b[h:, :h]), top)
        upper = jnp.concatenate([top, jnp.zeros((h, h), F32)], 1)
        lower = jnp.concatenate([corner, bottom], 1)
        out.append(jnp.concatenate([upper, lower], 0))
    return out


def house(u, taps_ref, aux, taps_n):
    mixed = taps_ref[0:1, :] * u
    for s in range(1, taps_n):
        mixed = mixed + (taps_ref[s : s + 1, :] * aux[:, s : s + 1]) * pltpu.roll(u, s, 0)
    inv = lax.rsqrt(jnp.sum(mixed * mixed, -1, keepdims=True) + NORM_EPS)
    return mixed * inv, inv


def lane_pick(aux, lane):
    pos = lax.broadcasted_iota(jnp.int32, aux.shape, 1)
    return jnp.sum(jnp.where(pos == lane, aux, 0.0), 1, keepdims=True)


def fwd_kernel(taps_n, at_ref, join_ref, aux_ref, logit_ref, doc_ref, taps_ref, *rest):
    length = join_ref.shape[1]
    out_ref, rest = rest[0], rest[1:]
    part = out_ref.shape[1]
    (p_refs, x_ref, n_ref, m_ref, z_ref, qt_ref, w_ref, kt_ref, e_ref, run) = (rest[:-9],) + rest[-9:]
    d = taps_ref.shape[1]
    nb = length // BLOCK
    lane = at_ref[0] * pl.num_programs(1) + pl.program_id(1)
    aux = aux_ref[0]
    beta_all = 2.0 * jax.nn.sigmoid(lane_pick(logit_ref[0].astype(F32), lane))
    u = join_ref[0, :, 3 * d : 4 * d].astype(F32)
    w_all, _ = house(u, taps_ref, aux, taps_n)
    w_ref[0] = w_all.astype(BF)
    row, col = indices(BLOCK, BLOCK)
    later = row > col
    notbefore = row >= col
    scale = d ** -0.5
    sl = [slice(b * BLOCK, (b + 1) * BLOCK) for b in range(nb)]
    w = [w_ref[0, s, :] for s in sl]
    beta = [beta_all[s] for s in sl]
    k = [join_ref[0, s, d : 2 * d] for s in sl]
    q = [join_ref[0, s, 0:d] for s in sl]
    g = [jnp.where(later, beta[b] * dot_nt(w[b], w[b]), 0.0) for b in range(nb)]
    side_products = [[None] * nb for _ in range(3)]

    def make(i, b):
        def run_one():
            if i == 0:
                side_products[0][b] = jnp.where(later, beta[b] * dot_nt(w[b], k[b]), 0.0).astype(BF)
            elif i == 1:
                m_ref[0, b] = jnp.where(notbefore, dot_nt(q[b], w[b]), 0.0).astype(BF)
            else:
                side_products[2][b] = dot_nt(q[b], k[b])

        return run_one

    inv = block_inverse(g, [make(i, b) for i in range(3) for b in range(nb)])
    for b in range(nb):
        nn = inv[b].astype(BF)
        n_ref[0, b] = nn
        r = side_products[0][b]
        z = dot_nn(nn, (beta[b] * w_all[sl[b]]).astype(BF)).astype(BF)
        z_ref[0, sl[b], :] = z
        x = dot_nn(nn, r).astype(BF)
        x_ref[0, b] = x
        m = m_ref[0, b]
        diag = side_products[2][b] - dot_nn(m, x)
        kb = k[b].astype(F32) - dot_tn(x, w[b])
        allowed = notbefore & (aux[sl[b], 0:1] == doc_ref[0, 0:1, sl[b]])
        diag = jnp.where(allowed, diag * scale, -1e30)
        if b > 0:
            start = b * BLOCK
            qt = (q[b].astype(F32) - dot_nn(m, z)).astype(BF)
            qt_ref[0, sl[b], :] = qt
            off = start * (b - 1) // 2
            kt = run[0:start, :].astype(BF)
            kt_ref[0, off : off + start, :] = kt
            side = dot_nt(qt, kt)
            ok = aux[sl[b], 0:1] == doc_ref[0, 0:1, 0:start]
            side = jnp.where(ok, side * scale, -1e30)
            peak = jnp.maximum(jnp.max(diag, 1, keepdims=True), jnp.max(side, 1, keepdims=True))
            ps = jnp.exp(side - peak)
            pd = jnp.exp(diag - peak)
            inv_total = 1.0 / (jnp.sum(ps, 1, keepdims=True) + jnp.sum(pd, 1, keepdims=True))
            ps = (ps * inv_total).astype(BF)
            pd = (pd * inv_total).astype(BF)
            p_refs[b][0, :, 0:start] = ps
            p_refs[b][0, :, start : start + BLOCK] = pd
            o = dot_nn(ps, join_ref[0, 0:start, 2 * d : 3 * d]) + dot_nn(pd, join_ref[0, sl[b], 2 * d : 3 * d])
        else:
            qt_ref[0, sl[b], :] = jnp.zeros((BLOCK, d), BF)
            peak = jnp.max(diag, 1, keepdims=True)
            pd = jnp.exp(diag - peak)
            pd = (pd / jnp.sum(pd, 1, keepdims=True)).astype(BF)
            p_refs[b][0] = pd
            o = dot_nn(pd, join_ref[0, sl[b], 2 * d : 3 * d])
        if part % BLOCK == 0:
            out_ref[(b * BLOCK // part) ^ at_ref[0], b * BLOCK % part : b * BLOCK % part + BLOCK, :] = o.astype(BF)
        else:
            for c in range(BLOCK // part):
                out_ref[(b * BLOCK // part + c) ^ at_ref[0]] = o[c * part : (c + 1) * part].astype(BF)
        if b < nb - 1:
            e = dot_tn(w[b], z).astype(BF)
            e_ref[0, b] = e
            if b > 0:
                run[0:start, :] = run[0:start, :] - dot_nt(kt, e)
            run[sl[b], :] = kb
        else:
            e_ref[0, b] = jnp.zeros((d, d), BF)


def bwd_kernel(taps_n, seq_n, has_prior, at_ref, join_ref, aux_ref, logit_ref, taps_ref, *rest):
    nb = join_ref.shape[1] // BLOCK
    go_parts, rest = rest[:seq_n], rest[seq_n:]
    if has_prior:
        rest = rest[: nb + 8] + rest[nb + 9 :]
    p_refs = rest[:nb]
    (x_ref, n_ref, m_ref, z_ref, qt_ref, w_ref, kt_ref, e_ref, gj_ref, gt_ref, gk, gv, gw, go_ref) = rest[nb:]
    part = go_parts[0].shape[1]
    for m in range(seq_n):
        go_ref[pl.ds(pl.multiple_of((at_ref[0] ^ m) * part, part), part), :] = go_parts[m][0]
    length = join_ref.shape[1]
    d = taps_ref.shape[1]
    head = pl.program_id(1)
    lane = at_ref[0] * pl.num_programs(1) + head
    aux = aux_ref[0]
    beta_all = 2.0 * jax.nn.sigmoid(lane_pick(logit_ref[0].astype(F32), lane))
    row, col = indices(BLOCK, BLOCK)
    later = row > col
    notbefore = row >= col
    scale = d ** -0.5
    gbeta = [None] * nb

    def span(i):
        return pl.ds(pl.multiple_of((4 * head + i) * d, d), d)

    for b in reversed(range(nb)):
        start, end = b * BLOCK, (b + 1) * BLOCK
        s = slice(start, end)
        last = b == nb - 1
        w, q, k = w_ref[0, s, :], join_ref[0, s, 0:d], join_ref[0, s, d : 2 * d]
        beta = beta_all[s]
        x, n, m, z = x_ref[0, b], n_ref[0, b], m_ref[0, b], z_ref[0, s, :]
        go = go_ref[s, :]
        p = p_refs[b][0]
        gp = dot_nt(go, join_ref[0, 0:end, 2 * d : 3 * d])
        pf = p.astype(F32)
        inner = jnp.sum(pf * gp, 1, keepdims=True)
        gs = (pf * (gp - inner) * scale).astype(BF)
        gv_new = dot_tn(p, go)
        gsd = gs[:, start:end]
        if last:
            gv[...] = gv_new
        else:
            gv[0:end, :] += gv_new
        stack_m = [gsd]
        if b > 0:
            off = start * (b - 1) // 2
            kt, qt = kt_ref[0, off : off + start, :], qt_ref[0, s, :]
            gside = gs[:, 0:start]
            gqt_f = dot_nn(gside, kt)
            gqt = gqt_f.astype(BF)
            fresh = dot_tn(gside, qt)
        if not last:
            gkt_f = gk[s, :]
            gkt = gkt_f.astype(BF)
        if b > 0 and not last:
            e = e_ref[0, b]
            old = gk[0:start, :]
            old_b = old.astype(BF)
            ge = (-dot_tn(old_b, kt)).astype(BF)
            gk[0:start, :] = old - dot_nn(old_b, e) + fresh
        elif b > 0:
            gk[0:start, :] = fresh
        has_z = b > 0
        xz = jnp.concatenate([x, z], 1) if has_z else x
        g_xz = jnp.concatenate([gsd, gqt], 1) if has_z else gsd
        mt = dot_tn(m, g_xz)
        gm = jnp.where(notbefore, -dot_nt(g_xz, xz), 0.0).astype(BF)
        gx = -mt[:, :BLOCK]
        if not last:
            gx = gx - dot_nt(w, gkt)
        gx = jnp.where(later, gx, 0.0).astype(BF)
        if has_z:
            gz = -mt[:, BLOCK:]
            if not last:
                gz = gz + dot_nn(w, ge)
            y = dot_tn(n, jnp.concatenate([gx, gz.astype(BF)], 1))
            y_z = y[:, BLOCK:]
        else:
            y = dot_tn(n, gx)
        gg = jnp.where(later, -dot_nt(y.astype(BF), xz), 0.0)
        y_x = jnp.where(later, y[:, :BLOCK], 0.0)
        wk = jnp.concatenate([w, k], 0)
        ww_wk = dot_nt(w, wk)
        gbv = jnp.sum(y_x * ww_wk[:, BLOCK:] + gg * ww_wk[:, :BLOCK], 1, keepdims=True)
        by = (beta * y_x).astype(BF)
        bg = (beta * gg).astype(BF)
        qw = jnp.concatenate([q, w], 0)
        gw_b = dot_tn(jnp.concatenate([gm, bg], 0), qw)
        if last:
            gw_b = gw_b + dot_nn(jnp.concatenate([bg, by], 1), wk)
        else:
            gw_b = gw_b + dot_nn(jnp.concatenate([bg, by, x], 1), jnp.concatenate([wk, -gkt], 0))
        gq_b = dot_nn(jnp.concatenate([gm, gsd], 1), wk)
        gk_b = dot_tn(jnp.concatenate([gsd, by], 0), qw)
        if has_z:
            gq_b = gq_b + gqt_f
            gw_b = gw_b + beta * y_z
            gbv = gbv + jnp.sum(y_z * w.astype(F32), 1, keepdims=True)
        if not last:
            gk_b = gk_b + gkt_f
            if has_z:
                gw_b = gw_b + dot_nt(z, ge)
        gbeta[b] = gbv
        gw[s, :] = gw_b
        gj_ref[0, s, span(0)] = gq_b.astype(BF)
        gj_ref[0, s, span(1)] = gk_b.astype(BF)
    gj_ref[0, :, span(2)] = gv[...].astype(BF)
    u = join_ref[0, :, 3 * d : 4 * d].astype(F32)
    w_all, inv = house(u, taps_ref, aux, taps_n)
    gw_all = gw[...]
    gc = inv * (gw_all - w_all * jnp.sum(gw_all * w_all, 1, keepdims=True))
    gu = taps_ref[0:1, :] * gc
    gt = [jnp.sum(gc * u, 0, keepdims=True)]
    for s in range(1, taps_n):
        held = gc * aux[:, s : s + 1]
        gt.append(jnp.sum(held * pltpu.roll(u, s, 0), 0, keepdims=True))
        gu = gu + taps_ref[s : s + 1, :] * pltpu.roll(held, length - s, 0)
    gj_ref[0, :, span(3)] = gu.astype(BF)
    gt.append(jnp.zeros((8 - taps_n, d), F32))
    gt_ref[0, 0] = jnp.concatenate(gt, 0)
    gb_all = jnp.concatenate(gbeta, 0) * beta_all * (1.0 - 0.5 * beta_all)
    pos = lax.broadcasted_iota(jnp.int32, aux.shape, 1)
    mine = jnp.where(pos == lane, gb_all, 0.0).astype(BF)
    tail = slice(gj_ref.shape[2] - 128, gj_ref.shape[2])

    @pl.when(head == 0)
    def _():
        gj_ref[0, :, tail] = mine

    @pl.when(head != 0)
    def _():
        gj_ref[0, :, tail] += mine


def res_specs(length, d, heads):
    nb = length // BLOCK
    shapes = [(BLOCK, (b + 1) * BLOCK) for b in range(nb)]
    shapes += [(nb, BLOCK, BLOCK)] * 3 + [(length, d)] * 3
    shapes += [(max(1, nb * (nb - 1) // 2) * BLOCK, d), (nb, d, d)]
    specs = [
        pl.BlockSpec((1,) + s, functools.partial(lambda n, r, h: (r * heads + h,) + (0,) * n, len(s))) for s in shapes
    ]
    return shapes, specs


def attend_fwd(joined, aux, logit, doc_rows, taps, at, heads, taps_n, seq_n):
    rows, length, packed = joined.shape
    d = taps.shape[1] // heads
    shapes, specs = res_specs(length, d, heads)
    return pl.pallas_call(
        functools.partial(fwd_kernel, taps_n),
        grid=(rows, heads),
        in_specs=[
            pl.BlockSpec(memory_space=pltpu.SMEM),
            pl.BlockSpec((1, length, 4 * d), lambda r, h: (r, 0, h)),
            pl.BlockSpec((1, length, 128), lambda r, h: (r, 0, 0)),
            pl.BlockSpec((1, length, 128), lambda r, h: (r, 0, 0)),
            pl.BlockSpec((1, 8, length), lambda r, h: (r, 0, 0)),
            pl.BlockSpec((8, d), lambda r, h: (0, h)),
        ],
        out_specs=[pl.BlockSpec((seq_n, length // seq_n, d), lambda r, h: (0, 0, h))] + specs,
        out_shape=[jax.ShapeDtypeStruct((seq_n, length // seq_n, heads * d), BF)]
        + [jax.ShapeDtypeStruct((rows * heads,) + s, BF) for s in shapes],
        scratch_shapes=[pltpu.VMEM((length, d), F32)],
        compiler_params=pltpu.CompilerParams(vmem_limit_bytes=56 * 2**20),
        cost_estimate=pl.CostEstimate(
            flops=rows * heads * 8 * 10**9, bytes_accessed=rows * heads * 5 * 10**6, transcendentals=0
        ),
    )(at[None], joined, aux, logit, doc_rows, taps)


def attend_bwd(joined, aux, logit, taps, grad_parts, res, at, heads, taps_n, row, rows_n, prior):
    rows, length, packed = joined.shape
    d = taps.shape[1] // heads
    shapes, specs = res_specs(length, d, heads)
    wide = heads * 4 * d + 128
    seq_n = len(grad_parts)
    args = [at[None], joined, aux, logit, taps, *[p for p, _ in grad_parts], *res]
    aliases = {}
    if prior is not None:
        aliases = {len(args): 0}
        args.append(prior)
    return pl.pallas_call(
        functools.partial(bwd_kernel, taps_n, seq_n, prior is not None),
        grid=(rows, heads),
        in_specs=[
            pl.BlockSpec(memory_space=pltpu.SMEM),
            pl.BlockSpec((1, length, 4 * d), lambda r, h: (r, 0, h)),
            pl.BlockSpec((1, length, 128), lambda r, h: (r, 0, 0)),
            pl.BlockSpec((1, length, 128), lambda r, h: (r, 0, 0)),
            pl.BlockSpec((8, d), lambda r, h: (0, h)),
        ]
        + [
            pl.BlockSpec((1, length // seq_n, d), functools.partial(lambda i, r, h: (i, 0, h), i)) for _, i in grad_parts
        ]
        + specs
        + [pl.BlockSpec(memory_space=pl.ANY)] * (0 if prior is None else 1),
        out_specs=[
            pl.BlockSpec((1, length, wide), lambda r, h: (row, 0, 0)),
            pl.BlockSpec((1, 1, 8, d), lambda r, h: (r, h, 0, 0)),
        ],
        out_shape=[
            jax.ShapeDtypeStruct((rows_n, length, wide), BF),
            jax.ShapeDtypeStruct((rows, heads, 8, d), F32),
        ],
        scratch_shapes=[pltpu.VMEM((length, d), F32)] * 3 + [pltpu.VMEM((length, d), BF)],
        input_output_aliases=aliases,
        compiler_params=pltpu.CompilerParams(vmem_limit_bytes=56 * 2**20),
        cost_estimate=pl.CostEstimate(
            flops=rows * heads * 16 * 10**9, bytes_accessed=rows * heads * 6 * 10**6, transcendentals=0
        ),
    )(*args)


def rects_of(sizes, rows):
    rects, at = [], 0
    for i, (r, c) in enumerate(sizes):
        if r == rows:
            rects.append((i, 0, r, 0, c, 0, at))
            at += c
        else:
            wide, rest = r * c // rows, rows - r
            rects.append((i, 0, r, 0, wide, 0, at))
            rects.append((i, 0, rest, wide, wide // 2, r, at))
            rects.append((i, rest, rest, wide, wide // 2, r, at + wide // 2))
            at += wide
    return rects, at


def clip(rects, low, high):
    out = []
    for i, r0, rows, c0, cols, p0, pc in rects:
        a, b = max(p0, low), min(p0 + rows, high)
        if a < b:
            out.append((i, r0 + a - p0, b - a, c0, cols, a - low, pc))
    return out


def ring_order(n):
    return list(range(0, n, 2)) + list(range(n - 1, 0, -2))


def ring_index(steps):
    n = lax.axis_size("dp")
    me = lax.axis_index("dp")
    place = jnp.where(me % 2 == 0, me // 2, n - 1 - me // 2)
    there = (place + jnp.array([(k + n) % n for k in steps], jnp.int32)) % n
    return jnp.where(there < n // 2, 2 * there, 2 * (n - 1 - there) + 1)


def to_right(value):
    order = ring_order(lax.axis_size("dp"))
    return lax.ppermute(value, "dp", [(a, b) for a, b in zip(order, order[1:] + order[:1])])


def to_left(value):
    order = ring_order(lax.axis_size("dp"))
    return lax.ppermute(value, "dp", [(b, a) for a, b in zip(order, order[1:] + order[:1])])


def middle_row(rows):
    return (rows // 2 + 15) // 16 * 16


def ring_gather(own, sent=None):
    n = lax.axis_size("dp")
    cut = middle_row(own.shape[0])
    pieces, steps = [own], [0]
    pair = (own, own)
    for k in range(1, n // 2 + 1):
        if k == n // 2:
            pair = (pair[0][:cut], pair[1][cut:])
        if sent is not None:
            sent[:] = pair
        pair = yield (to_right(pair[0]), to_left(pair[1]))
        pieces += list(pair)
        steps += [-k, k] if k < n // 2 else [k]
    return pieces, ring_index(steps)


def drain(gen, value=None):
    try:
        value = next(gen) if value is None else gen.send(value)
        while True:
            value = gen.send(value)
    except StopIteration as stop:
        return stop.value


def place_kernel(rects, count, cut, index_ref, *refs):
    pieces, outs = refs[:count], refs[count:]
    for w in range(count - 1):
        @pl.when(pl.program_id(0) == w)
        def _():
            for i, r0, rows, c0, cols, p0, pc in rects:
                if w < count - 2:
                    outs[i][r0 : r0 + rows, c0 : c0 + cols] = pieces[w][p0 : p0 + rows, pc : pc + cols]
                    continue
                for piece, low, high in ((pieces[w], 0, cut), (pieces[w + 1], cut, 1 << 20)):
                    for i2, q0, r, d0, c, s0, sc in clip([(i, r0, rows, c0, cols, p0, pc)], low, high):
                        outs[i][q0 : q0 + r, d0 : d0 + c] = piece[s0 : s0 + r, sc : sc + c]


def place(gathered, sizes):
    pieces, index = gathered
    n = lax.axis_size("dp")
    rows = pieces[0].shape[0]
    rects, width = rects_of(sizes, rows)
    return pl.pallas_call(
        functools.partial(place_kernel, rects, len(pieces), middle_row(rows)),
        grid_spec=pltpu.PrefetchScalarGridSpec(
            num_scalar_prefetch=1,
            grid=(n,),
            in_specs=[pl.BlockSpec(p.shape, lambda i, ref: (0, 0)) for p in pieces],
            out_specs=[pl.BlockSpec(size, lambda i, ref: (ref[i], 0)) for size in sizes],
        ),
        out_shape=[jax.ShapeDtypeStruct((n * r, c), BF) for r, c in sizes],
        compiler_params=pltpu.CompilerParams(vmem_limit_bytes=48 * 2**20),
        cost_estimate=pl.CostEstimate(flops=0, bytes_accessed=4 * n * rows * width, transcendentals=0),
    )(index, *pieces)


def join_kernel(rects, lanes, count, has_extra, index_ref, *refs):
    outs, refs = refs[-len(lanes) :], refs[: -len(lanes)]
    srcs, got = refs[: count * len(lanes)], refs[count * len(lanes) :]
    if has_extra:
        extra, got = got[: len(lanes)], got[len(lanes) :]
    for j, (low, high, adds) in enumerate(lanes):
        for i, r0, rows, c0, cols, p0, pc in clip(rects, low, high):
            value = srcs[j * count + i][r0 : r0 + rows, c0 : c0 + cols]
            if not adds:
                outs[j][p0 : p0 + rows, pc : pc + cols] = value
                continue
            total = value.astype(F32)
            spans = []
            for g, first in adds:
                top, end = first, first + got[g].shape[0]
                spans.append((g, top, end))
            if all(top <= p0 and p0 + rows <= end for _, top, end in spans):
                for g, top, _ in spans:
                    total = total + got[g][p0 - top : p0 - top + rows, pc : pc + cols].astype(F32)
                outs[j][p0 : p0 + rows, pc : pc + cols] = total.astype(BF)
            else:
                outs[j][p0 : p0 + rows, pc : pc + cols] = value
                for g, top, end in spans:
                    a, b = max(top, p0), min(end, p0 + rows)
                    if a < b:
                        sub = total[a - p0 : b - p0] + got[g][a - top : b - top, pc : pc + cols].astype(F32)
                        outs[j][a:b, pc : pc + cols] = sub.astype(BF)
        if has_extra:
            tail = slice(outs[j].shape[1] - extra[j].shape[1], outs[j].shape[1])
            outs[j][:, tail] = (outs[j][:, tail].astype(F32) + extra[j][low:high].astype(F32)).astype(BF)


def join(sources, index, received, lanes, extra=None):
    n = lax.axis_size("dp")
    sizes = [(s.shape[0] // n, s.shape[1]) for s in sources]
    rows = max(r for r, _ in sizes)
    rects, width = rects_of(sizes, rows)
    specs, args = [], []
    for j in range(len(lanes)):
        for s, size in zip(sources, sizes):
            specs.append(pl.BlockSpec(size, functools.partial(lambda j, i, ref: (ref[j], 0), j)))
            args.append(s)
    if extra is not None:
        for j in range(len(lanes)):
            specs.append(pl.BlockSpec((rows, extra.shape[1]), functools.partial(lambda j, i, ref: (ref[j], 0), j)))
            args.append(extra)
    for v in received:
        specs.append(pl.BlockSpec(v.shape, lambda i, ref: (0, 0)))
    heights = [high - low for low, high, _ in lanes]
    return pl.pallas_call(
        functools.partial(join_kernel, rects, lanes, len(sources), extra is not None),
        grid_spec=pltpu.PrefetchScalarGridSpec(
            num_scalar_prefetch=1,
            grid=(1,),
            in_specs=specs,
            out_specs=[pl.BlockSpec((h, width), lambda i, ref: (0, 0)) for h in heights],
        ),
        out_shape=[jax.ShapeDtypeStruct((h, width), BF) for h in heights],
        compiler_params=pltpu.CompilerParams(vmem_limit_bytes=48 * 2**20),
        cost_estimate=pl.CostEstimate(
            flops=0, bytes_accessed=6 * sum(heights) * width, transcendentals=0
        ),
    )(index, *args, *received)


def ring_scatter(sources, extra=None, sent=None):
    n = lax.axis_size("dp")
    half = n // 2
    rows = max(s.shape[0] // n for s in sources)
    cut = middle_row(rows)
    out = join(sources, ring_index([half, half]), [], [(0, cut, []), (cut, rows, [])], extra)
    for k in range(half - 1, -1, -1):
        if sent is not None:
            sent[:] = out
        got = yield (to_right(out[0]), to_left(out[1]))
        first = cut if k == half - 1 else 0
        if k > 0:
            out = join(sources, ring_index([k, -k]), got, [(0, rows, [(0, 0)]), (0, rows, [(1, first)])], extra)
    return join(sources, ring_index([0]), got, [(0, rows, [(0, 0), (1, first)])], extra)[0]


def pack_units_kernel(seq_n, at_ref, gate_ref, up_ref, down_ref, out_ref):
    i = pl.program_id(0)
    n = pl.num_programs(0)
    unit = gate_ref.shape[1]
    rows, wide = out_ref.shape
    mine = wide // 3
    out_ref[:, pl.ds(pl.multiple_of(i * unit, unit), unit)] = gate_ref[...].astype(BF)
    out_ref[:, pl.ds(pl.multiple_of(mine + i * unit, unit), unit)] = up_ref[...].astype(BF)

    @pl.when(i == 0)
    def _():
        rects, _ = rects_of([(rows, mine), (rows, mine), down_ref.shape], rows)
        for _, r0, r, c0, c, p0, pc in rects[2:]:
            out_ref[p0 : p0 + r, pc : pc + c] = down_ref[r0 : r0 + r, c0 : c0 + c].astype(BF)


def pack_units(w_gate, w_up, w_down, at):
    dp_n, seq_n = lax.axis_size("dp"), lax.axis_size("seq")
    shard, ff = w_gate.shape
    unit = ff // (dp_n * seq_n)
    mine = dp_n * unit
    if unit % 128:
        def units(w):
            w = w.reshape(shard, dp_n, seq_n, unit)
            return lax.dynamic_index_in_dim(w, at, 2, keepdims=False).astype(BF).reshape(shard, mine)

        down = lax.dynamic_slice_in_dim(w_down, at * unit, unit, 0).astype(BF)
        rects, _ = rects_of([(shard, mine), (shard, mine), down.shape], shard)
        tops = [down[r0 : r0 + r, c0 : c0 + c] for _, r0, r, c0, c, _, _ in rects[2:]]
        folded = jnp.concatenate([tops[0], jnp.concatenate(tops[1:], 1)], 0)
        return jnp.concatenate([units(w_gate), units(w_up), folded], 1)
    return pl.pallas_call(
        functools.partial(pack_units_kernel, seq_n),
        grid_spec=pltpu.PrefetchScalarGridSpec(
            num_scalar_prefetch=1,
            grid=(dp_n,),
            in_specs=[
                pl.BlockSpec((shard, unit), lambda i, ref: (0, i * seq_n + ref[0])),
                pl.BlockSpec((shard, unit), lambda i, ref: (0, i * seq_n + ref[0])),
                pl.BlockSpec((unit, w_down.shape[1]), lambda i, ref: (ref[0], 0)),
            ],
            out_specs=pl.BlockSpec((shard, 3 * mine), lambda i, ref: (0, 0)),
        ),
        out_shape=jax.ShapeDtypeStruct((shard, 3 * mine), BF),
        compiler_params=pltpu.CompilerParams(vmem_limit_bytes=48 * 2**20),
        cost_estimate=pl.CostEstimate(flops=0, bytes_accessed=6 * 3 * shard * mine, transcendentals=0),
    )(at[None], w_gate, w_up, w_down)


def spread_kernel(seq_n, at_ref, *refs):
    gates, ups = refs[:seq_n], refs[seq_n : 2 * seq_n]
    wg_ref, wu_ref, og_ref, ou_ref, gain_ref = refs[2 * seq_n :]
    unit = gates[0].shape[1]
    total = jnp.zeros((wg_ref.shape[0], unit), F32)
    for m in range(seq_n):
        span = pl.ds(pl.multiple_of((at_ref[0] ^ m) * unit, unit), unit)
        for piece, w, out in ((gates[m], wg_ref, og_ref), (ups[m], wu_ref, ou_ref)):
            value = piece[...].astype(F32)
            out[:, span] = value
            total = total + value * w[:, span].astype(BF).astype(F32)

    @pl.when(pl.program_id(0) == 0)
    def _():
        gain_ref[...] = total

    @pl.when(pl.program_id(0) != 0)
    def _():
        gain_ref[...] += total


def unfold_kernel(seq_n, at_ref, *refs):
    pieces, out = refs[:seq_n], refs[seq_n]
    rows, wide = pieces[0].shape
    rects, _ = rects_of([out.shape], rows)
    for m in range(seq_n):
        @pl.when(pl.program_id(0) == m)
        def _():
            for _, r0, r, c0, c, p0, pc in rects:
                out[r0 : r0 + r, c0 : c0 + c] = pieces[m][p0 : p0 + r, pc : pc + c].astype(F32)


def spread_units(rel, w_gate, w_up, at):
    dp_n, seq_n = lax.axis_size("dp"), lax.axis_size("seq")
    shard, ff = w_gate.shape
    unit = ff // (dp_n * seq_n)
    mine = dp_n * unit
    if unit % 128:
        pieces = in_order(rel, at)

        def spread(start):
            blocks = [g[:, start : start + mine].reshape(shard, dp_n, 1, unit) for g in pieces]
            return jnp.concatenate(blocks, 2).reshape(shard, ff).astype(F32)

        gate, up = spread(0), spread(mine)
        return gate, up, jnp.sum(gate * w_gate.astype(BF).astype(F32) + up * w_up.astype(BF).astype(F32), 1)
    gate, up, sums = pl.pallas_call(
        functools.partial(spread_kernel, seq_n),
        grid_spec=pltpu.PrefetchScalarGridSpec(
            num_scalar_prefetch=1,
            grid=(dp_n,),
            in_specs=[pl.BlockSpec((shard, unit), lambda i, ref: (0, i))] * seq_n
            + [pl.BlockSpec((shard, unit), lambda i, ref: (0, dp_n + i))] * seq_n
            + [pl.BlockSpec((shard, seq_n * unit), lambda i, ref: (0, i))] * 2,
            out_specs=[pl.BlockSpec((shard, seq_n * unit), lambda i, ref: (0, i))] * 2
            + [pl.BlockSpec((shard, unit), lambda i, ref: (0, 0))],
        ),
        out_shape=[jax.ShapeDtypeStruct((shard, ff), F32)] * 2 + [jax.ShapeDtypeStruct((shard, unit), F32)],
        compiler_params=pltpu.CompilerParams(vmem_limit_bytes=60 * 2**20),
        cost_estimate=pl.CostEstimate(flops=0, bytes_accessed=20 * shard * ff, transcendentals=0),
    )(at[None], *rel, *rel, w_gate, w_up)
    return gate, up, jnp.sum(sums, 1)


def unfold_units(rel, w_down, at):
    seq_n = len(rel)
    unit, model = w_down.shape[0] // seq_n, w_down.shape[1]
    shard, mine = rel[0].shape[0], rel[0].shape[1] // 3
    if unit % 128:
        rects, _ = rects_of([(unit, model)], shard)
        downs = []
        for p in in_order(rel, at):
            a, b, c = [p[p0 : p0 + r, 2 * mine + pc : 2 * mine + pc + w] for _, _, r, _, w, p0, pc in rects]
            downs.append(jnp.concatenate([a, jnp.concatenate([b, c], 0)], 1))
        return jnp.concatenate(downs, 0).astype(F32)
    return pl.pallas_call(
        functools.partial(unfold_kernel, seq_n),
        grid_spec=pltpu.PrefetchScalarGridSpec(
            num_scalar_prefetch=1,
            grid=(seq_n,),
            in_specs=[pl.BlockSpec((shard, mine), lambda i, ref: (0, 2))] * seq_n,
            out_specs=pl.BlockSpec((unit, model), lambda i, ref: (i ^ ref[0], 0)),
        ),
        out_shape=jax.ShapeDtypeStruct(w_down.shape, F32),
        compiler_params=pltpu.CompilerParams(vmem_limit_bytes=60 * 2**20),
        cost_estimate=pl.CostEstimate(flops=0, bytes_accessed=6 * w_down.size, transcendentals=0),
    )(at[None], *rel)


def lane_sums(value):
    total = value[:, 0:128]
    for c in range(128, value.shape[1], 128):
        total = total + value[:, c : c + 128]
    return total


def first_columns_kernel(seq_n, at_ref, *refs):
    pieces, (w_ref, out_ref, sum_ref) = refs[:seq_n], refs[seq_n:]
    cols = w_ref.shape[1]
    for m in range(seq_n):
        for h in range(2):
            @pl.when((pl.program_id(0) == m) & (pl.program_id(1) == h))
            def _():
                value = pieces[m][:, h * cols : (h + 1) * cols].astype(F32)
                out_ref[...] = value
                total = lane_sums(value * w_ref[...].astype(BF).astype(F32))
                if m + h == 0:
                    sum_ref[...] = total
                else:
                    sum_ref[...] += total


def spread_first(rel, w_proj, at):
    seq_n = lax.axis_size("seq")
    rows, cols = w_proj.shape[0], w_proj.shape[1] // seq_n // 3

    def block(i, h, ref):
        return (0, (i ^ ref[0]) * 3 + h)

    grad, sums = pl.pallas_call(
        functools.partial(first_columns_kernel, seq_n),
        grid_spec=pltpu.PrefetchScalarGridSpec(
            num_scalar_prefetch=1,
            grid=(seq_n, 2),
            in_specs=[pl.BlockSpec(rel[0].shape, lambda i, h, ref: (0, 0))] * seq_n + [pl.BlockSpec((rows, cols), block)],
            out_specs=[pl.BlockSpec((rows, cols), block), pl.BlockSpec((rows, 128), lambda i, h, ref: (0, 0))],
        ),
        out_shape=[jax.ShapeDtypeStruct(w_proj.shape, F32), jax.ShapeDtypeStruct((rows, 128), F32)],
        compiler_params=pltpu.CompilerParams(vmem_limit_bytes=60 * 2**20),
        cost_estimate=pl.CostEstimate(flops=0, bytes_accessed=7 * w_proj.size, transcendentals=0),
    )(at[None], *rel, w_proj)
    return grad, jnp.sum(sums, 1)


def last_columns_kernel(seq_n, first, at_ref, *refs):
    pieces, (w_ref, _, out_ref, first_ref, sum_ref) = refs[:seq_n], refs[seq_n:]
    cols = w_ref.shape[1]
    for m in range(seq_n):
        @pl.when(pl.program_id(0) == m)
        def _():
            first_ref[...] = pieces[m][:, :first].astype(F32)
            value = pieces[m][:, first : first + cols].astype(F32)
            out_ref[...] = value
            total = lane_sums(value * w_ref[...].astype(BF).astype(F32))
            if m == 0:
                sum_ref[...] = total
            else:
                sum_ref[...] += total


def spread_last(rel, w_proj, first, prior, at):
    seq_n = lax.axis_size("seq")
    rows, cols = w_proj.shape[0], w_proj.shape[1] // seq_n // 3

    def block(i, ref):
        return (0, (i ^ ref[0]) * 3 + 2)

    grad, grad_first, sums = pl.pallas_call(
        functools.partial(last_columns_kernel, seq_n, first),
        grid_spec=pltpu.PrefetchScalarGridSpec(
            num_scalar_prefetch=1,
            grid=(seq_n,),
            in_specs=[pl.BlockSpec(rel[0].shape, lambda i, ref: (0, 0))] * seq_n
            + [pl.BlockSpec((rows, cols), block), pl.BlockSpec(memory_space=pl.ANY)],
            out_specs=[
                pl.BlockSpec((rows, cols), block),
                pl.BlockSpec((rows, first), lambda i, ref: (0, i ^ ref[0])),
                pl.BlockSpec((rows, 128), lambda i, ref: (0, 0)),
            ],
        ),
        out_shape=[
            jax.ShapeDtypeStruct(w_proj.shape, F32),
            jax.ShapeDtypeStruct((rows, seq_n * first), F32),
            jax.ShapeDtypeStruct((rows, 128), F32),
        ],
        input_output_aliases={seq_n + 2: 0},
        compiler_params=pltpu.CompilerParams(vmem_limit_bytes=60 * 2**20),
        cost_estimate=pl.CostEstimate(flops=0, bytes_accessed=5 * w_proj.size, transcendentals=0),
    )(at[None], *rel, w_proj, prior)
    return grad, grad_first, jnp.sum(sums, 1)


def matmul_low(left, right):
    return jnp.dot(left, right, preferred_element_type=F32)


def matmul_tn(left, right):
    return dot_tn(left, right)


def matmul_nt(left, right):
    return dot_nt(left, right)


def inv_rms(values):
    return lax.rsqrt(jnp.mean(values * values, -1, keepdims=True) + NORM_EPS)


def norm_backward(values, scale_inv, gain, grad_norm):
    scaled = grad_norm * gain
    return scale_inv * scaled - values * scale_inv**3 * jnp.mean(scaled * values, -1, keepdims=True)


def after(value, earlier):
    return lax.optimization_barrier((value, earlier))[0]


def swap(value, m):
    n = lax.axis_size("seq")
    return lax.ppermute(value, "seq", [(i, i ^ m) for i in range(n)])


def gather_rel(own):
    far = swap(own, 2)
    return [own, swap(own, 1), far, swap(far, 1)]


def in_order(rel, seq_at):
    odd = seq_at % 2 == 1
    high = seq_at // 2 == 1
    pairs = []
    for a, b in (rel[0:2], rel[2:4]):
        pairs.append((jnp.where(odd, b, a), jnp.where(odd, a, b)))
    (a0, a1), (b0, b1) = pairs
    return [jnp.where(high, b0, a0), jnp.where(high, b1, a1), jnp.where(high, a0, b0), jnp.where(high, a1, b1)]


def piece_spec(shape, i, hold=False):
    more = {"pipeline_mode": pl.Buffered(1)} if hold else {}
    return pl.BlockSpec((1,) + shape[1:], lambda *_: (i,) + (0,) * (len(shape) - 1), **more)


def project_kernel(count, shards, cut, lane, has_prior, at_ref, index_ref, *refs):
    pieces, refs = refs[:count], refs[count:]
    tiles, sides = refs[:shards], refs[shards : 2 * shards]
    norm_ref, join_ref, logit_ref, gains_ref, w_ref, b_ref = refs[2 * shards + (1 if has_prior else 0) :]
    part = pieces[0].shape[1]
    rows = tiles[0].shape[0]
    starts = []
    for k in range(shards):
        which = min(k, shards - 2)
        first = index_ref[which] * rows + (cut if k == shards - 1 else 0)
        starts.append(pl.ds(pl.multiple_of(first, 16), tiles[k].shape[0]))
        w_ref[starts[k], :] = tiles[k][...]

    @pl.when(pl.program_id(0) == 0)
    def _():
        for k in range(shards):
            b_ref[starts[k], :] = sides[k][...]
        i, j = indices(8, 128)
        gains_ref[...] = dot_nt(jnp.where(j == lane + i, 1.0, 0.0).astype(BF), b_ref[...])
        for m in range(count):
            x = pieces[m][0].astype(F32)
            here = pl.ds(pl.multiple_of((at_ref[0] ^ m) * part, part), part)
            norm_ref[0, here, :] = (x * inv_rms(x) * gains_ref[0:1, :]).astype(BF)
        logit_ref[0] = dot_nn(norm_ref[0], b_ref[...]).astype(BF)

    join_ref[0] = dot_nn(norm_ref[0], w_ref[...]).astype(BF)


def project(x_rel, lane, gathered, wide, at, r, prior):
    shards, index = gathered
    count = len(x_rel)
    rows_n, part, model = x_rel[0][0].shape
    length = part * count
    tile = 256

    def whole(shape):
        return pl.BlockSpec(shape, lambda j, *_: (0,) * len(shape))

    args = [at[None], index, *[x for x, _ in x_rel], *shards, *shards]
    aliases = {}
    if prior is not None:
        aliases = {len(args): 0}
        args.append(prior)
    return pl.pallas_call(
        functools.partial(project_kernel, count, len(shards), middle_row(shards[0].shape[0]), lane, prior is not None),
        grid_spec=pltpu.PrefetchScalarGridSpec(
            num_scalar_prefetch=2,
            grid=(wide // tile,),
            in_specs=[piece_spec(x.shape, i, True) for x, i in x_rel]
            + [pl.BlockSpec((s.shape[0], tile), lambda j, *_: (0, j)) for s in shards]
            + [pl.BlockSpec((s.shape[0], 128), lambda j, *_: (0, wide // 128)) for s in shards]
            + [pl.BlockSpec(memory_space=pl.ANY)] * (0 if prior is None else 1),
            out_specs=[
                pl.BlockSpec((1, length, model), lambda j, *_: (r, 0, 0)),
                pl.BlockSpec((1, length, tile), lambda j, *_: (0, 0, j)),
                whole((1, length, 128)),
                whole((8, model)),
            ],
            scratch_shapes=[pltpu.VMEM((model, tile), BF), pltpu.VMEM((model, 128), BF)],
        ),
        out_shape=[
            jax.ShapeDtypeStruct((rows_n, length, model), BF),
            jax.ShapeDtypeStruct((1, length, wide), BF),
            jax.ShapeDtypeStruct((1, length, 128), BF),
            jax.ShapeDtypeStruct((8, model), F32),
        ],
        input_output_aliases=aliases,
        compiler_params=pltpu.CompilerParams(vmem_limit_bytes=56 * 2**20),
        cost_estimate=pl.CostEstimate(
            flops=2 * length * model * wide, bytes_accessed=6 * length * model, transcendentals=0
        ),
    )(*args)


def by_device(total, keep, send, part):
    for m in range(total.shape[0] // part):
        (keep, send)[m % 2][m // 2] = total[m * part : (m + 1) * part].astype(BF)


def feed_kernel(seq_n, tiles, has_prior, *refs):
    two, top = refs[:seq_n], refs[seq_n : 2 * seq_n]
    wg_ref, wu_ref, wd_ref, wg_rows, wu_rows, wd_cols = refs[2 * seq_n : 2 * seq_n + 6]
    refs = refs[2 * seq_n + (9 if has_prior else 6) :]
    hid_ref, gg_ref, gu_ref, keep_b, send_b, keep_f, send_f, two_ref, top_ref, hid, gg, gu = refs
    part = two[0].shape[0]
    j = pl.program_id(0)
    tile = wg_ref.shape[1]

    @pl.when(j == 0)
    def _():
        for m in range(seq_n):
            s = slice(m * part, (m + 1) * part)
            two_ref[s, :] = two[m][...]
            top_ref[s, :] = top[m][0]

    @pl.when(j < tiles)
    def _():
        gate = dot_nn(two_ref[...], wg_ref[...])
        up = dot_nn(two_ref[...], wu_ref[...])
        gh = dot_nt(top_ref[...], wd_ref[...])
        sig = jax.nn.sigmoid(gate)
        act = gate * sig
        here = pl.ds(pl.multiple_of(j * tile, tile), tile)
        for value, out, held in (
            (act * up, hid_ref, hid),
            (gh * up * sig * (1.0 + gate * (1.0 - sig)), gg_ref, gg),
            (gh * act, gu_ref, gu),
        ):
            low = value.astype(BF)
            out[0] = low
            held[:, here] = low

    @pl.when(j >= tiles)
    def _():
        by_device(dot_nt(gg[...], wg_rows[...]) + dot_nt(gu[...], wu_rows[...]), keep_b, send_b, part)
        by_device(dot_nn(hid[...], wd_cols[...]), keep_f, send_f, part)


def feed(two, top, gate_full, up_full, down_full, r, prior):
    seq_n = len(two)
    part, model = two[0].shape
    rows_n = top[0][0].shape[0]
    mine = gate_full.shape[1]
    tile = 256
    tiles = mine // tile
    length = part * seq_n

    def early(j):
        return jnp.minimum(j, tiles - 1)

    def late(j):
        return jnp.maximum(j - tiles, 0)

    piece = pl.BlockSpec((part, model), lambda j: (0, 0), pipeline_mode=pl.Buffered(1))
    columns = pl.BlockSpec((model, tile), lambda j: (0, early(j)))
    lines = pl.BlockSpec((tile, mine), lambda j: (late(j), 0))
    hidden = pl.BlockSpec((1, length, tile), lambda j: (r, 0, early(j)))
    args = [*two, *[g for g, _ in top], gate_full, up_full, down_full, gate_full, up_full, down_full]
    aliases = {}
    if prior is not None:
        aliases = {len(args) + i: i for i in range(3)}
        args += prior
    outs = pl.pallas_call(
        functools.partial(feed_kernel, seq_n, tiles, prior is not None),
        grid=(tiles + model // tile,),
        in_specs=[piece] * seq_n
        + [piece_spec(g.shape, i, True) for g, i in top]
        + [columns, columns, pl.BlockSpec((tile, model), lambda j: (early(j), 0))]
        + [lines, lines, pl.BlockSpec((mine, tile), lambda j: (0, late(j)))]
        + [pl.BlockSpec(memory_space=pl.ANY)] * (3 if prior is not None else 0),
        out_specs=[hidden] * 3 + [pl.BlockSpec((seq_n // 2, part, tile), lambda j: (0, 0, late(j)))] * 4,
        out_shape=[jax.ShapeDtypeStruct((rows_n, length, mine), BF)] * 3
        + [jax.ShapeDtypeStruct((seq_n // 2, part, model), BF)] * 4,
        scratch_shapes=[pltpu.VMEM((length, model), BF)] * 2 + [pltpu.VMEM((length, mine), BF)] * 3,
        input_output_aliases=aliases,
        compiler_params=pltpu.CompilerParams(vmem_limit_bytes=56 * 2**20),
        cost_estimate=pl.CostEstimate(
            flops=12 * length * model * mine, bytes_accessed=12 * length * model + 12 * model * mine, transcendentals=0
        ),
    )(*args)
    return outs[:3], outs[3:]


def outer_kernel(lefts, counts, lanes, *refs):
    left, refs = refs[:lefts], refs[lefts:]
    groups = []
    for n in counts:
        groups.append(refs[:n])
        refs = refs[n:]
    n = len(counts) if lanes is None else len(lanes)
    outs, scratch = refs[:n], list(refs[n:])

    def gather(pieces, into):
        row = 0
        for p in pieces:
            value = p[...] if len(p.shape) == 2 else p[0]
            into[row : row + value.shape[0], :] = value
            row += value.shape[0]

    if lefts > 1:
        tall = scratch.pop(0)
        gather(left, tall)
    else:
        tall = left[0]
    for n, group, out in zip(counts, groups, outs):
        if n > 1:
            whole = scratch.pop(0)

            @pl.when(pl.program_id(0) == 0)
            def _():
                gather(group, whole)
        else:
            whole = group[0]
        if lanes is None:
            out[...] = dot_tn(tall[...], whole[...]).astype(BF)
    if lanes is not None:
        for out, span in zip(outs, lanes):
            out[...] = dot_tn(tall[...], whole[:, slice(*span)]).astype(BF)


def outer(left, rights, lanes=None):
    total = sum(p.shape[0] for p in left)
    model = left[0].shape[1]
    tile = 256
    widths = [(g[0][0] if isinstance(g[0], tuple) else g[0]).shape[-1] for g in rights]
    spans = widths if lanes is None else [high - low for low, high in lanes]
    scratch = [pltpu.VMEM((total, tile), BF)] if len(left) > 1 else []
    scratch += [pltpu.VMEM((total, w), BF) for g, w in zip(rights, widths) if len(g) > 1]
    specs = [pl.BlockSpec((p.shape[0], tile), lambda j: (0, j)) for p in left]
    args = list(left)
    for g in rights:
        for p in g:
            if isinstance(p, tuple):
                specs.append(piece_spec(p[0].shape, p[1], True))
                args.append(p[0])
            else:
                specs.append(pl.BlockSpec(p.shape, lambda j: (0, 0), pipeline_mode=pl.Buffered(1)))
                args.append(p)
    return pl.pallas_call(
        functools.partial(outer_kernel, len(left), [len(g) for g in rights], lanes),
        grid=(model // tile,),
        in_specs=specs,
        out_specs=[pl.BlockSpec((tile, w), lambda j: (j, 0)) for w in spans],
        out_shape=[jax.ShapeDtypeStruct((model, w), BF) for w in spans],
        scratch_shapes=scratch,
        compiler_params=pltpu.CompilerParams(vmem_limit_bytes=56 * 2**20),
        cost_estimate=pl.CostEstimate(
            flops=2 * total * model * sum(widths), bytes_accessed=2 * total * (model + sum(widths)), transcendentals=0
        ),
    )(*args)


def middle_kernel(count, at_ref, *refs):
    parts, weights, (x_ref, gain_ref, mixed, mid, two) = refs[:count], refs[count : 2 * count], refs[2 * count :]
    cols = weights[0].shape[1]
    spans = [pl.ds(pl.multiple_of((at_ref[0] ^ m) * cols, cols), cols) for m in range(count)]
    for m in range(count):
        mixed[:, spans[m]] = parts[m][0]
    for m in range(count):
        mid[:, spans[m]] = x_ref[0, :, spans[m]].astype(F32) + dot_nn(mixed[...], weights[m][...])
    value = mid[...]
    two[...] = (value * inv_rms(value) * gain_ref[...]).astype(BF)


def to_middle(parts, out_rel, x, r, gain, at):
    _, part, model = x.shape
    count = len(out_rel)
    return pl.pallas_call(
        functools.partial(middle_kernel, count),
        grid=(1,),
        in_specs=[pl.BlockSpec(memory_space=pltpu.SMEM)]
        + [piece_spec(p.shape, i) for p, i in parts]
        + [pl.BlockSpec(w.shape, lambda j: (0, 0)) for w in out_rel]
        + [piece_spec(x.shape, r), pl.BlockSpec(gain.shape, lambda j: (0, 0))],
        out_specs=[pl.BlockSpec((part, model), lambda j: (0, 0))] * 3,
        out_shape=[
            jax.ShapeDtypeStruct((part, model), BF),
            jax.ShapeDtypeStruct((part, model), F32),
            jax.ShapeDtypeStruct((part, model), BF),
        ],
        compiler_params=pltpu.CompilerParams(vmem_limit_bytes=48 * 2**20),
        cost_estimate=pl.CostEstimate(flops=2 * part * model * model, bytes_accessed=3 * model * model, transcendentals=0),
    )(at[None], *[p for p, _ in parts], *out_rel, x, gain)


def stacked(refs):
    values = [v[...].astype(F32) for v in refs]
    return values[0] if len(values) == 1 else jnp.concatenate(values, 0)


def second_kernel(count, fars, at_ref, *refs):
    weights, far, refs = refs[:count], refs[count : count + fars], refs[count + fars :]
    own_ref, near_ref, mid_ref, g_ref, gain_ref, grad_ref, low_ref, parts, mixed = refs
    cols = parts.shape[2]
    spans = [pl.ds(pl.multiple_of((at_ref[0] ^ m) * cols, cols), cols) for m in range(count)]
    got = own_ref[0].astype(F32) + near_ref[0].astype(F32) + stacked(far)
    mid = mid_ref[...]
    grad_ref[...] = g_ref[0].astype(F32) + norm_backward(mid, inv_rms(mid), gain_ref[...], got)
    low_ref[...] = grad_ref[...].astype(BF)
    total = dot_nt(low_ref[:, spans[0]], weights[0][...])
    for m in range(1, count):
        total = total + dot_nt(low_ref[:, spans[m]], weights[m][...])
    mixed[...] = total
    for m in range(count):
        parts[m] = mixed[:, spans[m]].astype(BF)


def second_back(keep, near, far, mid, out_grad, r, gain, out_rel, at):
    part, model = mid.shape
    count = len(out_rel)
    cols = out_rel[0].shape[1]

    def whole(v):
        return pl.BlockSpec(v.shape, lambda j: (0, 0))

    return pl.pallas_call(
        functools.partial(second_kernel, count, len(far)),
        grid=(1,),
        in_specs=[pl.BlockSpec(memory_space=pltpu.SMEM)]
        + [whole(w) for w in [*out_rel, *far]]
        + [piece_spec(keep.shape, 0), piece_spec(near.shape, 0), whole(mid)]
        + [piece_spec(out_grad.shape, r), whole(gain)],
        out_specs=[whole(mid), whole(mid), pl.BlockSpec((count, part, cols), lambda j: (0, 0, 0))],
        out_shape=[
            jax.ShapeDtypeStruct((part, model), F32),
            jax.ShapeDtypeStruct((part, model), BF),
            jax.ShapeDtypeStruct((count, part, cols), BF),
        ],
        scratch_shapes=[pltpu.VMEM((part, model), F32)],
        compiler_params=pltpu.CompilerParams(vmem_limit_bytes=48 * 2**20),
        cost_estimate=pl.CostEstimate(flops=2 * part * model * model, bytes_accessed=3 * model * model, transcendentals=0),
    )(at[None], *out_rel, *far, keep, near, mid, out_grad, gain)


def out_kernel(count, rows_n, at_ref, *refs):
    mixed, low, outs = refs[:rows_n], refs[rows_n : 2 * rows_n], refs[2 * rows_n :]
    cols = outs[0].shape[2]
    for m in range(count):
        span = pl.ds(pl.multiple_of((at_ref[0] ^ m) * cols, cols), cols)
        total = dot_tn(mixed[0][...], low[0][:, span])
        for r in range(1, rows_n):
            total = total + dot_tn(mixed[r][...], low[r][:, span])
        outs[m % 2][m // 2] = total.astype(BF)


def grad_out_parts(mixed, low, count, at):
    part, model = mixed[0].shape
    rows_n = len(mixed)
    cols = model // count
    tile = 256
    return pl.pallas_call(
        functools.partial(out_kernel, count, rows_n),
        grid_spec=pltpu.PrefetchScalarGridSpec(
            num_scalar_prefetch=1,
            grid=(model // tile,),
            in_specs=[pl.BlockSpec((part, tile), lambda j, ref: (0, j))] * rows_n
            + [pl.BlockSpec((part, model), lambda j, ref: (0, 0))] * rows_n,
            out_specs=[pl.BlockSpec((count // 2, tile, cols), lambda j, ref: (0, j, 0))] * 2,
        ),
        out_shape=[jax.ShapeDtypeStruct((count // 2, model, cols), BF)] * 2,
        compiler_params=pltpu.CompilerParams(vmem_limit_bytes=48 * 2**20),
        cost_estimate=pl.CostEstimate(flops=4 * part * model * model, bytes_accessed=3 * model * model, transcendentals=0),
    )(at[None], *mixed, *low)


def first_kernel(count, at_ref, grad_ref, w_ref, keep, send, total):
    part = keep.shape[1]
    total[...] = dot_nt(grad_ref[0], w_ref[...])
    for m in range(count):
        here = pl.ds(pl.multiple_of((at_ref[0] ^ m) * part, part), part)
        (keep, send)[m % 2][m // 2] = total[here, :].astype(BF)


def first_parts(grad_joined, w_side, r, count, at):
    _, length, wide = grad_joined.shape
    model = w_side.shape[0]
    part = length // count
    tile = 256
    return pl.pallas_call(
        functools.partial(first_kernel, count),
        grid_spec=pltpu.PrefetchScalarGridSpec(
            num_scalar_prefetch=1,
            grid=(model // tile,),
            in_specs=[
                pl.BlockSpec((1, length, wide), lambda j, ref: (r, 0, 0), pipeline_mode=pl.Buffered(1)),
                pl.BlockSpec((tile, wide), lambda j, ref: (j, 0)),
            ],
            out_specs=[pl.BlockSpec((count // 2, part, tile), lambda j, ref: (0, 0, j))] * 2,
            scratch_shapes=[pltpu.VMEM((length, tile), F32)],
        ),
        out_shape=[jax.ShapeDtypeStruct((count // 2, part, model), BF)] * 2,
        compiler_params=pltpu.CompilerParams(vmem_limit_bytes=48 * 2**20),
        cost_estimate=pl.CostEstimate(
            flops=2 * length * wide * model, bytes_accessed=4 * length * wide, transcendentals=0
        ),
    )(at[None], grad_joined, w_side)


def last_kernel(rows_n, spans, *refs):
    keeps, nears, mids, refs = refs[:rows_n], refs[rows_n : 2 * rows_n], refs[2 * rows_n : 3 * rows_n], refs[3 * rows_n :]
    fars, (x_ref, gain_ref, out_ref) = refs[:-3], refs[-3:]
    for r, (low, high) in enumerate(spans):
        got = keeps[r][0].astype(F32) + nears[r][0].astype(F32) + stacked(fars[low:high])
        x = x_ref[r].astype(F32)
        out_ref[r] = mids[r][...] + norm_backward(x, inv_rms(x), gain_ref[...], got)


def layer_kernel(rows_n, spans, *refs):
    keeps, nears, mids, refs = refs[:rows_n], refs[rows_n : 2 * rows_n], refs[2 * rows_n : 3 * rows_n], refs[3 * rows_n :]
    fars, out_ref = refs[:-1], refs[-1]
    for r, (low, high) in enumerate(spans):
        got = keeps[r][0].astype(F32) + nears[r][0].astype(F32) + stacked(fars[low:high])
        out_ref[r] = (mids[r][...] + got).astype(BF)


def sum_rows(kernel, dtype, keep, near, far, mids, *more):
    rows_n = len(mids)
    shape = (rows_n,) + mids[0].shape
    spans, flat = [], []
    for row in far:
        spans.append((len(flat), len(flat) + len(row)))
        flat += row
    return pl.pallas_call(
        functools.partial(kernel, rows_n, spans),
        grid=(1,),
        in_specs=[piece_spec(v.shape, 0) for v in [*keep, *near]]
        + [pl.BlockSpec(v.shape, lambda j: (0, 0)) for v in mids]
        + [pl.BlockSpec((n, v.shape[1]), functools.partial(lambda i, j: (i, 0), i)) for v, i, n in flat]
        + [pl.BlockSpec(v.shape, functools.partial(lambda n, j: (0,) * n, v.ndim)) for v in more],
        out_specs=pl.BlockSpec(shape, lambda j: (0, 0, 0)),
        out_shape=jax.ShapeDtypeStruct(shape, dtype),
        compiler_params=pltpu.CompilerParams(vmem_limit_bytes=48 * 2**20),
        cost_estimate=pl.CostEstimate(flops=0, bytes_accessed=16 * rows_n * mids[0].size, transcendentals=0),
    )(*keep, *near, *mids, *[v for v, _, _ in flat], *more)


def fold(keep, got, low=0, high=None):
    return (keep[1, low:high].astype(F32) + got[1, low:high].astype(F32)).astype(BF)


def tie(*groups):
    return lax.optimization_barrier(groups)


def per_device(
    inputs,
    doc_ids,
    gain_attn,
    w_proj,
    w_beta,
    conv_taps,
    w_out,
    gain_mlp,
    w_gate,
    w_up,
    w_down,
    out_grad,
):
    rows_n, part, model = inputs.shape
    heads_n = w_beta.shape[1]
    taps_n, width_out = conv_taps.shape
    dp_n, seq_n = lax.axis_size("dp"), lax.axis_size("seq")
    at = lax.axis_index("seq")
    length = part * seq_n
    heads = heads_n // seq_n
    width = model // heads_n
    cols = heads * width
    wide = 4 * cols
    shard = w_proj.shape[0]
    ff = w_gate.shape[1]
    unit = ff // (dp_n * seq_n)
    mine_n = dp_n * unit
    quarter = model // seq_n
    rows = range(rows_n)
    last = rows_n - 1

    proj_mine = lax.dynamic_slice_in_dim(w_proj, at * wide, wide, 1)
    side = jnp.concatenate([w_beta, gain_attn[:, None], gain_mlp[:, None]], 1)
    side = jnp.pad(side.astype(BF), ((0, 0), (0, 126 - heads_n)))
    packed = jnp.concatenate([proj_mine.astype(BF), side], 1)
    sent = []
    ring = ring_gather(packed, sent)
    hop = next(ring)

    flat = jnp.concatenate([doc_ids.astype(BF).reshape(-1), conv_taps.astype(BF).reshape(-1)])
    flat = after(flat, packed)
    flat = [flat, swap(flat, 1), swap(flat, 2), swap(flat, 3)]
    own_x, units = inputs, pack_units(w_gate, w_up, w_down, at)
    hop, flat, own_x, units = tie(hop, flat, own_x, units)
    hop = ring.send(hop)
    flat, own_x, _ = tie(flat, own_x, sent)
    far_x = [swap(own_x[0:1], 2)]
    flat = in_order(flat, at)
    cut = rows_n * part
    doc = jnp.concatenate([t[:cut].reshape(rows_n, part) for t in flat], 1).astype(F32)
    taps_shard = jnp.concatenate([t[cut:].reshape(taps_n, width_out) for t in flat], 1)
    taps_shard = jnp.pad(taps_shard, ((0, 16 - taps_n), (0, quarter - taps_shard.shape[1])))
    out_mine = lax.dynamic_slice_in_dim(w_out, at * quarter, quarter, 1).astype(BF)
    out_mine = lax.all_gather(jnp.concatenate([out_mine, taps_shard], 0), "dp", axis=0)
    hop, far_x, doc = tie(hop, far_x, doc)
    hop = ring.send(hop)
    doc, own_x, far_x, _ = tie(doc, own_x, far_x, sent)
    far_x += [swap(own_x[r : r + 1], 2) for r in rows[1:]]
    skew_x = [swap(far_x[0], 1)]
    near_x = swap(own_x, 1)
    lanes = lax.broadcasted_iota(jnp.int32, (1, 1, 128), 2)
    info = jnp.where(lanes == 0, doc[:, :, None], 0.0)
    for shift_by in range(1, taps_n):
        same = (doc[:, shift_by:] == doc[:, :-shift_by]).astype(F32)
        info = jnp.where(lanes == shift_by, jnp.pad(same, ((0, 0), (shift_by, 0)))[:, :, None], info)
    aux = [info[r : r + 1] for r in rows]
    doc_rows = [jnp.broadcast_to(doc[r : r + 1, None, :], (1, 8, length)) for r in rows]
    hop, far_x, near_x, skew_x, aux, doc_rows = tie(hop, far_x, near_x, skew_x, aux, doc_rows)
    hop = ring.send(hop)
    far_x, _ = tie(far_x, sent)
    skew_x += [swap(far_x[r], 1) for r in rows[1:]]
    hop, skew_x = tie(hop, skew_x)
    proj_shards = drain(ring, hop)
    x_rel = [[(own_x, r), (near_x, r), (far_x[r], 0), (skew_x[r], 0)] for r in rows]

    ring = ring_gather(after(units, proj_shards[0]), sent)
    hop = next(ring)
    own_g, _ = tie(out_grad, sent)
    far_g, near_g = swap(own_g, 2), swap(own_g, 1)
    normed, joined, logit = None, [], []
    for r in rows:
        normed, j, l, gains = project(x_rel[r], heads_n, proj_shards, wide, at, r, normed)
        joined.append(j)
        logit.append(l)
    gain_one, gain_two = gains[0:1], gains[1:2]
    hop, joined, logit, out_mine = tie(hop, joined, logit, out_mine)
    hop = ring.send(hop)
    joined, out_mine, _ = tie(joined, out_mine, sent)
    taps_full = out_mine[:, shard : shard + taps_n, :shard].transpose(1, 0, 2).reshape(taps_n, model)
    taps_mine = lax.dynamic_slice_in_dim(taps_full.astype(F32), at * cols, cols, 1)
    taps_mine = jnp.pad(taps_mine, ((0, 8 - taps_n), (0, 0)))
    out_mine = out_mine[:, :shard].reshape(model, quarter)
    out_far, out_near = swap(out_mine, 2), swap(out_mine, 1)

    def exchange(parts):
        return [(parts, 0)] + [(swap(parts[m : m + 1], m), 0) for m in range(1, seq_n)]

    kept, attn, pair = [], [], []
    for r in rows:
        outs = attend_fwd(joined[r], aux[r], logit[r], doc_rows[r], taps_mine, at, heads, taps_n, seq_n)
        if r == 0:
            outs, hop, joined, out_far, out_near, near_g, far_g = tie(
                outs, hop, joined, out_far, out_near, near_g, far_g
            )
        elif r == last:
            outs, hop, pair, out_skew, skew_g = tie(outs, hop, pair, out_skew, skew_g)
        hop = ring.send(hop)
        mine, joined, pair, _ = tie(outs[0], joined, pair, sent)
        attn.append(mine)
        pair.append(swap(mine[2:], 2))
        if r == 0:
            out_skew, skew_g = swap(out_far, 1), swap(far_g, 1)
        kept.append(outs[1:])
    pair_near = [swap(jnp.stack([attn[0][1], pair[0][1]]), 1)]
    out_rel = [out_mine, out_near, out_far, out_skew]

    def middle_of(r):
        parts = [(attn[r], 0), (pair_near[r], 0), (pair[r], 0), (pair_near[r], 1)]
        return to_middle(parts, out_rel, inputs, r, gain_two, at)

    done = [middle_of(0)]
    done[0], pair[1], hop = tie(done[0], pair[1], hop)
    pair_near.append(swap(jnp.stack([attn[1][1], pair[1][1]]), 1))
    two = done[0][2]
    two_rel = [[two, swap(two, 1), swap(two, 2)]]
    done.append(middle_of(1))
    done[1], two_rel[0][0] = tie(done[1], two_rel[0][0])
    mixed, middle = [v[0] for v in done], [v[1] for v in done]
    two = done[1][2]
    two_rel.append([two, swap(two, 1), swap(two, 2)])
    full = place(drain(ring, hop), [(shard, mine_n), (shard, mine_n), (unit, model)])
    full, two_rel[0] = tie(full, two_rel[0])
    g_rel = [[(own_g, r), (near_g, r), (far_g, r), (skew_g, r)] for r in rows]

    prior, norm, layer = None, [], []
    for r in rows:
        two_rel[r].append(swap(two_rel[r][2], 1))
        if r > 0:
            two_rel[r], near_n = tie(two_rel[r], near_n)
            far_n = [[swap(fold(norm[0][0], near_n[0]), 2)]]
        prior, outs = feed(two_rel[r], g_rel[r], *full, r, prior)
        if r == 0:
            prior, outs, two_rel[1] = tie(prior, outs, two_rel[1])
            near_n = [swap(outs[1], 1)]
        norm.append(outs[:2])
        layer.append(outs[2:])
    hid, g_gate, g_up = [v.reshape(rows_n * length, -1) for v in prior]
    upper, lower = (0, part // 2), (part // 2, part)

    def second(r):
        return second_back(norm[r][0], near_n[r], far_n[r], middle[r], out_grad, r, gain_two, out_rel, at)

    norm[last], layer, hid, far_n = tie(norm[last], layer, hid, far_n)
    near_n.append(swap(norm[last][1], 1))
    done = [second(0)]
    done[0], hid, near_n, layer = tie(done[0], hid, near_n, layer)
    heads_rel = [exchange(done[0][2])]
    far_n.append([fold(norm[last][0], near_n[last], *upper)])
    hid, far_n[last] = tie(hid, far_n[last])
    far_n[last] = [swap(far_n[last][0], 2)]
    near_l = [swap(layer[r][1], 1) for r in rows]
    (grad_down,) = outer([hid], [[g for rel in g_rel for g in rel]])
    grad_down, g_gate, near_l, far_n, heads_got = tie(grad_down, g_gate, near_l, far_n, [p for p, _ in heads_rel[0]])
    heads_rel = [[(p, 0) for p in heads_got]]
    far_n[last].append(fold(norm[last][0], near_n[last], *lower))
    far_l = [fold(layer[0][0], near_l[0], *upper)]
    g_gate, far_n[last][1], far_l = tie(g_gate, far_n[last][1], far_l)
    far_n[last][1] = swap(far_n[last][1], 2)
    far_l = [swap(far_l[0], 2)]
    grad_gate, grad_up = outer([p for rel in two_rel for p in rel], [[g_gate], [g_up]])
    grad_gate, grad_up, far_n, far_l = tie(grad_gate, grad_up, far_n, far_l)
    ring = ring_scatter([grad_gate, grad_up, grad_down], None, sent)
    hop = next(ring)
    far_n, _ = tie(far_n, sent)
    done.append(second(last))
    grad_mid, low = [d[0] for d in done], [d[1] for d in done]
    keep_out, send_out = grad_out_parts(mixed, low, seq_n, at)
    hop, keep_out, send_out, heads_1, grad_mid = tie(hop, keep_out, send_out, done[last][2], grad_mid)
    hop = ring.send(hop)
    far_l.append(jnp.concatenate([fold(layer[0][0], near_l[0], *lower), fold(layer[last][0], near_l[last], *upper)], 0))
    send_out, heads_1, far_l, _ = tie(send_out, heads_1, far_l, sent)
    pair = swap(heads_1[2:], 2)
    near_out = swap(send_out, 1)
    far_l[1] = swap(far_l[1], 2)

    def backward(r, prior):
        return attend_bwd(
            joined[r], aux[r], logit[r], taps_mine, heads_rel[r], kept[r], at, heads, taps_n, r, rows_n, prior
        )

    outs = backward(0, None)
    outs, hop, pair, near_out, far_l = tie(outs, hop, pair, near_out, far_l)
    (proj_full,) = place(proj_shards, [(shard, packed.shape[1])])
    hop = ring.send(hop)
    far_out = fold(keep_out, near_out)
    outs, far_out, pair, _ = tie(outs, far_out, pair, sent)
    pair_near = swap(jnp.stack([heads_1[1], pair[1]]), 1)
    far_out = swap(far_out, 2)
    parts = [first_parts(outs[0], proj_full, 0, seq_n, at)]
    outs, parts, pair_near = tie(outs, parts, pair_near)
    heads_rel.append([(heads_1, 0), (pair_near, 0), (pair, 0), (pair_near, 1)])
    near_in = [swap(parts[0][1], 1)]
    far_l.append(swap(fold(layer[last][0], near_l[last], *lower), 2))
    grad_taps = [outs[1][0]]
    outs = backward(last, outs[0])
    outs, hop, far_out, far_l, near_in = tie(outs, hop, far_out, far_l, near_in)
    hop = ring.send(hop)
    grad_joined = outs[0]
    grad_taps.append(outs[1][0])
    far_in = [fold(parts[0][0], near_in[0])]
    grad_joined, far_in, far_out, _ = tie(grad_joined, far_in, far_out, sent)
    far_in = [swap(far_in[0], 2)]

    grad_out = (keep_out[0].astype(F32) + near_out[0].astype(F32) + far_out.astype(F32)).astype(BF)
    taps_grad = sum(grad_taps)[:, :taps_n].transpose(1, 0, 2).reshape(taps_n, cols)
    taps_grad = lax.dynamic_update_slice_in_dim(jnp.zeros((taps_n, model), F32), taps_grad, at * cols, 1)
    taps_grad = jnp.pad(taps_grad.T.astype(BF), ((0, 0), (heads_n, 128 - heads_n - taps_n)))
    tall, joined_all = normed.reshape(rows_n * length, model), grad_joined.reshape(rows_n * length, -1)
    split = wide // 3 * 2
    grad_one, grad_two = outer([tall], [[joined_all]], [(0, split), (split, joined_all.shape[1])])
    grad_one, grad_two, taps_grad, grad_out, far_in, grad_joined = tie(
        grad_one, grad_two, taps_grad, grad_out, far_in, grad_joined
    )
    more = []
    ring_one = ring_scatter([grad_one], None, sent)
    hop_one = next(ring_one)
    ring_two = ring_scatter([grad_out, grad_two], taps_grad, more)
    hop_two = next(ring_two)
    grad_joined, hop, _, _ = tie(grad_joined, hop, sent, more)
    grad_units = drain(ring, hop)
    grad_joined, grad_units, _, _ = tie(grad_joined, grad_units, sent, more)
    thirds = [i * (shard // 48) * 16 for i in range(3)] + [shard]
    units_cut = [grad_units[lo:hi] for lo, hi in zip(thirds, thirds[1:])]
    units_far = [swap(units_cut[0], 2)]
    parts.append(first_parts(grad_joined, proj_full, last, seq_n, at))
    parts, hop_one, hop_two, units_far, units_cut = tie(parts, hop_one, hop_two, units_far, units_cut)
    hop_one = ring_one.send(hop_one)
    hop_two = ring_two.send(hop_two)
    near_in.append(swap(parts[last][1], 1))
    middle, near_in, units_cut, _, _ = tie(middle, near_in, units_cut, sent, more)
    far_in.append(swap(fold(parts[last][0], near_in[last]), 2))
    half = part // 2
    layer_out = sum_rows(
        layer_kernel,
        BF,
        [v[0] for v in layer],
        near_l,
        [[(far_l[0], 0, half), (far_l[1], 0, half)], [(far_l[1], 1, half), (far_l[2], 0, half)]],
        middle,
    )
    layer_out, hop_one, units_cut = tie(layer_out, hop_one, units_cut)
    hop_one = ring_one.send(hop_one)
    hop_two, units_cut, far_in, _ = tie(hop_two, units_cut, far_in, sent)
    hop_two = ring_two.send(hop_two)
    units_cut, far_in, _ = tie(units_cut, far_in, more)
    units_far.append(swap(units_cut[1], 2))
    grad_in = sum_rows(
        last_kernel, F32, [v[0] for v in parts], near_in, [[(v, 0, part)] for v in far_in], grad_mid, inputs, gain_one
    )
    hop_one, units_far, grad_in, units_cut = tie(hop_one, units_far, grad_in, units_cut)
    grad_one = drain(ring_one, hop_one)
    units_far.append(swap(units_cut[2], 2))
    hop_two, grad_one, units_far = tie(hop_two, grad_one, units_far)
    hop_two = ring_two.send(hop_two)
    far_all = jnp.concatenate(units_far, 0)
    far_all, grad_one, _ = tie(far_all, grad_one, more)
    units_near, units_skew = swap(grad_units, 1), swap(far_all, 1)
    one_far, one_near = swap(grad_one, 2), swap(grad_one, 1)
    units_rel = [grad_units, units_near, far_all, units_skew]
    gate_out, up_out, sums = spread_units(units_rel, w_gate, w_up, at)
    gain_two_out = sums / gain_mlp.astype(BF).astype(F32)
    hop_two, gate_out, up_out, gain_two_out, one_far, one_near = tie(
        hop_two, gate_out, up_out, gain_two_out, one_far, one_near
    )
    grad_two = drain(ring_two, hop_two)
    two_far, two_near = swap(grad_two, 2), swap(grad_two, 1)
    units_rel, one_far, _ = tie(units_rel, one_far, grad_two)
    down_out = unfold_units(units_rel, w_down, at)
    proj_out, sums = spread_first([grad_one, one_near, one_far, swap(one_far, 1)], w_proj, at)
    two_far, two_near, proj_out, down_out = tie(two_far, two_near, proj_out, down_out)
    rel = [grad_two, two_near, two_far, swap(two_far, 1)]
    proj_out, out_out, more_sums = spread_last(rel, w_proj, quarter, proj_out, at)
    sums = sums + more_sums
    tail = [t[:, -128:].astype(F32) for t in rel]
    tail = (tail[0] + tail[1]) + (tail[2] + tail[3])
    beta_out = tail[:, :heads_n]
    sums = sums + jnp.sum(beta_out * w_beta.astype(BF).astype(F32), 1)
    gain_one_out = sums / gain_attn.astype(BF).astype(F32)
    taps_out = lax.dynamic_slice_in_dim(tail[:, heads_n : heads_n + taps_n], at * width_out, width_out, 0).T
    return (
        layer_out,
        grad_in,
        gain_one_out,
        proj_out,
        beta_out,
        taps_out,
        out_out,
        gain_two_out,
        gate_out,
        up_out,
        down_out,
    )


def solution(mesh):
    in_specs = (
        P("dp", "seq", None),
        P("dp", "seq"),
        P("dp"),
        P("dp", None),
        P("dp", None),
        P(None, ("dp", "seq")),
        P("dp", None),
        P("dp"),
        P("dp", None),
        P("dp", None),
        P("dp", None),
        P("dp", "seq", None),
    )
    out_specs = (
        P("dp", "seq", None),
        P("dp", "seq", None),
        P("dp"),
        P("dp", None),
        P("dp", None),
        P(None, ("dp", "seq")),
        P("dp", None),
        P("dp"),
        P("dp", None),
        P("dp", None),
        P("dp", None),
    )
    return jax.shard_map(per_device, mesh=mesh, in_specs=in_specs, out_specs=out_specs, check_vma=False)
```

```python
import functools
import jax
import jax.numpy as jnp
from jax import lax
from jax.experimental import pallas as pl
from jax.experimental.pallas import tpu as pltpu
from jax.sharding import PartitionSpec as P

F32 = jnp.float32
BF = jnp.bfloat16
NORM_EPS = 1e-06
BLOCK = 256
HALF = 128


def dot_nn(a, b):
    return lax.dot_general(a, b, (((1,), (0,)), ((), ())), preferred_element_type=F32)


def dot_nt(a, b):
    return lax.dot_general(a, b, (((1,), (1,)), ((), ())), preferred_element_type=F32)


def dot_tn(a, b):
    return lax.dot_general(a, b, (((0,), (0,)), ((), ())), preferred_element_type=F32)


def mul(a, b):
    return dot_nn(a.astype(BF), b.astype(BF))


def indices(rows, cols):
    return (
        lax.broadcasted_iota(jnp.int32, (rows, cols), 0),
        lax.broadcasted_iota(jnp.int32, (rows, cols), 1),
    )


def unit_inverse(systems, fill=()):
    size = systems[0].shape[0]
    row, col = indices(size, size)
    eye = jnp.where(row == col, 1.0, 0.0).astype(F32)
    near = (row - col == 1) & (row % 2 == 1)
    solved = [eye - jnp.where(near, g, 0.0) for g in systems]
    span = 2
    fill = list(fill)
    share = -(-len(fill) // 6)
    while span < size:
        for _ in range(share):
            if fill:
                fill.pop(0)()
        corner = (row // (2 * span) == col // (2 * span)) & (row % (2 * span) >= span) & (col % (2 * span) < span)
        below = [jnp.where(corner, g, 0.0) for g in systems]
        step = [mul(n, c) for n, c in zip(solved, below)]
        solved = [n - mul(s, n) for n, s in zip(solved, step)]
        span *= 2
    for more in fill:
        more()
    return solved


def block_inverse(g, fill=()):
    h = HALF
    parts = unit_inverse([p for b in g for p in (b[:h, :h], b[h:, h:])], fill)
    out = []
    for i, b in enumerate(g):
        top, bottom = parts[2 * i], parts[2 * i + 1]
        corner = -mul(mul(bottom, b[h:, :h]), top)
        upper = jnp.concatenate([top, jnp.zeros((h, h), F32)], 1)
        lower = jnp.concatenate([corner, bottom], 1)
        out.append(jnp.concatenate([upper, lower], 0))
    return out


def house(u, taps_ref, aux, taps_n):
    mixed = taps_ref[0:1, :] * u
    for s in range(1, taps_n):
        mixed = mixed + (taps_ref[s : s + 1, :] * aux[:, s : s + 1]) * pltpu.roll(u, s, 0)
    inv = lax.rsqrt(jnp.sum(mixed * mixed, -1, keepdims=True) + NORM_EPS)
    return mixed * inv, inv


def lane_pick(aux, lane):
    pos = lax.broadcasted_iota(jnp.int32, aux.shape, 1)
    return jnp.sum(jnp.where(pos == lane, aux, 0.0), 1, keepdims=True)


def fwd_kernel(taps_n, at_ref, join_ref, aux_ref, logit_ref, doc_ref, taps_ref, *rest):
    length = join_ref.shape[1]
    out_ref, rest = rest[0], rest[1:]
    part = out_ref.shape[1]
    (p_refs, x_ref, n_ref, m_ref, z_ref, qt_ref, w_ref, kt_ref, e_ref, run) = (rest[:-9],) + rest[-9:]
    d = taps_ref.shape[1]
    nb = length // BLOCK
    lane = at_ref[0] * pl.num_programs(1) + pl.program_id(1)
    aux = aux_ref[0]
    beta_all = 2.0 * jax.nn.sigmoid(lane_pick(logit_ref[0].astype(F32), lane))
    u = join_ref[0, :, 3 * d : 4 * d].astype(F32)
    w_all, _ = house(u, taps_ref, aux, taps_n)
    w_ref[0] = w_all.astype(BF)
    row, col = indices(BLOCK, BLOCK)
    later = row > col
    notbefore = row >= col
    scale = d ** -0.5
    sl = [slice(b * BLOCK, (b + 1) * BLOCK) for b in range(nb)]
    w = [w_ref[0, s, :] for s in sl]
    beta = [beta_all[s] for s in sl]
    k = [join_ref[0, s, d : 2 * d] for s in sl]
    q = [join_ref[0, s, 0:d] for s in sl]
    g = [jnp.where(later, beta[b] * dot_nt(w[b], w[b]), 0.0) for b in range(nb)]
    side_products = [[None] * nb for _ in range(3)]

    def make(i, b):
        def run_one():
            if i == 0:
                side_products[0][b] = jnp.where(later, beta[b] * dot_nt(w[b], k[b]), 0.0).astype(BF)
            elif i == 1:
                m_ref[0, b] = jnp.where(notbefore, dot_nt(q[b], w[b]), 0.0).astype(BF)
            else:
                side_products[2][b] = dot_nt(q[b], k[b])

        return run_one

    inv = block_inverse(g, [make(i, b) for i in range(3) for b in range(nb)])
    for b in range(nb):
        nn = inv[b].astype(BF)
        n_ref[0, b] = nn
        r = side_products[0][b]
        z = dot_nn(nn, (beta[b] * w_all[sl[b]]).astype(BF)).astype(BF)
        z_ref[0, sl[b], :] = z
        x = dot_nn(nn, r).astype(BF)
        x_ref[0, b] = x
        m = m_ref[0, b]
        diag = side_products[2][b] - dot_nn(m, x)
        kb = k[b].astype(F32) - dot_tn(x, w[b])
        allowed = notbefore & (aux[sl[b], 0:1] == doc_ref[0, 0:1, sl[b]])
        diag = jnp.where(allowed, diag * scale, -1e30)
        if b > 0:
            start = b * BLOCK
            qt = (q[b].astype(F32) - dot_nn(m, z)).astype(BF)
            qt_ref[0, sl[b], :] = qt
            off = start * (b - 1) // 2
            kt = run[0:start, :].astype(BF)
            kt_ref[0, off : off + start, :] = kt
            side = dot_nt(qt, kt)
            ok = aux[sl[b], 0:1] == doc_ref[0, 0:1, 0:start]
            side = jnp.where(ok, side * scale, -1e30)
            peak = jnp.maximum(jnp.max(diag, 1, keepdims=True), jnp.max(side, 1, keepdims=True))
            ps = jnp.exp(side - peak)
            pd = jnp.exp(diag - peak)
            inv_total = 1.0 / (jnp.sum(ps, 1, keepdims=True) + jnp.sum(pd, 1, keepdims=True))
            ps = (ps * inv_total).astype(BF)
            pd = (pd * inv_total).astype(BF)
            p_refs[b][0, :, 0:start] = ps
            p_refs[b][0, :, start : start + BLOCK] = pd
            o = dot_nn(ps, join_ref[0, 0:start, 2 * d : 3 * d]) + dot_nn(pd, join_ref[0, sl[b], 2 * d : 3 * d])
        else:
            qt_ref[0, sl[b], :] = jnp.zeros((BLOCK, d), BF)
            peak = jnp.max(diag, 1, keepdims=True)
            pd = jnp.exp(diag - peak)
            pd = (pd / jnp.sum(pd, 1, keepdims=True)).astype(BF)
            p_refs[b][0] = pd
            o = dot_nn(pd, join_ref[0, sl[b], 2 * d : 3 * d])
        if part % BLOCK == 0:
            out_ref[(b * BLOCK // part) ^ at_ref[0], b * BLOCK % part : b * BLOCK % part + BLOCK, :] = o.astype(BF)
        else:
            for c in range(BLOCK // part):
                out_ref[(b * BLOCK // part + c) ^ at_ref[0]] = o[c * part : (c + 1) * part].astype(BF)
        if b < nb - 1:
            e = dot_tn(w[b], z).astype(BF)
            e_ref[0, b] = e
            if b > 0:
                run[0:start, :] = run[0:start, :] - dot_nt(kt, e)
            run[sl[b], :] = kb
        else:
            e_ref[0, b] = jnp.zeros((d, d), BF)


def bwd_kernel(taps_n, seq_n, has_prior, at_ref, join_ref, aux_ref, logit_ref, taps_ref, *rest):
    nb = join_ref.shape[1] // BLOCK
    go_parts, rest = rest[:seq_n], rest[seq_n:]
    if has_prior:
        rest = rest[: nb + 8] + rest[nb + 9 :]
    p_refs = rest[:nb]
    (x_ref, n_ref, m_ref, z_ref, qt_ref, w_ref, kt_ref, e_ref, gj_ref, gt_ref, gk, gv, gw, go_ref) = rest[nb:]
    part = go_parts[0].shape[1]
    for m in range(seq_n):
        go_ref[pl.ds(pl.multiple_of((at_ref[0] ^ m) * part, part), part), :] = go_parts[m][0]
    length = join_ref.shape[1]
    d = taps_ref.shape[1]
    head = pl.program_id(1)
    lane = at_ref[0] * pl.num_programs(1) + head
    aux = aux_ref[0]
    beta_all = 2.0 * jax.nn.sigmoid(lane_pick(logit_ref[0].astype(F32), lane))
    row, col = indices(BLOCK, BLOCK)
    later = row > col
    notbefore = row >= col
    scale = d ** -0.5
    gbeta = [None] * nb

    def span(i):
        return pl.ds(pl.multiple_of((4 * head + i) * d, d), d)

    for b in reversed(range(nb)):
        start, end = b * BLOCK, (b + 1) * BLOCK
        s = slice(start, end)
        last = b == nb - 1
        w, q, k = w_ref[0, s, :], join_ref[0, s, 0:d], join_ref[0, s, d : 2 * d]
        beta = beta_all[s]
        x, n, m, z = x_ref[0, b], n_ref[0, b], m_ref[0, b], z_ref[0, s, :]
        go = go_ref[s, :]
        p = p_refs[b][0]
        gp = dot_nt(go, join_ref[0, 0:end, 2 * d : 3 * d])
        pf = p.astype(F32)
        inner = jnp.sum(pf * gp, 1, keepdims=True)
        gs = (pf * (gp - inner) * scale).astype(BF)
        gv_new = dot_tn(p, go)
        gsd = gs[:, start:end]
        if last:
            gv[...] = gv_new
        else:
            gv[0:end, :] += gv_new
        stack_m = [gsd]
        if b > 0:
            off = start * (b - 1) // 2
            kt, qt = kt_ref[0, off : off + start, :], qt_ref[0, s, :]
            gside = gs[:, 0:start]
            gqt_f = dot_nn(gside, kt)
            gqt = gqt_f.astype(BF)
            fresh = dot_tn(gside, qt)
        if not last:
            gkt_f = gk[s, :]
            gkt = gkt_f.astype(BF)
        if b > 0 and not last:
            e = e_ref[0, b]
            old = gk[0:start, :]
            old_b = old.astype(BF)
            ge = (-dot_tn(old_b, kt)).astype(BF)
            gk[0:start, :] = old - dot_nn(old_b, e) + fresh
        elif b > 0:
            gk[0:start, :] = fresh
        has_z = b > 0
        xz = jnp.concatenate([x, z], 1) if has_z else x
        g_xz = jnp.concatenate([gsd, gqt], 1) if has_z else gsd
        mt = dot_tn(m, g_xz)
        gm = jnp.where(notbefore, -dot_nt(g_xz, xz), 0.0).astype(BF)
        gx = -mt[:, :BLOCK]
        if not last:
            gx = gx - dot_nt(w, gkt)
        gx = jnp.where(later, gx, 0.0).astype(BF)
        if has_z:
            gz = -mt[:, BLOCK:]
            if not last:
                gz = gz + dot_nn(w, ge)
            y = dot_tn(n, jnp.concatenate([gx, gz.astype(BF)], 1))
            y_z = y[:, BLOCK:]
        else:
            y = dot_tn(n, gx)
        gg = jnp.where(later, -dot_nt(y.astype(BF), xz), 0.0)
        y_x = jnp.where(later, y[:, :BLOCK], 0.0)
        wk = jnp.concatenate([w, k], 0)
        ww_wk = dot_nt(w, wk)
        gbv = jnp.sum(y_x * ww_wk[:, BLOCK:] + gg * ww_wk[:, :BLOCK], 1, keepdims=True)
        by = (beta * y_x).astype(BF)
        bg = (beta * gg).astype(BF)
        qw = jnp.concatenate([q, w], 0)
        gw_b = dot_tn(jnp.concatenate([gm, bg], 0), qw)
        if last:
            gw_b = gw_b + dot_nn(jnp.concatenate([bg, by], 1), wk)
        else:
            gw_b = gw_b + dot_nn(jnp.concatenate([bg, by, x], 1), jnp.concatenate([wk, -gkt], 0))
        gq_b = dot_nn(jnp.concatenate([gm, gsd], 1), wk)
        gk_b = dot_tn(jnp.concatenate([gsd, by], 0), qw)
        if has_z:
            gq_b = gq_b + gqt_f
            gw_b = gw_b + beta * y_z
            gbv = gbv + jnp.sum(y_z * w.astype(F32), 1, keepdims=True)
        if not last:
            gk_b = gk_b + gkt_f
            if has_z:
                gw_b = gw_b + dot_nt(z, ge)
        gbeta[b] = gbv
        gw[s, :] = gw_b
        gj_ref[0, s, span(0)] = gq_b.astype(BF)
        gj_ref[0, s, span(1)] = gk_b.astype(BF)
    gj_ref[0, :, span(2)] = gv[...].astype(BF)
    u = join_ref[0, :, 3 * d : 4 * d].astype(F32)
    w_all, inv = house(u, taps_ref, aux, taps_n)
    gw_all = gw[...]
    gc = inv * (gw_all - w_all * jnp.sum(gw_all * w_all, 1, keepdims=True))
    gu = taps_ref[0:1, :] * gc
    gt = [jnp.sum(gc * u, 0, keepdims=True)]
    for s in range(1, taps_n):
        held = gc * aux[:, s : s + 1]
        gt.append(jnp.sum(held * pltpu.roll(u, s, 0), 0, keepdims=True))
        gu = gu + taps_ref[s : s + 1, :] * pltpu.roll(held, length - s, 0)
    gj_ref[0, :, span(3)] = gu.astype(BF)
    gt.append(jnp.zeros((8 - taps_n, d), F32))
    gt_ref[0, 0] = jnp.concatenate(gt, 0)
    gb_all = jnp.concatenate(gbeta, 0) * beta_all * (1.0 - 0.5 * beta_all)
    pos = lax.broadcasted_iota(jnp.int32, aux.shape, 1)
    mine = jnp.where(pos == lane, gb_all, 0.0).astype(BF)
    tail = slice(gj_ref.shape[2] - 128, gj_ref.shape[2])

    @pl.when(head == 0)
    def _():
        gj_ref[0, :, tail] = mine

    @pl.when(head != 0)
    def _():
        gj_ref[0, :, tail] += mine


def res_specs(length, d, heads):
    nb = length // BLOCK
    shapes = [(BLOCK, (b + 1) * BLOCK) for b in range(nb)]
    shapes += [(nb, BLOCK, BLOCK)] * 3 + [(length, d)] * 3
    shapes += [(max(1, nb * (nb - 1) // 2) * BLOCK, d), (nb, d, d)]
    specs = [
        pl.BlockSpec((1,) + s, functools.partial(lambda n, r, h: (r * heads + h,) + (0,) * n, len(s))) for s in shapes
    ]
    return shapes, specs


def attend_fwd(joined, aux, logit, doc_rows, taps, at, heads, taps_n, seq_n):
    rows, length, packed = joined.shape
    d = taps.shape[1] // heads
    shapes, specs = res_specs(length, d, heads)
    return pl.pallas_call(
        functools.partial(fwd_kernel, taps_n),
        grid=(rows, heads),
        in_specs=[
            pl.BlockSpec(memory_space=pltpu.SMEM),
            pl.BlockSpec((1, length, 4 * d), lambda r, h: (r, 0, h)),
            pl.BlockSpec((1, length, 128), lambda r, h: (r, 0, 0)),
            pl.BlockSpec((1, length, 128), lambda r, h: (r, 0, 0)),
            pl.BlockSpec((1, 8, length), lambda r, h: (r, 0, 0)),
            pl.BlockSpec((8, d), lambda r, h: (0, h)),
        ],
        out_specs=[pl.BlockSpec((seq_n, length // seq_n, d), lambda r, h: (0, 0, h))] + specs,
        out_shape=[jax.ShapeDtypeStruct((seq_n, length // seq_n, heads * d), BF)]
        + [jax.ShapeDtypeStruct((rows * heads,) + s, BF) for s in shapes],
        scratch_shapes=[pltpu.VMEM((length, d), F32)],
        compiler_params=pltpu.CompilerParams(vmem_limit_bytes=56 * 2**20),
        cost_estimate=pl.CostEstimate(
            flops=rows * heads * 8 * 10**9, bytes_accessed=rows * heads * 5 * 10**6, transcendentals=0
        ),
    )(at[None], joined, aux, logit, doc_rows, taps)


def attend_bwd(joined, aux, logit, taps, grad_parts, res, at, heads, taps_n, row, rows_n, prior):
    rows, length, packed = joined.shape
    d = taps.shape[1] // heads
    shapes, specs = res_specs(length, d, heads)
    wide = heads * 4 * d + 128
    seq_n = len(grad_parts)
    args = [at[None], joined, aux, logit, taps, *[p for p, _ in grad_parts], *res]
    aliases = {}
    if prior is not None:
        aliases = {len(args): 0}
        args.append(prior)
    return pl.pallas_call(
        functools.partial(bwd_kernel, taps_n, seq_n, prior is not None),
        grid=(rows, heads),
        in_specs=[
            pl.BlockSpec(memory_space=pltpu.SMEM),
            pl.BlockSpec((1, length, 4 * d), lambda r, h: (r, 0, h)),
            pl.BlockSpec((1, length, 128), lambda r, h: (r, 0, 0)),
            pl.BlockSpec((1, length, 128), lambda r, h: (r, 0, 0)),
            pl.BlockSpec((8, d), lambda r, h: (0, h)),
        ]
        + [
            pl.BlockSpec((1, length // seq_n, d), functools.partial(lambda i, r, h: (i, 0, h), i)) for _, i in grad_parts
        ]
        + specs
        + [pl.BlockSpec(memory_space=pl.ANY)] * (0 if prior is None else 1),
        out_specs=[
            pl.BlockSpec((1, length, wide), lambda r, h: (row, 0, 0)),
            pl.BlockSpec((1, 1, 8, d), lambda r, h: (r, h, 0, 0)),
        ],
        out_shape=[
            jax.ShapeDtypeStruct((rows_n, length, wide), BF),
            jax.ShapeDtypeStruct((rows, heads, 8, d), F32),
        ],
        scratch_shapes=[pltpu.VMEM((length, d), F32)] * 3 + [pltpu.VMEM((length, d), BF)],
        input_output_aliases=aliases,
        compiler_params=pltpu.CompilerParams(vmem_limit_bytes=56 * 2**20),
        cost_estimate=pl.CostEstimate(
            flops=rows * heads * 16 * 10**9, bytes_accessed=rows * heads * 6 * 10**6, transcendentals=0
        ),
    )(*args)


def rects_of(sizes, rows):
    rects, at = [], 0
    for i, (r, c) in enumerate(sizes):
        if r == rows:
            rects.append((i, 0, r, 0, c, 0, at))
            at += c
        else:
            wide, rest = r * c // rows, rows - r
            rects.append((i, 0, r, 0, wide, 0, at))
            rects.append((i, 0, rest, wide, wide // 2, r, at))
            rects.append((i, rest, rest, wide, wide // 2, r, at + wide // 2))
            at += wide
    return rects, at


def clip(rects, low, high):
    out = []
    for i, r0, rows, c0, cols, p0, pc in rects:
        a, b = max(p0, low), min(p0 + rows, high)
        if a < b:
            out.append((i, r0 + a - p0, b - a, c0, cols, a - low, pc))
    return out


def ring_order(n):
    return list(range(0, n, 2)) + list(range(n - 1, 0, -2))


def ring_index(steps):
    n = lax.axis_size("dp")
    me = lax.axis_index("dp")
    place = jnp.where(me % 2 == 0, me // 2, n - 1 - me // 2)
    there = (place + jnp.array([(k + n) % n for k in steps], jnp.int32)) % n
    return jnp.where(there < n // 2, 2 * there, 2 * (n - 1 - there) + 1)


def to_right(value):
    order = ring_order(lax.axis_size("dp"))
    return lax.ppermute(value, "dp", [(a, b) for a, b in zip(order, order[1:] + order[:1])])


def to_left(value):
    order = ring_order(lax.axis_size("dp"))
    return lax.ppermute(value, "dp", [(b, a) for a, b in zip(order, order[1:] + order[:1])])


def middle_row(rows):
    return (rows // 2 + 15) // 16 * 16


def ring_gather(own, sent=None):
    n = lax.axis_size("dp")
    cut = middle_row(own.shape[0])
    pieces, steps = [own], [0]
    pair = (own, own)
    for k in range(1, n // 2 + 1):
        if k == n // 2:
            pair = (pair[0][:cut], pair[1][cut:])
        if sent is not None:
            sent[:] = pair
        pair = yield (to_right(pair[0]), to_left(pair[1]))
        pieces += list(pair)
        steps += [-k, k] if k < n // 2 else [k]
    return pieces, ring_index(steps)


def drain(gen, value=None):
    try:
        value = next(gen) if value is None else gen.send(value)
        while True:
            value = gen.send(value)
    except StopIteration as stop:
        return stop.value


def place_kernel(rects, count, cut, index_ref, *refs):
    pieces, outs = refs[:count], refs[count:]
    for w in range(count - 1):
        @pl.when(pl.program_id(0) == w)
        def _():
            for i, r0, rows, c0, cols, p0, pc in rects:
                if w < count - 2:
                    outs[i][r0 : r0 + rows, c0 : c0 + cols] = pieces[w][p0 : p0 + rows, pc : pc + cols]
                    continue
                for piece, low, high in ((pieces[w], 0, cut), (pieces[w + 1], cut, 1 << 20)):
                    for i2, q0, r, d0, c, s0, sc in clip([(i, r0, rows, c0, cols, p0, pc)], low, high):
                        outs[i][q0 : q0 + r, d0 : d0 + c] = piece[s0 : s0 + r, sc : sc + c]


def place(gathered, sizes):
    pieces, index = gathered
    n = lax.axis_size("dp")
    rows = pieces[0].shape[0]
    rects, width = rects_of(sizes, rows)
    return pl.pallas_call(
        functools.partial(place_kernel, rects, len(pieces), middle_row(rows)),
        grid_spec=pltpu.PrefetchScalarGridSpec(
            num_scalar_prefetch=1,
            grid=(n,),
            in_specs=[pl.BlockSpec(p.shape, lambda i, ref: (0, 0)) for p in pieces],
            out_specs=[pl.BlockSpec(size, lambda i, ref: (ref[i], 0)) for size in sizes],
        ),
        out_shape=[jax.ShapeDtypeStruct((n * r, c), BF) for r, c in sizes],
        compiler_params=pltpu.CompilerParams(vmem_limit_bytes=48 * 2**20),
        cost_estimate=pl.CostEstimate(flops=0, bytes_accessed=4 * n * rows * width, transcendentals=0),
    )(index, *pieces)


def join_kernel(rects, lanes, count, has_extra, index_ref, *refs):
    outs, refs = refs[-len(lanes) :], refs[: -len(lanes)]
    srcs, got = refs[: count * len(lanes)], refs[count * len(lanes) :]
    if has_extra:
        extra, got = got[: len(lanes)], got[len(lanes) :]
    for j, (low, high, adds) in enumerate(lanes):
        for i, r0, rows, c0, cols, p0, pc in clip(rects, low, high):
            value = srcs[j * count + i][r0 : r0 + rows, c0 : c0 + cols]
            if not adds:
                outs[j][p0 : p0 + rows, pc : pc + cols] = value
                continue
            total = value.astype(F32)
            spans = []
            for g, first in adds:
                top, end = first, first + got[g].shape[0]
                spans.append((g, top, end))
            if all(top <= p0 and p0 + rows <= end for _, top, end in spans):
                for g, top, _ in spans:
                    total = total + got[g][p0 - top : p0 - top + rows, pc : pc + cols].astype(F32)
                outs[j][p0 : p0 + rows, pc : pc + cols] = total.astype(BF)
            else:
                outs[j][p0 : p0 + rows, pc : pc + cols] = value
                for g, top, end in spans:
                    a, b = max(top, p0), min(end, p0 + rows)
                    if a < b:
                        sub = total[a - p0 : b - p0] + got[g][a - top : b - top, pc : pc + cols].astype(F32)
                        outs[j][a:b, pc : pc + cols] = sub.astype(BF)
        if has_extra:
            tail = slice(outs[j].shape[1] - extra[j].shape[1], outs[j].shape[1])
            outs[j][:, tail] = (outs[j][:, tail].astype(F32) + extra[j][low:high].astype(F32)).astype(BF)


def join(sources, index, received, lanes, extra=None):
    n = lax.axis_size("dp")
    sizes = [(s.shape[0] // n, s.shape[1]) for s in sources]
    rows = max(r for r, _ in sizes)
    rects, width = rects_of(sizes, rows)
    specs, args = [], []
    for j in range(len(lanes)):
        for s, size in zip(sources, sizes):
            specs.append(pl.BlockSpec(size, functools.partial(lambda j, i, ref: (ref[j], 0), j)))
            args.append(s)
    if extra is not None:
        for j in range(len(lanes)):
            specs.append(pl.BlockSpec((rows, extra.shape[1]), functools.partial(lambda j, i, ref: (ref[j], 0), j)))
            args.append(extra)
    for v in received:
        specs.append(pl.BlockSpec(v.shape, lambda i, ref: (0, 0)))
    heights = [high - low for low, high, _ in lanes]
    return pl.pallas_call(
        functools.partial(join_kernel, rects, lanes, len(sources), extra is not None),
        grid_spec=pltpu.PrefetchScalarGridSpec(
            num_scalar_prefetch=1,
            grid=(1,),
            in_specs=specs,
            out_specs=[pl.BlockSpec((h, width), lambda i, ref: (0, 0)) for h in heights],
        ),
        out_shape=[jax.ShapeDtypeStruct((h, width), BF) for h in heights],
        compiler_params=pltpu.CompilerParams(vmem_limit_bytes=48 * 2**20),
        cost_estimate=pl.CostEstimate(
            flops=0, bytes_accessed=6 * sum(heights) * width, transcendentals=0
        ),
    )(index, *args, *received)


def ring_scatter(sources, extra=None, sent=None):
    n = lax.axis_size("dp")
    half = n // 2
    rows = max(s.shape[0] // n for s in sources)
    cut = middle_row(rows)
    out = join(sources, ring_index([half, half]), [], [(0, cut, []), (cut, rows, [])], extra)
    for k in range(half - 1, -1, -1):
        if sent is not None:
            sent[:] = out
        got = yield (to_right(out[0]), to_left(out[1]))
        first = cut if k == half - 1 else 0
        if k > 0:
            out = join(sources, ring_index([k, -k]), got, [(0, rows, [(0, 0)]), (0, rows, [(1, first)])], extra)
    return join(sources, ring_index([0]), got, [(0, rows, [(0, 0), (1, first)])], extra)[0]


def pack_units_kernel(seq_n, at_ref, gate_ref, up_ref, down_ref, out_ref):
    i = pl.program_id(0)
    n = pl.num_programs(0)
    unit = gate_ref.shape[1]
    rows, wide = out_ref.shape
    mine = wide // 3
    out_ref[:, pl.ds(pl.multiple_of(i * unit, unit), unit)] = gate_ref[...].astype(BF)
    out_ref[:, pl.ds(pl.multiple_of(mine + i * unit, unit), unit)] = up_ref[...].astype(BF)

    @pl.when(i == 0)
    def _():
        rects, _ = rects_of([(rows, mine), (rows, mine), down_ref.shape], rows)
        for _, r0, r, c0, c, p0, pc in rects[2:]:
            out_ref[p0 : p0 + r, pc : pc + c] = down_ref[r0 : r0 + r, c0 : c0 + c].astype(BF)


def pack_units(w_gate, w_up, w_down, at):
    dp_n, seq_n = lax.axis_size("dp"), lax.axis_size("seq")
    shard, ff = w_gate.shape
    unit = ff // (dp_n * seq_n)
    mine = dp_n * unit
    if unit % 128:
        def units(w):
            w = w.reshape(shard, dp_n, seq_n, unit)
            return lax.dynamic_index_in_dim(w, at, 2, keepdims=False).astype(BF).reshape(shard, mine)

        down = lax.dynamic_slice_in_dim(w_down, at * unit, unit, 0).astype(BF)
        rects, _ = rects_of([(shard, mine), (shard, mine), down.shape], shard)
        tops = [down[r0 : r0 + r, c0 : c0 + c] for _, r0, r, c0, c, _, _ in rects[2:]]
        folded = jnp.concatenate([tops[0], jnp.concatenate(tops[1:], 1)], 0)
        return jnp.concatenate([units(w_gate), units(w_up), folded], 1)
    return pl.pallas_call(
        functools.partial(pack_units_kernel, seq_n),
        grid_spec=pltpu.PrefetchScalarGridSpec(
            num_scalar_prefetch=1,
            grid=(dp_n,),
            in_specs=[
                pl.BlockSpec((shard, unit), lambda i, ref: (0, i * seq_n + ref[0])),
                pl.BlockSpec((shard, unit), lambda i, ref: (0, i * seq_n + ref[0])),
                pl.BlockSpec((unit, w_down.shape[1]), lambda i, ref: (ref[0], 0)),
            ],
            out_specs=pl.BlockSpec((shard, 3 * mine), lambda i, ref: (0, 0)),
        ),
        out_shape=jax.ShapeDtypeStruct((shard, 3 * mine), BF),
        compiler_params=pltpu.CompilerParams(vmem_limit_bytes=48 * 2**20),
        cost_estimate=pl.CostEstimate(flops=0, bytes_accessed=6 * 3 * shard * mine, transcendentals=0),
    )(at[None], w_gate, w_up, w_down)


def spread_kernel(seq_n, at_ref, *refs):
    gates, ups = refs[:seq_n], refs[seq_n : 2 * seq_n]
    wg_ref, wu_ref, og_ref, ou_ref, gain_ref = refs[2 * seq_n :]
    unit = gates[0].shape[1]
    total = jnp.zeros((wg_ref.shape[0], unit), F32)
    for m in range(seq_n):
        span = pl.ds(pl.multiple_of((at_ref[0] ^ m) * unit, unit), unit)
        for piece, w, out in ((gates[m], wg_ref, og_ref), (ups[m], wu_ref, ou_ref)):
            value = piece[...].astype(F32)
            out[:, span] = value
            total = total + value * w[:, span].astype(BF).astype(F32)

    @pl.when(pl.program_id(0) == 0)
    def _():
        gain_ref[...] = total

    @pl.when(pl.program_id(0) != 0)
    def _():
        gain_ref[...] += total


def unfold_kernel(seq_n, at_ref, *refs):
    pieces, out = refs[:seq_n], refs[seq_n]
    rows, wide = pieces[0].shape
    rects, _ = rects_of([out.shape], rows)
    for m in range(seq_n):
        @pl.when(pl.program_id(0) == m)
        def _():
            for _, r0, r, c0, c, p0, pc in rects:
                out[r0 : r0 + r, c0 : c0 + c] = pieces[m][p0 : p0 + r, pc : pc + c].astype(F32)


def spread_units(rel, w_gate, w_up, at):
    dp_n, seq_n = lax.axis_size("dp"), lax.axis_size("seq")
    shard, ff = w_gate.shape
    unit = ff // (dp_n * seq_n)
    mine = dp_n * unit
    if unit % 128:
        pieces = in_order(rel, at)

        def spread(start):
            blocks = [g[:, start : start + mine].reshape(shard, dp_n, 1, unit) for g in pieces]
            return jnp.concatenate(blocks, 2).reshape(shard, ff).astype(F32)

        gate, up = spread(0), spread(mine)
        return gate, up, jnp.sum(gate * w_gate.astype(BF).astype(F32) + up * w_up.astype(BF).astype(F32), 1)
    gate, up, sums = pl.pallas_call(
        functools.partial(spread_kernel, seq_n),
        grid_spec=pltpu.PrefetchScalarGridSpec(
            num_scalar_prefetch=1,
            grid=(dp_n,),
            in_specs=[pl.BlockSpec((shard, unit), lambda i, ref: (0, i))] * seq_n
            + [pl.BlockSpec((shard, unit), lambda i, ref: (0, dp_n + i))] * seq_n
            + [pl.BlockSpec((shard, seq_n * unit), lambda i, ref: (0, i))] * 2,
            out_specs=[pl.BlockSpec((shard, seq_n * unit), lambda i, ref: (0, i))] * 2
            + [pl.BlockSpec((shard, unit), lambda i, ref: (0, 0))],
        ),
        out_shape=[jax.ShapeDtypeStruct((shard, ff), F32)] * 2 + [jax.ShapeDtypeStruct((shard, unit), F32)],
        compiler_params=pltpu.CompilerParams(vmem_limit_bytes=60 * 2**20),
        cost_estimate=pl.CostEstimate(flops=0, bytes_accessed=20 * shard * ff, transcendentals=0),
    )(at[None], *rel, *rel, w_gate, w_up)
    return gate, up, jnp.sum(sums, 1)


def unfold_units(rel, w_down, at):
    seq_n = len(rel)
    unit, model = w_down.shape[0] // seq_n, w_down.shape[1]
    shard, mine = rel[0].shape[0], rel[0].shape[1] // 3
    if unit % 128:
        rects, _ = rects_of([(unit, model)], shard)
        downs = []
        for p in in_order(rel, at):
            a, b, c = [p[p0 : p0 + r, 2 * mine + pc : 2 * mine + pc + w] for _, _, r, _, w, p0, pc in rects]
            downs.append(jnp.concatenate([a, jnp.concatenate([b, c], 0)], 1))
        return jnp.concatenate(downs, 0).astype(F32)
    return pl.pallas_call(
        functools.partial(unfold_kernel, seq_n),
        grid_spec=pltpu.PrefetchScalarGridSpec(
            num_scalar_prefetch=1,
            grid=(seq_n,),
            in_specs=[pl.BlockSpec((shard, mine), lambda i, ref: (0, 2))] * seq_n,
            out_specs=pl.BlockSpec((unit, model), lambda i, ref: (i ^ ref[0], 0)),
        ),
        out_shape=jax.ShapeDtypeStruct(w_down.shape, F32),
        compiler_params=pltpu.CompilerParams(vmem_limit_bytes=60 * 2**20),
        cost_estimate=pl.CostEstimate(flops=0, bytes_accessed=6 * w_down.size, transcendentals=0),
    )(at[None], *rel)


def lane_sums(value):
    total = value[:, 0:128]
    for c in range(128, value.shape[1], 128):
        total = total + value[:, c : c + 128]
    return total


def first_columns_kernel(seq_n, at_ref, *refs):
    pieces, (w_ref, out_ref, sum_ref) = refs[:seq_n], refs[seq_n:]
    cols = w_ref.shape[1]
    for m in range(seq_n):
        for h in range(2):
            @pl.when((pl.program_id(0) == m) & (pl.program_id(1) == h))
            def _():
                value = pieces[m][:, h * cols : (h + 1) * cols].astype(F32)
                out_ref[...] = value
                total = lane_sums(value * w_ref[...].astype(BF).astype(F32))
                if m + h == 0:
                    sum_ref[...] = total
                else:
                    sum_ref[...] += total


def spread_first(rel, w_proj, at):
    seq_n = lax.axis_size("seq")
    rows, cols = w_proj.shape[0], w_proj.shape[1] // seq_n // 3

    def block(i, h, ref):
        return (0, (i ^ ref[0]) * 3 + h)

    grad, sums = pl.pallas_call(
        functools.partial(first_columns_kernel, seq_n),
        grid_spec=pltpu.PrefetchScalarGridSpec(
            num_scalar_prefetch=1,
            grid=(seq_n, 2),
            in_specs=[pl.BlockSpec(rel[0].shape, lambda i, h, ref: (0, 0))] * seq_n + [pl.BlockSpec((rows, cols), block)],
            out_specs=[pl.BlockSpec((rows, cols), block), pl.BlockSpec((rows, 128), lambda i, h, ref: (0, 0))],
        ),
        out_shape=[jax.ShapeDtypeStruct(w_proj.shape, F32), jax.ShapeDtypeStruct((rows, 128), F32)],
        compiler_params=pltpu.CompilerParams(vmem_limit_bytes=60 * 2**20),
        cost_estimate=pl.CostEstimate(flops=0, bytes_accessed=7 * w_proj.size, transcendentals=0),
    )(at[None], *rel, w_proj)
    return grad, sums


def last_columns_kernel(seq_n, first, at_ref, *refs):
    pieces, (w_ref, _, out_ref, first_ref, sum_ref) = refs[:seq_n], refs[seq_n:]
    cols = w_ref.shape[1]
    for m in range(seq_n):
        @pl.when(pl.program_id(0) == m)
        def _():
            first_ref[...] = pieces[m][:, :first].astype(F32)
            value = pieces[m][:, first : first + cols].astype(F32)
            out_ref[...] = value
            total = lane_sums(value * w_ref[...].astype(BF).astype(F32))
            if m == 0:
                sum_ref[...] = total
            else:
                sum_ref[...] += total


def spread_last(rel, w_proj, first, prior, at):
    seq_n = lax.axis_size("seq")
    rows, cols = w_proj.shape[0], w_proj.shape[1] // seq_n // 3

    def block(i, ref):
        return (0, (i ^ ref[0]) * 3 + 2)

    grad, grad_first, sums = pl.pallas_call(
        functools.partial(last_columns_kernel, seq_n, first),
        grid_spec=pltpu.PrefetchScalarGridSpec(
            num_scalar_prefetch=1,
            grid=(seq_n,),
            in_specs=[pl.BlockSpec(rel[0].shape, lambda i, ref: (0, 0))] * seq_n
            + [pl.BlockSpec((rows, cols), block), pl.BlockSpec(memory_space=pl.ANY)],
            out_specs=[
                pl.BlockSpec((rows, cols), block),
                pl.BlockSpec((rows, first), lambda i, ref: (0, i ^ ref[0])),
                pl.BlockSpec((rows, 128), lambda i, ref: (0, 0)),
            ],
        ),
        out_shape=[
            jax.ShapeDtypeStruct(w_proj.shape, F32),
            jax.ShapeDtypeStruct((rows, seq_n * first), F32),
            jax.ShapeDtypeStruct((rows, 128), F32),
        ],
        input_output_aliases={seq_n + 2: 0},
        compiler_params=pltpu.CompilerParams(vmem_limit_bytes=60 * 2**20),
        cost_estimate=pl.CostEstimate(flops=0, bytes_accessed=5 * w_proj.size, transcendentals=0),
    )(at[None], *rel, w_proj, prior)
    return grad, grad_first, sums


def matmul_low(left, right):
    return jnp.dot(left, right, preferred_element_type=F32)


def matmul_tn(left, right):
    return dot_tn(left, right)


def matmul_nt(left, right):
    return dot_nt(left, right)


def inv_rms(values):
    return lax.rsqrt(jnp.mean(values * values, -1, keepdims=True) + NORM_EPS)


def norm_backward(values, scale_inv, gain, grad_norm):
    scaled = grad_norm * gain
    return scale_inv * scaled - values * scale_inv**3 * jnp.mean(scaled * values, -1, keepdims=True)


def after(value, earlier):
    return lax.optimization_barrier((value, earlier))[0]


def swap(value, m):
    n = lax.axis_size("seq")
    return lax.ppermute(value, "seq", [(i, i ^ m) for i in range(n)])


def gather_rel(own):
    far = swap(own, 2)
    return [own, swap(own, 1), far, swap(far, 1)]


def in_order(rel, seq_at):
    odd = seq_at % 2 == 1
    high = seq_at // 2 == 1
    pairs = []
    for a, b in (rel[0:2], rel[2:4]):
        pairs.append((jnp.where(odd, b, a), jnp.where(odd, a, b)))
    (a0, a1), (b0, b1) = pairs
    return [jnp.where(high, b0, a0), jnp.where(high, b1, a1), jnp.where(high, a0, b0), jnp.where(high, a1, b1)]


def piece_spec(shape, i, hold=False):
    more = {"pipeline_mode": pl.Buffered(1)} if hold else {}
    return pl.BlockSpec((1,) + shape[1:], lambda *_: (i,) + (0,) * (len(shape) - 1), **more)


def project_kernel(count, shards, cut, lane, has_prior, at_ref, index_ref, *refs):
    pieces, refs = refs[:count], refs[count:]
    tiles, sides = refs[:shards], refs[shards : 2 * shards]
    norm_ref, join_ref, logit_ref, gains_ref, w_ref, b_ref = refs[2 * shards + (1 if has_prior else 0) :]
    part = pieces[0].shape[1]
    rows = tiles[0].shape[0]
    starts = []
    for k in range(shards):
        which = min(k, shards - 2)
        first = index_ref[which] * rows + (cut if k == shards - 1 else 0)
        starts.append(pl.ds(pl.multiple_of(first, 16), tiles[k].shape[0]))
        w_ref[starts[k], :] = tiles[k][...]

    @pl.when(pl.program_id(0) == 0)
    def _():
        for k in range(shards):
            b_ref[starts[k], :] = sides[k][...]
        i, j = indices(8, 128)
        gains_ref[...] = dot_nt(jnp.where(j == lane + i, 1.0, 0.0).astype(BF), b_ref[...])
        for m in range(count):
            x = pieces[m][0].astype(F32)
            here = pl.ds(pl.multiple_of((at_ref[0] ^ m) * part, part), part)
            norm_ref[0, here, :] = (x * inv_rms(x) * gains_ref[0:1, :]).astype(BF)
        logit_ref[0] = dot_nn(norm_ref[0], b_ref[...]).astype(BF)

    join_ref[0] = dot_nn(norm_ref[0], w_ref[...]).astype(BF)


def project(x_rel, lane, gathered, wide, at, r, prior):
    shards, index = gathered
    count = len(x_rel)
    rows_n, part, model = x_rel[0][0].shape
    length = part * count
    tile = 256

    def whole(shape):
        return pl.BlockSpec(shape, lambda j, *_: (0,) * len(shape))

    args = [at[None], index, *[x for x, _ in x_rel], *shards, *shards]
    aliases = {}
    if prior is not None:
        aliases = {len(args): 0}
        args.append(prior)
    return pl.pallas_call(
        functools.partial(project_kernel, count, len(shards), middle_row(shards[0].shape[0]), lane, prior is not None),
        grid_spec=pltpu.PrefetchScalarGridSpec(
            num_scalar_prefetch=2,
            grid=(wide // tile,),
            in_specs=[piece_spec(x.shape, i, True) for x, i in x_rel]
            + [pl.BlockSpec((s.shape[0], tile), lambda j, *_: (0, j)) for s in shards]
            + [pl.BlockSpec((s.shape[0], 128), lambda j, *_: (0, wide // 128)) for s in shards]
            + [pl.BlockSpec(memory_space=pl.ANY)] * (0 if prior is None else 1),
            out_specs=[
                pl.BlockSpec((1, length, model), lambda j, *_: (r, 0, 0)),
                pl.BlockSpec((1, length, tile), lambda j, *_: (0, 0, j)),
                whole((1, length, 128)),
                whole((8, model)),
            ],
            scratch_shapes=[pltpu.VMEM((model, tile), BF), pltpu.VMEM((model, 128), BF)],
        ),
        out_shape=[
            jax.ShapeDtypeStruct((rows_n, length, model), BF),
            jax.ShapeDtypeStruct((1, length, wide), BF),
            jax.ShapeDtypeStruct((1, length, 128), BF),
            jax.ShapeDtypeStruct((8, model), F32),
        ],
        input_output_aliases=aliases,
        compiler_params=pltpu.CompilerParams(vmem_limit_bytes=56 * 2**20),
        cost_estimate=pl.CostEstimate(
            flops=2 * length * model * wide, bytes_accessed=6 * length * model, transcendentals=0
        ),
    )(*args)


def by_device(total, keep, send, part):
    for m in range(total.shape[0] // part):
        (keep, send)[m % 2][m // 2] = total[m * part : (m + 1) * part].astype(BF)


def feed_kernel(seq_n, tiles, has_prior, *refs):
    two, top = refs[:seq_n], refs[seq_n : 2 * seq_n]
    wg_ref, wu_ref, wd_ref, wg_rows, wu_rows, wd_cols = refs[2 * seq_n : 2 * seq_n + 6]
    refs = refs[2 * seq_n + (9 if has_prior else 6) :]
    hid_ref, gg_ref, gu_ref, keep_b, send_b, keep_f, send_f, two_ref, top_ref, hid, gg, gu = refs
    part = two[0].shape[0]
    j = pl.program_id(0)
    tile = wg_ref.shape[1]

    @pl.when(j == 0)
    def _():
        for m in range(seq_n):
            s = slice(m * part, (m + 1) * part)
            two_ref[s, :] = two[m][...]
            top_ref[s, :] = top[m][0]

    @pl.when(j < tiles)
    def _():
        gate = dot_nn(two_ref[...], wg_ref[...])
        up = dot_nn(two_ref[...], wu_ref[...])
        gh = dot_nt(top_ref[...], wd_ref[...])
        sig = jax.nn.sigmoid(gate)
        act = gate * sig
        here = pl.ds(pl.multiple_of(j * tile, tile), tile)
        for value, out, held in (
            (act * up, hid_ref, hid),
            (gh * up * sig * (1.0 + gate * (1.0 - sig)), gg_ref, gg),
            (gh * act, gu_ref, gu),
        ):
            low = value.astype(BF)
            out[0] = low
            held[:, here] = low

    @pl.when(j >= tiles)
    def _():
        by_device(dot_nt(gg[...], wg_rows[...]) + dot_nt(gu[...], wu_rows[...]), keep_b, send_b, part)
        by_device(dot_nn(hid[...], wd_cols[...]), keep_f, send_f, part)


def feed(two, top, gate_full, up_full, down_full, r, prior):
    seq_n = len(two)
    part, model = two[0].shape
    rows_n = top[0][0].shape[0]
    mine = gate_full.shape[1]
    tile = 256
    tiles = mine // tile
    length = part * seq_n

    def early(j):
        return jnp.minimum(j, tiles - 1)

    def late(j):
        return jnp.maximum(j - tiles, 0)

    piece = pl.BlockSpec((part, model), lambda j: (0, 0), pipeline_mode=pl.Buffered(1))
    columns = pl.BlockSpec((model, tile), lambda j: (0, early(j)))
    lines = pl.BlockSpec((tile, mine), lambda j: (late(j), 0))
    hidden = pl.BlockSpec((1, length, tile), lambda j: (r, 0, early(j)))
    args = [*two, *[g for g, _ in top], gate_full, up_full, down_full, gate_full, up_full, down_full]
    aliases = {}
    if prior is not None:
        aliases = {len(args) + i: i for i in range(3)}
        args += prior
    outs = pl.pallas_call(
        functools.partial(feed_kernel, seq_n, tiles, prior is not None),
        grid=(tiles + model // tile,),
        in_specs=[piece] * seq_n
        + [piece_spec(g.shape, i, True) for g, i in top]
        + [columns, columns, pl.BlockSpec((tile, model), lambda j: (early(j), 0))]
        + [lines, lines, pl.BlockSpec((mine, tile), lambda j: (0, late(j)))]
        + [pl.BlockSpec(memory_space=pl.ANY)] * (3 if prior is not None else 0),
        out_specs=[hidden] * 3 + [pl.BlockSpec((seq_n // 2, part, tile), lambda j: (0, 0, late(j)))] * 4,
        out_shape=[jax.ShapeDtypeStruct((rows_n, length, mine), BF)] * 3
        + [jax.ShapeDtypeStruct((seq_n // 2, part, model), BF)] * 4,
        scratch_shapes=[pltpu.VMEM((length, model), BF)] * 2 + [pltpu.VMEM((length, mine), BF)] * 3,
        input_output_aliases=aliases,
        compiler_params=pltpu.CompilerParams(vmem_limit_bytes=56 * 2**20),
        cost_estimate=pl.CostEstimate(
            flops=12 * length * model * mine, bytes_accessed=12 * length * model + 12 * model * mine, transcendentals=0
        ),
    )(*args)
    return outs[:3], outs[3:]


def outer_kernel(lefts, counts, lanes, *refs):
    left, refs = refs[:lefts], refs[lefts:]
    groups = []
    for n in counts:
        groups.append(refs[:n])
        refs = refs[n:]
    n = len(counts) if lanes is None else len(lanes)
    outs, scratch = refs[:n], list(refs[n:])

    def gather(pieces, into):
        row = 0
        for p in pieces:
            value = p[...] if len(p.shape) == 2 else p[0]
            into[row : row + value.shape[0], :] = value
            row += value.shape[0]

    if lefts > 1:
        tall = scratch.pop(0)
        gather(left, tall)
    else:
        tall = left[0]
    for n, group, out in zip(counts, groups, outs):
        if n > 1:
            whole = scratch.pop(0)

            @pl.when(pl.program_id(0) == 0)
            def _():
                gather(group, whole)
        else:
            whole = group[0]
        if lanes is None:
            out[...] = dot_tn(tall[...], whole[...]).astype(BF)
    if lanes is not None:
        for out, span in zip(outs, lanes):
            out[...] = dot_tn(tall[...], whole[:, slice(*span)]).astype(BF)


def outer(left, rights, lanes=None):
    total = sum(p.shape[0] for p in left)
    model = left[0].shape[1]
    tile = 256
    widths = [(g[0][0] if isinstance(g[0], tuple) else g[0]).shape[-1] for g in rights]
    spans = widths if lanes is None else [high - low for low, high in lanes]
    scratch = [pltpu.VMEM((total, tile), BF)] if len(left) > 1 else []
    scratch += [pltpu.VMEM((total, w), BF) for g, w in zip(rights, widths) if len(g) > 1]
    specs = [pl.BlockSpec((p.shape[0], tile), lambda j: (0, j)) for p in left]
    args = list(left)
    for g in rights:
        for p in g:
            if isinstance(p, tuple):
                specs.append(piece_spec(p[0].shape, p[1], True))
                args.append(p[0])
            else:
                specs.append(pl.BlockSpec(p.shape, lambda j: (0, 0), pipeline_mode=pl.Buffered(1)))
                args.append(p)
    return pl.pallas_call(
        functools.partial(outer_kernel, len(left), [len(g) for g in rights], lanes),
        grid=(model // tile,),
        in_specs=specs,
        out_specs=[pl.BlockSpec((tile, w), lambda j: (j, 0)) for w in spans],
        out_shape=[jax.ShapeDtypeStruct((model, w), BF) for w in spans],
        scratch_shapes=scratch,
        compiler_params=pltpu.CompilerParams(vmem_limit_bytes=56 * 2**20),
        cost_estimate=pl.CostEstimate(
            flops=2 * total * model * sum(widths), bytes_accessed=2 * total * (model + sum(widths)), transcendentals=0
        ),
    )(*args)


def middle_kernel(count, at_ref, *refs):
    parts, weights, (x_ref, gain_ref, mixed, mid, two) = refs[:count], refs[count : 2 * count], refs[2 * count :]
    cols = weights[0].shape[1]
    spans = [pl.ds(pl.multiple_of((at_ref[0] ^ m) * cols, cols), cols) for m in range(count)]
    for m in range(count):
        mixed[:, spans[m]] = parts[m][0]
    for m in range(count):
        mid[:, spans[m]] = x_ref[0, :, spans[m]].astype(F32) + dot_nn(mixed[...], weights[m][...])
    value = mid[...]
    two[...] = (value * inv_rms(value) * gain_ref[...]).astype(BF)


def to_middle(parts, out_rel, x, r, gain, at):
    _, part, model = x.shape
    count = len(out_rel)
    return pl.pallas_call(
        functools.partial(middle_kernel, count),
        grid=(1,),
        in_specs=[pl.BlockSpec(memory_space=pltpu.SMEM)]
        + [piece_spec(p.shape, i) for p, i in parts]
        + [pl.BlockSpec(w.shape, lambda j: (0, 0)) for w in out_rel]
        + [piece_spec(x.shape, r), pl.BlockSpec(gain.shape, lambda j: (0, 0))],
        out_specs=[pl.BlockSpec((part, model), lambda j: (0, 0))] * 3,
        out_shape=[
            jax.ShapeDtypeStruct((part, model), BF),
            jax.ShapeDtypeStruct((part, model), F32),
            jax.ShapeDtypeStruct((part, model), BF),
        ],
        compiler_params=pltpu.CompilerParams(vmem_limit_bytes=48 * 2**20),
        cost_estimate=pl.CostEstimate(flops=2 * part * model * model, bytes_accessed=3 * model * model, transcendentals=0),
    )(at[None], *[p for p, _ in parts], *out_rel, x, gain)


def stacked(refs):
    values = [v[...].astype(F32) for v in refs]
    return values[0] if len(values) == 1 else jnp.concatenate(values, 0)


def second_kernel(count, fars, at_ref, *refs):
    weights, far, refs = refs[:count], refs[count : count + fars], refs[count + fars :]
    own_ref, near_ref, mid_ref, g_ref, gain_ref, grad_ref, low_ref, parts, mixed = refs
    cols = parts.shape[2]
    spans = [pl.ds(pl.multiple_of((at_ref[0] ^ m) * cols, cols), cols) for m in range(count)]
    got = own_ref[0].astype(F32) + near_ref[0].astype(F32) + stacked(far)
    mid = mid_ref[...]
    grad_ref[...] = g_ref[0].astype(F32) + norm_backward(mid, inv_rms(mid), gain_ref[...], got)
    low_ref[...] = grad_ref[...].astype(BF)
    total = dot_nt(low_ref[:, spans[0]], weights[0][...])
    for m in range(1, count):
        total = total + dot_nt(low_ref[:, spans[m]], weights[m][...])
    mixed[...] = total
    for m in range(count):
        parts[m] = mixed[:, spans[m]].astype(BF)


def second_back(keep, near, far, mid, out_grad, r, gain, out_rel, at):
    part, model = mid.shape
    count = len(out_rel)
    cols = out_rel[0].shape[1]

    def whole(v):
        return pl.BlockSpec(v.shape, lambda j: (0, 0))

    return pl.pallas_call(
        functools.partial(second_kernel, count, len(far)),
        grid=(1,),
        in_specs=[pl.BlockSpec(memory_space=pltpu.SMEM)]
        + [whole(w) for w in [*out_rel, *far]]
        + [piece_spec(keep.shape, 0), piece_spec(near.shape, 0), whole(mid)]
        + [piece_spec(out_grad.shape, r), whole(gain)],
        out_specs=[whole(mid), whole(mid), pl.BlockSpec((count, part, cols), lambda j: (0, 0, 0))],
        out_shape=[
            jax.ShapeDtypeStruct((part, model), F32),
            jax.ShapeDtypeStruct((part, model), BF),
            jax.ShapeDtypeStruct((count, part, cols), BF),
        ],
        scratch_shapes=[pltpu.VMEM((part, model), F32)],
        compiler_params=pltpu.CompilerParams(vmem_limit_bytes=48 * 2**20),
        cost_estimate=pl.CostEstimate(flops=2 * part * model * model, bytes_accessed=3 * model * model, transcendentals=0),
    )(at[None], *out_rel, *far, keep, near, mid, out_grad, gain)


def out_kernel(count, rows_n, at_ref, *refs):
    mixed, low, outs = refs[:rows_n], refs[rows_n : 2 * rows_n], refs[2 * rows_n :]
    cols = outs[0].shape[2]
    for m in range(count):
        span = pl.ds(pl.multiple_of((at_ref[0] ^ m) * cols, cols), cols)
        total = dot_tn(mixed[0][...], low[0][:, span])
        for r in range(1, rows_n):
            total = total + dot_tn(mixed[r][...], low[r][:, span])
        outs[m % 2][m // 2] = total.astype(BF)


def grad_out_parts(mixed, low, count, at):
    part, model = mixed[0].shape
    rows_n = len(mixed)
    cols = model // count
    tile = 256
    return pl.pallas_call(
        functools.partial(out_kernel, count, rows_n),
        grid_spec=pltpu.PrefetchScalarGridSpec(
            num_scalar_prefetch=1,
            grid=(model // tile,),
            in_specs=[pl.BlockSpec((part, tile), lambda j, ref: (0, j))] * rows_n
            + [pl.BlockSpec((part, model), lambda j, ref: (0, 0))] * rows_n,
            out_specs=[pl.BlockSpec((count // 2, tile, cols), lambda j, ref: (0, j, 0))] * 2,
        ),
        out_shape=[jax.ShapeDtypeStruct((count // 2, model, cols), BF)] * 2,
        compiler_params=pltpu.CompilerParams(vmem_limit_bytes=48 * 2**20),
        cost_estimate=pl.CostEstimate(flops=4 * part * model * model, bytes_accessed=3 * model * model, transcendentals=0),
    )(at[None], *mixed, *low)


def first_kernel(count, at_ref, grad_ref, w_ref, keep, send, total):
    part = keep.shape[1]
    total[...] = dot_nt(grad_ref[0], w_ref[...])
    for m in range(count):
        here = pl.ds(pl.multiple_of((at_ref[0] ^ m) * part, part), part)
        (keep, send)[m % 2][m // 2] = total[here, :].astype(BF)


def first_parts(grad_joined, w_side, r, count, at):
    _, length, wide = grad_joined.shape
    model = w_side.shape[0]
    part = length // count
    tile = 256
    return pl.pallas_call(
        functools.partial(first_kernel, count),
        grid_spec=pltpu.PrefetchScalarGridSpec(
            num_scalar_prefetch=1,
            grid=(model // tile,),
            in_specs=[
                pl.BlockSpec((1, length, wide), lambda j, ref: (r, 0, 0), pipeline_mode=pl.Buffered(1)),
                pl.BlockSpec((tile, wide), lambda j, ref: (j, 0)),
            ],
            out_specs=[pl.BlockSpec((count // 2, part, tile), lambda j, ref: (0, 0, j))] * 2,
            scratch_shapes=[pltpu.VMEM((length, tile), F32)],
        ),
        out_shape=[jax.ShapeDtypeStruct((count // 2, part, model), BF)] * 2,
        compiler_params=pltpu.CompilerParams(vmem_limit_bytes=48 * 2**20),
        cost_estimate=pl.CostEstimate(
            flops=2 * length * wide * model, bytes_accessed=4 * length * wide, transcendentals=0
        ),
    )(at[None], grad_joined, w_side)


def last_kernel(rows_n, spans, *refs):
    keeps, nears, mids, refs = refs[:rows_n], refs[rows_n : 2 * rows_n], refs[2 * rows_n : 3 * rows_n], refs[3 * rows_n :]
    fars, (x_ref, gain_ref, out_ref) = refs[:-3], refs[-3:]
    for r, (low, high) in enumerate(spans):
        got = keeps[r][0].astype(F32) + nears[r][0].astype(F32) + stacked(fars[low:high])
        x = x_ref[r].astype(F32)
        out_ref[r] = mids[r][...] + norm_backward(x, inv_rms(x), gain_ref[...], got)


def layer_kernel(rows_n, spans, *refs):
    keeps, nears, mids, refs = refs[:rows_n], refs[rows_n : 2 * rows_n], refs[2 * rows_n : 3 * rows_n], refs[3 * rows_n :]
    fars, out_ref = refs[:-1], refs[-1]
    for r, (low, high) in enumerate(spans):
        got = keeps[r][0].astype(F32) + nears[r][0].astype(F32) + stacked(fars[low:high])
        out_ref[r] = (mids[r][...] + got).astype(BF)


def sum_rows(kernel, dtype, keep, near, far, mids, *more):
    rows_n = len(mids)
    shape = (rows_n,) + mids[0].shape
    spans, flat = [], []
    for row in far:
        spans.append((len(flat), len(flat) + len(row)))
        flat += row
    return pl.pallas_call(
        functools.partial(kernel, rows_n, spans),
        grid=(1,),
        in_specs=[piece_spec(v.shape, 0) for v in [*keep, *near]]
        + [pl.BlockSpec(v.shape, lambda j: (0, 0)) for v in mids]
        + [pl.BlockSpec((n, v.shape[1]), functools.partial(lambda i, j: (i, 0), i)) for v, i, n in flat]
        + [pl.BlockSpec(v.shape, functools.partial(lambda n, j: (0,) * n, v.ndim)) for v in more],
        out_specs=pl.BlockSpec(shape, lambda j: (0, 0, 0)),
        out_shape=jax.ShapeDtypeStruct(shape, dtype),
        compiler_params=pltpu.CompilerParams(vmem_limit_bytes=48 * 2**20),
        cost_estimate=pl.CostEstimate(flops=0, bytes_accessed=16 * rows_n * mids[0].size, transcendentals=0),
    )(*keep, *near, *mids, *[v for v, _, _ in flat], *more)


def fold(keep, got, low=0, high=None):
    return (keep[1, low:high].astype(F32) + got[1, low:high].astype(F32)).astype(BF)


def tie(*groups):
    return lax.optimization_barrier(groups)


def per_device(
    inputs,
    doc_ids,
    gain_attn,
    w_proj,
    w_beta,
    conv_taps,
    w_out,
    gain_mlp,
    w_gate,
    w_up,
    w_down,
    out_grad,
):
    rows_n, part, model = inputs.shape
    heads_n = w_beta.shape[1]
    taps_n, width_out = conv_taps.shape
    dp_n, seq_n = lax.axis_size("dp"), lax.axis_size("seq")
    at = lax.axis_index("seq")
    length = part * seq_n
    heads = heads_n // seq_n
    width = model // heads_n
    cols = heads * width
    wide = 4 * cols
    shard = w_proj.shape[0]
    ff = w_gate.shape[1]
    unit = ff // (dp_n * seq_n)
    mine_n = dp_n * unit
    quarter = model // seq_n
    rows = range(rows_n)
    last = rows_n - 1

    proj_mine = lax.dynamic_slice_in_dim(w_proj, at * wide, wide, 1)
    lanes = lax.broadcasted_iota(jnp.int32, (1, 128), 1)
    side = jnp.pad(w_beta, ((0, 0), (0, 128 - heads_n)))
    side = jnp.where(lanes == heads_n, gain_attn[:, None], jnp.where(lanes == heads_n + 1, gain_mlp[:, None], side)).astype(BF)
    packed = jnp.concatenate([proj_mine.astype(BF), side], 1)
    sent = []
    ring = ring_gather(packed, sent)
    hop = next(ring)

    flat = jnp.concatenate([doc_ids.astype(BF).reshape(-1), conv_taps.astype(BF).reshape(-1)])
    flat = after(flat, packed)
    flat = [flat, swap(flat, 1), swap(flat, 2), swap(flat, 3)]
    own_x, units = inputs, pack_units(w_gate, w_up, w_down, at)
    hop, flat, own_x, units = tie(hop, flat, own_x, units)
    hop = ring.send(hop)
    flat, own_x, _ = tie(flat, own_x, sent)
    far_x = [swap(own_x[0:1], 2)]
    flat = in_order(flat, at)
    cut = rows_n * part
    doc = jnp.concatenate([t[:cut].reshape(rows_n, part) for t in flat], 1).astype(F32)
    taps_shard = jnp.concatenate([t[cut:].reshape(taps_n, width_out) for t in flat], 1)
    taps_shard = jnp.pad(taps_shard, ((0, 16 - taps_n), (0, quarter - taps_shard.shape[1])))
    out_mine = lax.dynamic_slice_in_dim(w_out, at * quarter, quarter, 1).astype(BF)
    out_mine = lax.all_gather(jnp.concatenate([out_mine, taps_shard], 0), "dp", axis=0)
    hop, far_x, doc = tie(hop, far_x, doc)
    hop = ring.send(hop)
    doc, own_x, far_x, _ = tie(doc, own_x, far_x, sent)
    far_x += [swap(own_x[r : r + 1], 2) for r in rows[1:]]
    skew_x = [swap(far_x[0], 1)]
    near_x = swap(own_x, 1)
    lanes = lax.broadcasted_iota(jnp.int32, (1, 1, 128), 2)
    info = jnp.where(lanes == 0, doc[:, :, None], 0.0)
    for shift_by in range(1, taps_n):
        same = (doc[:, shift_by:] == doc[:, :-shift_by]).astype(F32)
        info = jnp.where(lanes == shift_by, jnp.pad(same, ((0, 0), (shift_by, 0)))[:, :, None], info)
    aux = [info[r : r + 1] for r in rows]
    doc_rows = [jnp.broadcast_to(doc[r : r + 1, None, :], (1, 8, length)) for r in rows]
    hop, far_x, near_x, skew_x, aux, doc_rows = tie(hop, far_x, near_x, skew_x, aux, doc_rows)
    hop = ring.send(hop)
    far_x, _ = tie(far_x, sent)
    skew_x += [swap(far_x[r], 1) for r in rows[1:]]
    hop, skew_x = tie(hop, skew_x)
    proj_shards = drain(ring, hop)
    x_rel = [[(own_x, r), (near_x, r), (far_x[r], 0), (skew_x[r], 0)] for r in rows]

    ring = ring_gather(after(units, proj_shards[0]), sent)
    hop = next(ring)
    own_g, _ = tie(out_grad, sent)
    far_g, near_g = swap(own_g, 2), swap(own_g, 1)
    normed, joined, logit = None, [], []
    for r in rows:
        normed, j, l, gains = project(x_rel[r], heads_n, proj_shards, wide, at, r, normed)
        joined.append(j)
        logit.append(l)
    gain_one, gain_two = gains[0:1], gains[1:2]
    hop, joined, logit, out_mine = tie(hop, joined, logit, out_mine)
    hop = ring.send(hop)
    joined, out_mine, _ = tie(joined, out_mine, sent)
    taps_full = out_mine[:, shard : shard + taps_n, :shard].transpose(1, 0, 2).reshape(taps_n, model)
    taps_mine = lax.dynamic_slice_in_dim(taps_full.astype(F32), at * cols, cols, 1)
    taps_mine = jnp.pad(taps_mine, ((0, 8 - taps_n), (0, 0)))
    out_mine = out_mine[:, :shard].reshape(model, quarter)
    out_far, out_near = swap(out_mine, 2), swap(out_mine, 1)

    def exchange(parts):
        return [(parts, 0)] + [(swap(parts[m : m + 1], m), 0) for m in range(1, seq_n)]

    kept, attn, pair = [], [], []
    for r in rows:
        outs = attend_fwd(joined[r], aux[r], logit[r], doc_rows[r], taps_mine, at, heads, taps_n, seq_n)
        if r == 0:
            outs, hop, joined, out_far, out_near, near_g, far_g = tie(
                outs, hop, joined, out_far, out_near, near_g, far_g
            )
        elif r == last:
            outs, hop, pair, out_skew, skew_g = tie(outs, hop, pair, out_skew, skew_g)
        hop = ring.send(hop)
        mine, joined, pair, _ = tie(outs[0], joined, pair, sent)
        attn.append(mine)
        pair.append(swap(mine[2:], 2))
        if r == 0:
            out_skew, skew_g = swap(out_far, 1), swap(far_g, 1)
        kept.append(outs[1:])
    pair_near = [swap(jnp.stack([attn[0][1], pair[0][1]]), 1)]
    out_rel = [out_mine, out_near, out_far, out_skew]

    def middle_of(r):
        parts = [(attn[r], 0), (pair_near[r], 0), (pair[r], 0), (pair_near[r], 1)]
        return to_middle(parts, out_rel, inputs, r, gain_two, at)

    done = [middle_of(0)]
    done[0], pair[1], hop = tie(done[0], pair[1], hop)
    pair_near.append(swap(jnp.stack([attn[1][1], pair[1][1]]), 1))
    two = done[0][2]
    two_rel = [[two, swap(two, 1), swap(two, 2)]]
    done.append(middle_of(1))
    done[1], two_rel[0][0] = tie(done[1], two_rel[0][0])
    mixed, middle = [v[0] for v in done], [v[1] for v in done]
    two = done[1][2]
    two_rel.append([two, swap(two, 1), swap(two, 2)])
    full = place(drain(ring, hop), [(shard, mine_n), (shard, mine_n), (unit, model)])
    proj_index, full, _ = tie(proj_shards[1], full, middle[1])
    (proj_full,) = place((proj_shards[0], proj_index), [(shard, packed.shape[1])])
    full, two_rel[0], proj_full = tie(full, two_rel[0], proj_full)
    g_rel = [[(own_g, r), (near_g, r), (far_g, r), (skew_g, r)] for r in rows]

    prior, norm, layer = None, [], []
    for r in rows:
        two_rel[r].append(swap(two_rel[r][2], 1))
        if r > 0:
            two_rel[r], near_n = tie(two_rel[r], near_n)
            far_n = [[swap(fold(norm[0][0], near_n[0]), 2)]]
        prior, outs = feed(two_rel[r], g_rel[r], *full, r, prior)
        if r == 0:
            prior, outs, two_rel[1] = tie(prior, outs, two_rel[1])
            near_n = [swap(outs[1], 1)]
        norm.append(outs[:2])
        layer.append(outs[2:])
    hid, g_gate, g_up = [v.reshape(rows_n * length, -1) for v in prior]
    upper, lower = (0, part // 2), (part // 2, part)

    def second(r):
        return second_back(norm[r][0], near_n[r], far_n[r], middle[r], out_grad, r, gain_two, out_rel, at)

    norm[last], layer, hid, far_n = tie(norm[last], layer, hid, far_n)
    near_n.append(swap(norm[last][1], 1))
    done = [second(0)]
    done[0], hid, near_n, layer = tie(done[0], hid, near_n, layer)
    heads_rel = [exchange(done[0][2])]
    far_n.append([fold(norm[last][0], near_n[last], *upper)])
    hid, far_n[last] = tie(hid, far_n[last])
    far_n[last] = [swap(far_n[last][0], 2)]
    near_l = [swap(layer[r][1], 1) for r in rows]
    (grad_down,) = outer([hid], [[g for rel in g_rel for g in rel]])
    grad_down, g_gate, near_l, far_n, heads_got = tie(grad_down, g_gate, near_l, far_n, [p for p, _ in heads_rel[0]])
    heads_rel = [[(p, 0) for p in heads_got]]
    far_n[last].append(fold(norm[last][0], near_n[last], *lower))
    far_l = [fold(layer[0][0], near_l[0], *upper)]
    g_gate, far_n[last][1], far_l = tie(g_gate, far_n[last][1], far_l)
    far_n[last][1] = swap(far_n[last][1], 2)
    far_l = [swap(far_l[0], 2)]
    grad_gate, grad_up = outer([p for rel in two_rel for p in rel], [[g_gate], [g_up]])
    grad_gate, grad_up, far_n, far_l = tie(grad_gate, grad_up, far_n, far_l)
    ring = ring_scatter([grad_gate, grad_up, grad_down], None, sent)
    hop = next(ring)
    far_n, _ = tie(far_n, sent)
    done.append(second(last))
    grad_mid, low = [d[0] for d in done], [d[1] for d in done]
    keep_out, send_out = grad_out_parts(mixed, low, seq_n, at)
    hop, keep_out, send_out, heads_1, grad_mid = tie(hop, keep_out, send_out, done[last][2], grad_mid)
    hop = ring.send(hop)
    far_l.append(jnp.concatenate([fold(layer[0][0], near_l[0], *lower), fold(layer[last][0], near_l[last], *upper)], 0))
    send_out, heads_1, far_l, _ = tie(send_out, heads_1, far_l, sent)
    pair = swap(heads_1[2:], 2)
    near_out = swap(send_out, 1)
    far_l[1] = swap(far_l[1], 2)

    def backward(r, prior):
        return attend_bwd(
            joined[r], aux[r], logit[r], taps_mine, heads_rel[r], kept[r], at, heads, taps_n, r, rows_n, prior
        )

    outs = backward(0, None)
    outs, hop, pair, near_out, far_l = tie(outs, hop, pair, near_out, far_l)
    hop = ring.send(hop)
    far_out = fold(keep_out, near_out)
    outs, far_out, pair, _ = tie(outs, far_out, pair, sent)
    pair_near = swap(jnp.stack([heads_1[1], pair[1]]), 1)
    far_out = swap(far_out, 2)
    parts = [first_parts(outs[0], proj_full, 0, seq_n, at)]
    outs, parts, pair_near = tie(outs, parts, pair_near)
    heads_rel.append([(heads_1, 0), (pair_near, 0), (pair, 0), (pair_near, 1)])
    near_in = [swap(parts[0][1], 1)]
    far_l.append(swap(fold(layer[last][0], near_l[last], *lower), 2))
    grad_taps = [outs[1][0]]
    outs = backward(last, outs[0])
    outs, hop, far_out, far_l, near_in = tie(outs, hop, far_out, far_l, near_in)
    hop = ring.send(hop)
    grad_joined = outs[0]
    grad_taps.append(outs[1][0])
    far_in = [fold(parts[0][0], near_in[0])]
    grad_joined, far_in, far_out, _ = tie(grad_joined, far_in, far_out, sent)
    far_in = [swap(far_in[0], 2)]

    grad_out = (keep_out[0].astype(F32) + near_out[0].astype(F32) + far_out.astype(F32)).astype(BF)
    taps_grad = sum(grad_taps)[:, :taps_n].transpose(1, 0, 2).reshape(taps_n, cols)
    taps_grad = lax.dynamic_update_slice_in_dim(jnp.zeros((taps_n, model), F32), taps_grad, at * cols, 1)
    taps_grad = jnp.pad(taps_grad.T.astype(BF), ((0, 0), (heads_n, 128 - heads_n - taps_n)))
    tall, joined_all = normed.reshape(rows_n * length, model), grad_joined.reshape(rows_n * length, -1)
    split = wide // 3 * 2
    grad_one, grad_two = outer([tall], [[joined_all]], [(0, split), (split, joined_all.shape[1])])
    grad_one, grad_two, taps_grad, grad_out, far_in, grad_joined = tie(
        grad_one, grad_two, taps_grad, grad_out, far_in, grad_joined
    )
    more = []
    ring_one = ring_scatter([grad_one], None, sent)
    hop_one = next(ring_one)
    ring_two = ring_scatter([grad_out, grad_two], taps_grad, more)
    hop_two = next(ring_two)
    grad_joined, hop, _, _ = tie(grad_joined, hop, sent, more)
    grad_units = drain(ring, hop)
    grad_joined, grad_units, _, _ = tie(grad_joined, grad_units, sent, more)
    thirds = [i * (shard // 48) * 16 for i in range(3)] + [shard]
    units_cut = [grad_units[lo:hi] for lo, hi in zip(thirds, thirds[1:])]
    units_far = [swap(units_cut[0], 2)]
    parts.append(first_parts(grad_joined, proj_full, last, seq_n, at))
    parts, hop_one, hop_two, units_far, units_cut = tie(parts, hop_one, hop_two, units_far, units_cut)
    hop_one = ring_one.send(hop_one)
    hop_two = ring_two.send(hop_two)
    near_in.append(swap(parts[last][1], 1))
    middle, near_in, units_cut, _, _ = tie(middle, near_in, units_cut, sent, more)
    far_in.append(swap(fold(parts[last][0], near_in[last]), 2))
    half = part // 2
    layer_out = sum_rows(
        layer_kernel,
        BF,
        [v[0] for v in layer],
        near_l,
        [[(far_l[0], 0, half), (far_l[1], 0, half)], [(far_l[1], 1, half), (far_l[2], 0, half)]],
        middle,
    )
    layer_out, hop_one, units_cut = tie(layer_out, hop_one, units_cut)
    hop_one = ring_one.send(hop_one)
    hop_two, units_cut, far_in, _ = tie(hop_two, units_cut, far_in, sent)
    hop_two = ring_two.send(hop_two)
    units_cut, far_in, _ = tie(units_cut, far_in, more)
    units_far.append(swap(units_cut[1], 2))
    grad_in = sum_rows(
        last_kernel, F32, [v[0] for v in parts], near_in, [[(v, 0, part)] for v in far_in], grad_mid, inputs, gain_one
    )
    hop_one, units_far, grad_in, units_cut = tie(hop_one, units_far, grad_in, units_cut)
    grad_one = drain(ring_one, hop_one)
    units_far.append(swap(units_cut[2], 2))
    hop_two, grad_one, units_far = tie(hop_two, grad_one, units_far)
    hop_two = ring_two.send(hop_two)
    far_all = jnp.concatenate(units_far, 0)
    far_all, grad_one, _ = tie(far_all, grad_one, more)
    units_near, units_skew = swap(grad_units, 1), swap(far_all, 1)
    one_far, one_near = swap(grad_one, 2), swap(grad_one, 1)
    units_rel = [grad_units, units_near, far_all, units_skew]
    gate_out, up_out, sums = spread_units(units_rel, w_gate, w_up, at)
    gain_two_out = sums / gain_mlp.astype(BF).astype(F32)
    hop_two, gate_out, up_out, gain_two_out, one_far, one_near = tie(
        hop_two, gate_out, up_out, gain_two_out, one_far, one_near
    )
    grad_two = drain(ring_two, hop_two)
    two_far, two_near = swap(grad_two, 2), swap(grad_two, 1)
    units_rel, one_far, _ = tie(units_rel, one_far, grad_two)
    down_out = unfold_units(units_rel, w_down, at)
    proj_out, sums = spread_first([grad_one, one_near, one_far, swap(one_far, 1)], w_proj, at)
    two_far, two_near, proj_out, down_out = tie(two_far, two_near, proj_out, down_out)
    rel = [grad_two, two_near, two_far, swap(two_far, 1)]
    proj_out, out_out, more_sums = spread_last(rel, w_proj, quarter, proj_out, at)
    sums = jnp.sum(sums + more_sums, 1)
    tail = [t[:, -128:].astype(F32) for t in rel]
    tail = (tail[0] + tail[1]) + (tail[2] + tail[3])
    beta_out = tail[:, :heads_n]
    sums = sums + jnp.sum(beta_out * w_beta.astype(BF).astype(F32), 1)
    gain_one_out = sums / gain_attn.astype(BF).astype(F32)
    taps_out = lax.dynamic_slice_in_dim(tail[:, heads_n : heads_n + taps_n], at * width_out, width_out, 0).T
    return (
        layer_out,
        grad_in,
        gain_one_out,
        proj_out,
        beta_out,
        taps_out,
        out_out,
        gain_two_out,
        gate_out,
        up_out,
        down_out,
    )


def solution(mesh):
    in_specs = (
        P("dp", "seq", None),
        P("dp", "seq"),
        P("dp"),
        P("dp", None),
        P("dp", None),
        P(None, ("dp", "seq")),
        P("dp", None),
        P("dp"),
        P("dp", None),
        P("dp", None),
        P("dp", None),
        P("dp", "seq", None),
    )
    out_specs = (
        P("dp", "seq", None),
        P("dp", "seq", None),
        P("dp"),
        P("dp", None),
        P("dp", None),
        P(None, ("dp", "seq")),
        P("dp", None),
        P("dp"),
        P("dp", None),
        P("dp", None),
        P("dp", None),
    )
    return jax.shard_map(per_device, mesh=mesh, in_specs=in_specs, out_specs=out_specs, check_vma=False)
```
